32 devices in a mesh: ctx: 8 (over y, x, core), fsdp: 4 (over z).
Axes of the slice: x: 2, y: 2, z: 4, core: 2. Of those that a mesh axis runs over, the one named last changes fastest.
Arguments:
- queries: bfloat16 [4, 1024, 768], P('fsdp', 'ctx'), may hold values from -6 to 6
- key_rows: bfloat16 [4, 1024, 768], P('fsdp', 'ctx'), may hold values from -6 to 6
- value_rows: bfloat16 [4, 1024, 768], P('fsdp', 'ctx'), may hold values from -6 to 6
- lengths: int32 [4], P('fsdp'), may hold values from 512 to 1024, as said below
- out_weight: bfloat16 [768, 1536], P(None, 'fsdp'), may hold values from -0.21875 to 0.21875
Outputs:
- mixed: bfloat16 [4, 1024, 1536], P('fsdp', 'ctx')
The draws below stay inside these ranges and needn't reach their ends.
Inputs may be any that keep to these rules, and one draw needn't show every extreme that they name: `lengths`: keys at frame positions at or beyond a recording's length are ignored.
All inputs are finite; a program needn't handle non-finite values.
Results may differ from the reference program's by a relative error of at most 0.011.
Values may be sent and summed in bfloat16 or wider, within the bound.
No kernel may reach another device: no remote copies, remote signals or barrier semaphores. Data moves between devices by JAX's collectives and lax.ppermute only.
A program may use at most 128 MiB of HBM per device.

```python
import math
import jax
import jax.numpy as jnp
from jax import lax

D = 1536
HEADS = 8
HDIM = 96
HD = 768
FRAMES = 1024
RECS = 4


def draw_queries(key, part):
    base_key = jax.random.fold_in(key, 1)
    values = jnp.clip(1.6 * jax.random.normal(base_key, (RECS, FRAMES, HEADS * HDIM), jnp.float32), -6.0, 6.0)
    return values.astype(jnp.bfloat16)


def draw_key_rows(key, part):
    base_key = jax.random.fold_in(key, 2)
    values = jnp.clip(1.6 * jax.random.normal(base_key, (RECS, FRAMES, HEADS * HDIM), jnp.float32), -6.0, 6.0)
    return values.astype(jnp.bfloat16)


def draw_lengths(key, part):
    key_base, key_order = jax.random.split(jax.random.fold_in(key, 3))
    drawn = jax.random.randint(key_base, (RECS,), FRAMES // 2, FRAMES + 1)
    order = jax.random.permutation(key_order, RECS)
    drawn = drawn.at[order[0]].set(FRAMES)
    drawn = drawn.at[order[1]].set(FRAMES // 2)
    return drawn.astype(jnp.int32)


def levels(key, extent, shards, least, top_value):
    gain, own = 1.0, jax.random.fold_in(key, 6)
    for axis_at, blocks in shards:
        heights = jnp.exp(jax.random.uniform(jax.random.fold_in(own, axis_at), (blocks,), jnp.float32, least / len(shards), top_value / len(shards)))
        gain = gain * jnp.repeat(heights, extent[axis_at] // blocks).reshape([-1 if axis == axis_at else 1 for axis in range(len(extent))])
    return gain


def centred(own_key, extent, scale, most, cuts=(), kind=jnp.bfloat16):
    values = scale * jax.random.normal(own_key, extent, jnp.float32)
    if cuts:
        values = values * levels(own_key, extent, cuts, -0.22, 0.18)
    return jnp.clip(values, -most, most).astype(kind)


def setup_inputs(seed: int = 0) -> dict:
    keys = jax.random.split(jax.random.key(seed), 6)
    return {
        "queries": draw_queries(jax.random.fold_in(keys[5], 71), 0),
        "key_rows": draw_key_rows(jax.random.fold_in(keys[5], 71), 0),
        "value_rows": centred(keys[2], (RECS, FRAMES, HD), 1.0, 6.0, ((0, 4), (1, 8))),
        "lengths": draw_lengths(jax.random.fold_in(keys[5], 71), 0),
        "out_weight": centred(keys[4], (HD, D), HD ** -0.5, 0.21875, ((1, 4),)),
    }


def reference(queries, key_rows, value_rows, lengths, out_weight):
    frames = queries.shape[1]
    feature_width = queries.shape[2]
    head_size = feature_width // HEADS
    score_scale = 1.0 / math.sqrt(head_size)

    def per_recording(items):
        query_one, key_one, value_one, valid_frames = items
        inside = jnp.arange(frames, dtype=jnp.int32) < valid_frames
        outputs = []
        for head in range(HEADS):
            columns = slice(head * head_size, (head + 1) * head_size)
            scores = jnp.dot(query_one[:, columns], key_one[:, columns].T, preferred_element_type=jnp.float32) * score_scale
            scores = jnp.where(inside[None, :], scores, jnp.float32(-1e+30))
            row_max = lax.optimization_barrier(jnp.max(scores, axis=-1, keepdims=True))
            probs = jnp.where(inside[None, :], jnp.exp(scores - row_max), jnp.float32(0.0))
            row_sum = lax.optimization_barrier(jnp.sum(probs, axis=-1, keepdims=True))
            head_out = jnp.dot(probs.astype(jnp.bfloat16), value_one[:, columns], preferred_element_type=jnp.float32) / row_sum
            outputs.append(head_out)
        attention = jnp.concatenate(outputs, axis=1).astype(jnp.bfloat16)
        return jnp.dot(attention, out_weight, preferred_element_type=jnp.float32).astype(jnp.bfloat16)
    return lax.map(per_recording, (queries, key_rows, value_rows, lengths))
```

```python
import functools
import math

import jax
import jax.numpy as jnp
from jax import lax
from jax.experimental import pallas as pl
from jax.experimental.pallas import tpu as pltpu
from jax.sharding import PartitionSpec as P

HEADS = 8
VMEM_LIMIT = 48 * 1024 * 1024
WHOLE = pl.BlockSpec(memory_space=pltpu.VMEM)
SCALARS = pl.BlockSpec(memory_space=pltpu.SMEM)


def params():
    return pltpu.CompilerParams(vmem_limit_bytes=VMEM_LIMIT)


def pack_kernel(query_ref, key_ref, value_ref, packed_ref):
    head_size = packed_ref.shape[2]
    for part, ref in enumerate((query_ref, key_ref, value_ref)):
        turned = ref[0].T
        for head in range(HEADS):
            packed_ref[head, part] = turned[head * head_size : (head + 1) * head_size, :]


def pack(queries, key_rows, value_rows):
    _, frames, features = queries.shape
    return pl.pallas_call(
        pack_kernel,
        out_shape=jax.ShapeDtypeStruct((HEADS, 3, features // HEADS, frames), queries.dtype),
        in_specs=[WHOLE] * 3,
        out_specs=WHOLE,
        compiler_params=params(),
        name="pack_heads",
    )(queries, key_rows, value_rows)


def attention_kernel(chunk_blocks, lengths_ref, query_ref, key_ref, value_ref, out_ref, key_scr, value_scr):
    key_blocks, _, head_size, block = key_ref.shape
    query_blocks = query_ref.shape[0]
    keys = key_blocks * block
    for at in range(key_blocks):
        key_scr[at * block : (at + 1) * block, :] = key_ref[at, 0].T
        value_scr[:, at * block : (at + 1) * block] = value_ref[at, 0]
    scale = jnp.float32(1.0 / math.sqrt(head_size))
    log2e = jnp.float32(math.log2(math.e))
    valid = lengths_ref[0]
    inside = lax.broadcasted_iota(jnp.int32, (keys, chunk_blocks * block), 0) < valid
    for first in range(0, query_blocks, chunk_blocks):
        query = jnp.concatenate([query_ref[first + at, 0] for at in range(chunk_blocks)], axis=1)
        scores = jnp.dot(key_scr[...], query, preferred_element_type=jnp.float32) * (scale * log2e)
        scores = jnp.where(inside, scores, jnp.float32(-1e30))
        row_max = jnp.max(scores, axis=0, keepdims=True)
        probs = jnp.exp2(scores - row_max)
        total = jnp.sum(probs, axis=0, keepdims=True)
        mixed = jnp.dot(value_scr[...], probs.astype(jnp.bfloat16), preferred_element_type=jnp.float32)
        mixed = (mixed / total).astype(jnp.bfloat16)
        for at in range(chunk_blocks):
            out_ref[first + at] = mixed[:, at * block : (at + 1) * block]


def attend(lengths, query, key, value, parts):
    query_blocks, _, head_size, block = query.shape
    key_blocks = key.shape[0]
    chunk_blocks = 2 if query_blocks % 2 == 0 else 1
    specs = [
        pl.BlockSpec((array.shape[0], 1, head_size, block), functools.partial(lambda part, i: (0, part, 0, 0), part))
        for array, part in zip((query, key, value), parts)
    ]
    return pl.pallas_call(
        functools.partial(attention_kernel, chunk_blocks),
        grid=(1,),
        out_shape=jax.ShapeDtypeStruct((query_blocks, head_size, block), jnp.bfloat16),
        in_specs=[SCALARS] + specs,
        out_specs=pl.BlockSpec((query_blocks, head_size, block), lambda i: (0, 0, 0)),
        scratch_shapes=[
            pltpu.VMEM((key_blocks * block, head_size), jnp.bfloat16),
            pltpu.VMEM((head_size, key_blocks * block), jnp.bfloat16),
        ],
        compiler_params=params(),
        cost_estimate=pl.CostEstimate(
            flops=4 * query_blocks * key_blocks * block * block * head_size,
            bytes_accessed=2 * (2 * query_blocks + 2 * key_blocks) * head_size * block,
            transcendentals=query_blocks * key_blocks * block * block,
        ),
        name="attend_one_head",
    )(lengths, query, key, value)


def project_kernel(places_ref, turned_ref, own_ref, *refs):
    out_ref = refs[-1]
    pieces = refs[:-1]
    features, columns = own_ref.shape
    shards = out_ref.shape[2] // columns
    per_shard = len(pieces) // (shards - 1)
    rows = features // per_shard
    own = jnp.dot(turned_ref[...].T, own_ref[...], preferred_element_type=jnp.float32)
    place = pl.multiple_of(places_ref[0] * columns, 128)
    out_ref[0, :, pl.ds(place, columns)] = own.astype(out_ref.dtype)
    turned = [
        turned_ref[pl.ds(pl.multiple_of((places_ref[1] ^ e) * rows, 64), rows), :].T for e in range(per_shard)
    ]
    for shard in range(1, shards):
        total = jnp.zeros((out_ref.shape[1], columns), jnp.float32)
        for e in range(per_shard):
            piece = pieces[(shard - 1) * per_shard + e]
            total = total + jnp.dot(turned[e], piece[...], preferred_element_type=jnp.float32)
        place = pl.multiple_of((places_ref[0] ^ shard) * columns, 128)
        out_ref[0, :, pl.ds(place, columns)] = total.astype(out_ref.dtype)


def project(places, turned, own, pieces, shards):
    features, frames = turned.shape
    return pl.pallas_call(
        project_kernel,
        out_shape=jax.ShapeDtypeStruct((1, frames, shards * own.shape[1]), jnp.bfloat16),
        in_specs=[SCALARS] + [WHOLE] * (2 + len(pieces)),
        out_specs=WHOLE,
        compiler_params=params(),
        cost_estimate=pl.CostEstimate(
            flops=2 * features * frames * shards * own.shape[1],
            bytes_accessed=2 * features * shards * own.shape[1],
            transcendentals=0,
        ),
        name="project_pieces",
    )(places, turned, own, *pieces)


def exchange(array, axis, size, flip):
    return lax.ppermute(array, axis, [(i, i ^ flip) for i in range(size)])


def weight_pieces(out_weight, ctx, fsdp):
    quarter = lax.axis_index("ctx") % 4
    rows = out_weight.shape[0] // 4
    mine = lax.dynamic_slice_in_dim(out_weight, quarter * rows, rows, 0)
    pieces = []
    for flip in range(1, fsdp):
        same = exchange(mine, "fsdp", fsdp, flip)
        other_chip = exchange(same, "ctx", ctx, 2)
        pieces += [same, exchange(same, "ctx", ctx, 1), other_chip, exchange(other_chip, "ctx", ctx, 1)]
    return pieces


def per_device(ctx, fsdp, queries, key_rows, value_rows, lengths, out_weight):
    _, frames, features = queries.shape
    groups = [[first + at for at in range(HEADS)] for first in range(0, ctx, HEADS)]
    swap = functools.partial(
        lax.all_to_all, axis_name="ctx", split_axis=0, concat_axis=0, axis_index_groups=groups, tiled=True
    )
    split_weight = fsdp in (2, 4) and ctx % 4 == 0
    if split_weight:
        pieces = weight_pieces(out_weight, ctx, fsdp)
    else:
        whole_weight = lax.all_gather(out_weight, "fsdp", axis=1, tiled=True)
    by_head = swap(pack(queries, key_rows, value_rows))
    if ctx == HEADS:
        mixed = attend(lengths, by_head, by_head, by_head, (0, 1, 2))
    else:
        across = [[head + first for first in range(0, ctx, HEADS)] for head in range(HEADS)]
        rest = lax.all_gather(by_head[:, 1:], "ctx", axis=0, axis_index_groups=across, tiled=True)
        mixed = attend(lengths, by_head[:, :1], rest, rest, (0, 0, 1))
    turned = swap(mixed).reshape(features, frames)
    if split_weight:
        places = jnp.stack([lax.axis_index("fsdp"), lax.axis_index("ctx") % 4]).astype(jnp.int32)
        return project(places, turned, out_weight, pieces, fsdp)
    return jnp.dot(turned.T, whole_weight, preferred_element_type=jnp.float32).astype(jnp.bfloat16)[None]


def solution(mesh):
    return jax.shard_map(
        functools.partial(per_device, mesh.shape["ctx"], mesh.shape["fsdp"]),
        mesh=mesh,
        in_specs=(
            P("fsdp", "ctx", None),
            P("fsdp", "ctx", None),
            P("fsdp", "ctx", None),
            P("fsdp"),
            P(None, "fsdp"),
        ),
        out_specs=P("fsdp", "ctx", None),
        check_vma=False,
    )
```

```python
import functools
import math

import jax
import jax.numpy as jnp
from jax import lax
from jax.experimental import pallas as pl
from jax.experimental.pallas import tpu as pltpu
from jax.sharding import PartitionSpec as P

HEADS = 8
VMEM_LIMIT = 48 * 1024 * 1024
WHOLE = pl.BlockSpec(memory_space=pltpu.VMEM)
SCALARS = pl.BlockSpec(memory_space=pltpu.SMEM)


def params():
    return pltpu.CompilerParams(vmem_limit_bytes=VMEM_LIMIT)


def pack_kernel(query_ref, key_ref, value_ref, packed_ref, rows, turned, in_sems, out_sems):
    head_size = packed_ref.shape[2]
    arrivals = [
        pltpu.make_async_copy(ref.at[0], rows.at[part], in_sems.at[part])
        for part, ref in enumerate((query_ref, key_ref, value_ref))
    ]
    for copy in arrivals:
        copy.start()
    departures = []
    for part, copy in enumerate(arrivals):
        copy.wait()
        turned[:, part] = rows[part].T.reshape(HEADS, head_size, rows.shape[1])
        copy = pltpu.make_async_copy(turned.at[:, part], packed_ref.at[:, part], out_sems.at[part])
        copy.start()
        departures.append(copy)
    for copy in departures:
        copy.wait()


def pack(queries, key_rows, value_rows):
    _, frames, features = queries.shape
    packed = (HEADS, 3, features // HEADS, frames)
    return pl.pallas_call(
        pack_kernel,
        out_shape=jax.ShapeDtypeStruct(packed, queries.dtype),
        in_specs=[pl.BlockSpec(memory_space=pl.ANY)] * 3,
        out_specs=pl.BlockSpec(memory_space=pl.ANY),
        scratch_shapes=[
            pltpu.VMEM((3, frames, features), queries.dtype),
            pltpu.VMEM(packed, queries.dtype),
            pltpu.SemaphoreType.DMA((3,)),
            pltpu.SemaphoreType.DMA((3,)),
        ],
        compiler_params=pltpu.CompilerParams(vmem_limit_bytes=60 * 1024 * 1024),
        name="pack_heads",
    )(queries, key_rows, value_rows)


def attention_kernel(chunk_blocks, lengths_ref, query_ref, key_ref, value_ref, out_ref, key_scr, value_scr):
    key_blocks, _, head_size, block = key_ref.shape
    query_blocks = query_ref.shape[0]
    keys = key_blocks * block
    for at in range(key_blocks):
        key_scr[at * block : (at + 1) * block, :] = key_ref[at, 0].T
        value_scr[:, at * block : (at + 1) * block] = value_ref[at, 0]
    scale = jnp.float32(1.0 / math.sqrt(head_size))
    log2e = jnp.float32(math.log2(math.e))
    valid = lengths_ref[0]
    inside = lax.broadcasted_iota(jnp.int32, (keys, chunk_blocks * block), 0) < valid
    for first in range(0, query_blocks, chunk_blocks):
        query = jnp.concatenate([query_ref[first + at, 0] for at in range(chunk_blocks)], axis=1)
        scores = jnp.dot(key_scr[...], query, preferred_element_type=jnp.float32) * (scale * log2e)
        scores = jnp.where(inside, scores, jnp.float32(-1e30))
        row_max = jnp.max(scores, axis=0, keepdims=True)
        probs = jnp.exp2(scores - row_max)
        total = jnp.sum(probs, axis=0, keepdims=True)
        mixed = jnp.dot(value_scr[...], probs.astype(jnp.bfloat16), preferred_element_type=jnp.float32)
        mixed = (mixed / total).astype(jnp.bfloat16)
        for at in range(chunk_blocks):
            out_ref[first + at] = mixed[:, at * block : (at + 1) * block]


def attend(lengths, query, key, value, parts):
    query_blocks, _, head_size, block = query.shape
    key_blocks = key.shape[0]
    chunk_blocks = 2 if query_blocks % 2 == 0 else 1
    specs = [
        pl.BlockSpec((array.shape[0], 1, head_size, block), functools.partial(lambda part, i: (0, part, 0, 0), part))
        for array, part in zip((query, key, value), parts)
    ]
    return pl.pallas_call(
        functools.partial(attention_kernel, chunk_blocks),
        grid=(1,),
        out_shape=jax.ShapeDtypeStruct((query_blocks, head_size, block), jnp.bfloat16),
        in_specs=[SCALARS] + specs,
        out_specs=pl.BlockSpec((query_blocks, head_size, block), lambda i: (0, 0, 0)),
        scratch_shapes=[
            pltpu.VMEM((key_blocks * block, head_size), jnp.bfloat16),
            pltpu.VMEM((head_size, key_blocks * block), jnp.bfloat16),
        ],
        compiler_params=params(),
        cost_estimate=pl.CostEstimate(
            flops=4 * query_blocks * key_blocks * block * block * head_size,
            bytes_accessed=2 * (2 * query_blocks + 2 * key_blocks) * head_size * block,
            transcendentals=query_blocks * key_blocks * block * block,
        ),
        name="attend_one_head",
    )(lengths, query, key, value)


def project_kernel(places_ref, turned_ref, own_ref, *refs):
    out_ref = refs[-1]
    pieces = refs[:-1]
    features, columns = own_ref.shape
    shards = out_ref.shape[2] // columns
    rows = features // len(pieces)
    own = jnp.dot(turned_ref[...].T, own_ref[...], preferred_element_type=jnp.float32)
    place = pl.multiple_of(places_ref[0] * columns, 128)
    out_ref[0, :, pl.ds(place, columns)] = own.astype(out_ref.dtype)
    foreign = jnp.zeros((out_ref.shape[1], (shards - 1) * columns), jnp.float32)
    for at, piece in enumerate(pieces):
        turned = turned_ref[pl.ds(pl.multiple_of((places_ref[1] ^ at) * rows, 32), rows), :].T
        foreign = foreign + jnp.dot(turned, piece[...], preferred_element_type=jnp.float32)
    for shard in range(1, shards):
        place = pl.multiple_of((places_ref[0] ^ shard) * columns, 128)
        part = foreign[:, (shard - 1) * columns : shard * columns]
        out_ref[0, :, pl.ds(place, columns)] = part.astype(out_ref.dtype)


def project(places, turned, own, pieces, shards):
    features, frames = turned.shape
    return pl.pallas_call(
        project_kernel,
        out_shape=jax.ShapeDtypeStruct((1, frames, shards * own.shape[1]), jnp.bfloat16),
        in_specs=[SCALARS] + [WHOLE] * (2 + len(pieces)),
        out_specs=WHOLE,
        compiler_params=params(),
        cost_estimate=pl.CostEstimate(
            flops=2 * features * frames * shards * own.shape[1],
            bytes_accessed=2 * features * shards * own.shape[1],
            transcendentals=0,
        ),
        name="project_pieces",
    )(places, turned, own, *pieces)


def exchange(array, axis, size, flip):
    return lax.ppermute(array, axis, [(i, i ^ flip) for i in range(size)])


def weight_fetch(out_weight, ctx, fsdp, ways):
    share = lax.axis_index("ctx") % ways
    rows = out_weight.shape[0] // ways
    mine = lax.dynamic_slice_in_dim(out_weight, share * rows, rows, 0)
    fetched = jnp.concatenate([exchange(mine, "fsdp", fsdp, flip) for flip in range(1, fsdp)], axis=1)
    return [fetched] + [exchange(fetched, "ctx", ctx, flip) for flip in range(2, ways, 2)]


def weight_share(fetched, ctx):
    return [piece for same in fetched for piece in (same, exchange(same, "ctx", ctx, 1))]


def per_device(ctx, fsdp, queries, key_rows, value_rows, lengths, out_weight):
    _, frames, features = queries.shape
    groups = [[first + at for at in range(HEADS)] for first in range(0, ctx, HEADS)]
    swap = functools.partial(
        lax.all_to_all, axis_name="ctx", split_axis=0, concat_axis=0, axis_index_groups=groups, tiled=True
    )
    split_weight = fsdp in (2, 4) and ctx % HEADS == 0
    if split_weight:
        fetched = weight_fetch(out_weight, ctx, fsdp, HEADS)
    else:
        whole_weight = lax.all_gather(out_weight, "fsdp", axis=1, tiled=True)
    by_head = swap(pack(queries, key_rows, value_rows))
    if ctx == HEADS:
        mixed = attend(lengths, by_head, by_head, by_head, (0, 1, 2))
    else:
        across = [[head + first for first in range(0, ctx, HEADS)] for head in range(HEADS)]
        rest = lax.all_gather(by_head[:, 1:], "ctx", axis=0, axis_index_groups=across, tiled=True)
        mixed = attend(lengths, by_head[:, :1], rest, rest, (0, 0, 1))
    turned = swap(mixed).reshape(features, frames)
    if split_weight:
        fetched, _ = lax.optimization_barrier((fetched, mixed))
        pieces = weight_share(fetched, ctx)
        places = jnp.stack([lax.axis_index("fsdp"), lax.axis_index("ctx") % HEADS]).astype(jnp.int32)
        return project(places, turned, out_weight, pieces, fsdp)
    return jnp.dot(turned.T, whole_weight, preferred_element_type=jnp.float32).astype(jnp.bfloat16)[None]


def solution(mesh):
    return jax.shard_map(
        functools.partial(per_device, mesh.shape["ctx"], mesh.shape["fsdp"]),
        mesh=mesh,
        in_specs=(
            P("fsdp", "ctx", None),
            P("fsdp", "ctx", None),
            P("fsdp", "ctx", None),
            P("fsdp"),
            P(None, "fsdp"),
        ),
        out_specs=P("fsdp", "ctx", None),
        check_vma=False,
    )
```

```python
import functools
import math

import jax
import jax.numpy as jnp
from jax import lax
from jax.experimental import pallas as pl
from jax.experimental.pallas import tpu as pltpu
from jax.sharding import PartitionSpec as P

HEADS = 8
VMEM_LIMIT = 48 * 1024 * 1024
WHOLE = pl.BlockSpec(memory_space=pltpu.VMEM)
SCALARS = pl.BlockSpec(memory_space=pltpu.SMEM)


def params():
    return pltpu.CompilerParams(vmem_limit_bytes=VMEM_LIMIT)


def pack_kernel(query_ref, key_ref, value_ref, packed_ref, rows, turned, in_sems, out_sems):
    head_size = packed_ref.shape[2]
    arrivals = [
        pltpu.make_async_copy(ref.at[0], rows.at[part], in_sems.at[part])
        for part, ref in enumerate((query_ref, key_ref, value_ref))
    ]
    for copy in arrivals:
        copy.start()
    departures = []
    for part, copy in enumerate(arrivals):
        copy.wait()
        turned[:, part] = rows[part].T.reshape(HEADS, head_size, rows.shape[1])
        copy = pltpu.make_async_copy(turned.at[:, part], packed_ref.at[:, part], out_sems.at[part])
        copy.start()
        departures.append(copy)
    for copy in departures:
        copy.wait()


def pack(queries, key_rows, value_rows):
    _, frames, features = queries.shape
    packed = (HEADS, 3, features // HEADS, frames)
    return pl.pallas_call(
        pack_kernel,
        out_shape=jax.ShapeDtypeStruct(packed, queries.dtype),
        in_specs=[pl.BlockSpec(memory_space=pl.ANY)] * 3,
        out_specs=pl.BlockSpec(memory_space=pl.ANY),
        scratch_shapes=[
            pltpu.VMEM((3, frames, features), queries.dtype),
            pltpu.VMEM(packed, queries.dtype),
            pltpu.SemaphoreType.DMA((3,)),
            pltpu.SemaphoreType.DMA((3,)),
        ],
        compiler_params=pltpu.CompilerParams(vmem_limit_bytes=60 * 1024 * 1024),
        name="pack_heads",
    )(queries, key_rows, value_rows)


def attention_kernel(chunk_blocks, lengths_ref, query_ref, key_ref, value_ref, out_ref, key_scr, value_scr):
    key_blocks, _, head_size, block = key_ref.shape
    query_blocks = query_ref.shape[0]
    keys = key_blocks * block
    for at in range(key_blocks):
        key_scr[at * block : (at + 1) * block, :] = key_ref[at, 0].T
        value_scr[:, at * block : (at + 1) * block] = value_ref[at, 0]
    scale = jnp.float32(1.0 / math.sqrt(head_size))
    log2e = jnp.float32(math.log2(math.e))
    valid = lengths_ref[0]
    inside = lax.broadcasted_iota(jnp.int32, (keys, chunk_blocks * block), 0) < valid
    for first in range(0, query_blocks, chunk_blocks):
        query = jnp.concatenate([query_ref[first + at, 0] for at in range(chunk_blocks)], axis=1)
        scores = jnp.dot(key_scr[...], query, preferred_element_type=jnp.float32) * (scale * log2e)
        scores = jnp.where(inside, scores, jnp.float32(-1e30))
        row_max = jnp.max(scores, axis=0, keepdims=True)
        probs = jnp.exp2(scores - row_max)
        total = jnp.sum(probs, axis=0, keepdims=True)
        mixed = jnp.dot(value_scr[...], probs.astype(jnp.bfloat16), preferred_element_type=jnp.float32)
        mixed = (mixed / total).astype(jnp.bfloat16)
        for at in range(chunk_blocks):
            out_ref[first + at] = mixed[:, at * block : (at + 1) * block]


def attend(lengths, query, key, value, parts):
    query_blocks, _, head_size, block = query.shape
    key_blocks = key.shape[0]
    chunk_blocks = 2 if query_blocks % 2 == 0 else 1
    specs = [
        pl.BlockSpec((array.shape[0], 1, head_size, block), functools.partial(lambda part, i: (0, part, 0, 0), part))
        for array, part in zip((query, key, value), parts)
    ]
    return pl.pallas_call(
        functools.partial(attention_kernel, chunk_blocks),
        grid=(1,),
        out_shape=jax.ShapeDtypeStruct((query_blocks, head_size, block), jnp.bfloat16),
        in_specs=[SCALARS] + specs,
        out_specs=pl.BlockSpec((query_blocks, head_size, block), lambda i: (0, 0, 0)),
        scratch_shapes=[
            pltpu.VMEM((key_blocks * block, head_size), jnp.bfloat16),
            pltpu.VMEM((head_size, key_blocks * block), jnp.bfloat16),
        ],
        compiler_params=params(),
        cost_estimate=pl.CostEstimate(
            flops=4 * query_blocks * key_blocks * block * block * head_size,
            bytes_accessed=2 * (2 * query_blocks + 2 * key_blocks) * head_size * block,
            transcendentals=query_blocks * key_blocks * block * block,
        ),
        name="attend_one_head",
    )(lengths, query, key, value)


def project_kernel(place_ref, turned_ref, near_ref, far_ref, out_ref):
    rows = near_ref.shape[0]
    total = jnp.zeros(out_ref.shape[1:], jnp.float32)
    for flip, ref in enumerate((near_ref, far_ref)):
        turned = turned_ref[pl.ds(pl.multiple_of((place_ref[0] ^ flip) * rows, rows), rows), :].T
        total = total + jnp.dot(turned, ref[...], preferred_element_type=jnp.float32)
    out_ref[0] = total.astype(out_ref.dtype)


def project(place, turned, near, far):
    features, frames = turned.shape
    width = near.shape[1]
    return pl.pallas_call(
        project_kernel,
        out_shape=jax.ShapeDtypeStruct((1, frames, width), jnp.bfloat16),
        in_specs=[SCALARS] + [WHOLE] * 3,
        out_specs=WHOLE,
        compiler_params=params(),
        cost_estimate=pl.CostEstimate(
            flops=2 * features * frames * width, bytes_accessed=2 * features * width, transcendentals=0
        ),
        name="project_halves",
    )(place, turned, near, far)


def exchange(array, axis, size, flip):
    return lax.ppermute(array, axis, [(i, i ^ flip) for i in range(size)])


def weight_half(out_weight):
    rows = out_weight.shape[0] // 2
    mine = lax.dynamic_slice_in_dim(out_weight, lax.axis_index("ctx") % 2 * rows, rows, 0)
    return lax.all_gather(mine, "fsdp", axis=1, tiled=True)


def per_device(ctx, queries, key_rows, value_rows, lengths, out_weight):
    _, frames, features = queries.shape
    groups = [[first + at for at in range(HEADS)] for first in range(0, ctx, HEADS)]
    swap = functools.partial(
        lax.all_to_all, axis_name="ctx", split_axis=0, concat_axis=0, axis_index_groups=groups, tiled=True
    )
    near = weight_half(out_weight)
    by_head = swap(pack(queries, key_rows, value_rows))
    if ctx == HEADS:
        mixed = attend(lengths, by_head, by_head, by_head, (0, 1, 2))
    else:
        across = [[head + first for first in range(0, ctx, HEADS)] for head in range(HEADS)]
        rest = lax.all_gather(by_head[:, 1:], "ctx", axis=0, axis_index_groups=across, tiled=True)
        mixed = attend(lengths, by_head[:, :1], rest, rest, (0, 0, 1))
    turned = swap(mixed).reshape(features, frames)
    near, turned = lax.optimization_barrier((near, turned))
    far = exchange(near, "ctx", ctx, 1)
    place = (lax.axis_index("ctx") % 2).astype(jnp.int32).reshape(1)
    return project(place, turned, near, far)


def solution(mesh):
    return jax.shard_map(
        functools.partial(per_device, mesh.shape["ctx"]),
        mesh=mesh,
        in_specs=(
            P("fsdp", "ctx", None),
            P("fsdp", "ctx", None),
            P("fsdp", "ctx", None),
            P("fsdp"),
            P(None, "fsdp"),
        ),
        out_specs=P("fsdp", "ctx", None),
        check_vma=False,
    )
```

```python
import functools
import math

import jax
import jax.numpy as jnp
from jax import lax
from jax.experimental import pallas as pl
from jax.experimental.pallas import tpu as pltpu
from jax.sharding import PartitionSpec as P

HEADS = 8
FLIPS = tuple(range(0, HEADS, 2))
WHOLE = pl.BlockSpec(memory_space=pltpu.VMEM)
SCALARS = pl.BlockSpec(memory_space=pltpu.SMEM)
ANYWHERE = pl.BlockSpec(memory_space=pl.ANY)


def params(mebibytes=48):
    return pltpu.CompilerParams(vmem_limit_bytes=mebibytes * 1024 * 1024)


def place_in_group():
    return lax.axis_index("ctx") % HEADS


def pack_kernel(query_ref, key_ref, value_ref, weight_ref, *refs):
    outs, share_ref = refs[: len(FLIPS)], refs[len(FLIPS)]
    rows, turned, sems = refs[len(FLIPS) + 1 :]
    head_size = outs[0].shape[2]
    place = place_in_group()
    first = pl.multiple_of(place * share_ref.shape[0], 32)
    cut = pltpu.make_async_copy(weight_ref.at[pl.ds(first, share_ref.shape[0])], share_ref, sems.at[3])
    arrivals = [
        pltpu.make_async_copy(ref.at[0], rows.at[part], sems.at[part])
        for part, ref in enumerate((query_ref, key_ref, value_ref))
    ]
    for copy in arrivals:
        copy.start()
    cut.start()
    for part, copy in enumerate(arrivals):
        copy.wait()
        turned[...] = rows[part].T
        for flip, out_ref in zip(FLIPS, outs):
            for other in range(2):
                head = pl.multiple_of((place ^ (flip + other)) * head_size, 32)
                out_ref[other, part] = turned[pl.ds(head, head_size), :]
    cut.wait()


def pack(queries, key_rows, value_rows, out_weight):
    _, frames, features = queries.shape
    blocks = jax.ShapeDtypeStruct((2, 3, features // HEADS, frames), queries.dtype)
    share = jax.ShapeDtypeStruct((out_weight.shape[0] // HEADS, out_weight.shape[1]), out_weight.dtype)
    outs = pl.pallas_call(
        pack_kernel,
        out_shape=[blocks] * len(FLIPS) + [share],
        in_specs=[ANYWHERE] * 4,
        out_specs=[WHOLE] * (len(FLIPS) + 1),
        scratch_shapes=[
            pltpu.VMEM((3, frames, features), queries.dtype),
            pltpu.VMEM((features, frames), queries.dtype),
            pltpu.SemaphoreType.DMA((4,)),
        ],
        compiler_params=params(60),
        name="pack_heads",
    )(queries, key_rows, value_rows, out_weight)
    return outs[: len(FLIPS)], outs[len(FLIPS)]


def attention_kernel(groups, lengths_ref, *refs):
    same, other = refs[: len(FLIPS)], refs[len(FLIPS) : 2 * len(FLIPS)]
    rest_ref = refs[2 * len(FLIPS)] if groups > 1 else None
    outs, (keys, values, query) = refs[-3 - len(FLIPS) : -3], refs[-3:]
    head_size, block = outs[0].shape[1:]
    place = place_in_group()
    scale = jnp.float32(math.log2(math.e) / math.sqrt(head_size))
    pad = keys.shape[1] - head_size
    at_row = lax.broadcasted_iota(jnp.int32, (pad, block), 0)
    at_frame = lax.broadcasted_iota(jnp.int32, (pad, block), 1)
    first_row = jnp.where(at_row == 0, 1.0, 0.0).astype(keys.dtype)

    def piece(flip, part):
        return same[flip // 2][0, part] if flip % 2 == 0 else other[flip // 2][part]

    for at in range(groups * HEADS):
        flip = at % HEADS
        key = piece(flip, 1) if groups == 1 else rest_ref[at, 0]
        value = piece(flip, 2) if groups == 1 else rest_ref[at, 1]
        frame = (at // HEADS * HEADS + (place ^ flip)) * block + at_frame
        bias = jnp.where((at_row == 0) & (frame >= lengths_ref[0]), -1e30, 0.0).astype(keys.dtype)
        keys[at * block : (at + 1) * block, :] = jnp.concatenate([key, bias], axis=0).T
        values[:head_size, at * block : (at + 1) * block] = value
        values[head_size:, at * block : (at + 1) * block] = first_row
    for half in range(2):
        query[head_size:, half * block : (half + 1) * block] = first_row
    for flip, out_ref in zip(FLIPS, outs):
        for half in range(2):
            query[:head_size, half * block : (half + 1) * block] = piece(flip + half, 0)
        scores = jnp.dot(keys[...], query[...], preferred_element_type=jnp.float32)
        row_max = jnp.max(scores, axis=0, keepdims=True) * scale
        probs = jnp.exp2(scores * scale - row_max).astype(jnp.bfloat16)
        mixed = jnp.dot(values[...], probs, preferred_element_type=jnp.float32)
        mixed = (mixed[:head_size] / mixed[head_size : head_size + 1]).astype(jnp.bfloat16)
        for half in range(2):
            out_ref[half] = mixed[:, half * block : (half + 1) * block]


def attend(lengths, same, other, rest, groups):
    _, head_size, block = other[0].shape
    keys = groups * HEADS * block
    padded = head_size + 32
    queries = HEADS * block
    rest = [] if rest is None else [rest]
    return pl.pallas_call(
        functools.partial(attention_kernel, groups),
        out_shape=[jax.ShapeDtypeStruct((2, head_size, block), jnp.bfloat16)] * len(FLIPS),
        in_specs=[SCALARS] + [WHOLE] * (2 * len(FLIPS) + len(rest)),
        out_specs=[WHOLE] * len(FLIPS),
        scratch_shapes=[
            pltpu.VMEM((keys, padded), jnp.bfloat16),
            pltpu.VMEM((padded, keys), jnp.bfloat16),
            pltpu.VMEM((padded, 2 * block), jnp.bfloat16),
        ],
        compiler_params=params(),
        cost_estimate=pl.CostEstimate(
            flops=4 * queries * keys * head_size,
            bytes_accessed=4 * (queries + keys) * head_size,
            transcendentals=queries * keys,
        ),
        name="attend_one_head",
    )(lengths, *same, *other, *rest)


def project_kernel(shards, *refs):
    each = len(FLIPS)
    heads_same, heads_other, weight_same, weight_other = (refs[at : at + each] for at in range(0, 4 * each, each))
    own_ref = refs[4 * len(FLIPS)] if shards > 1 else None
    out_ref, turned, weight = refs[-3:]
    place = place_in_group()
    rows = turned.shape[0] // HEADS
    for flip in range(HEADS):
        here = pl.ds(pl.multiple_of((place ^ flip) * rows, 32), rows)
        turned[here, :] = heads_other[flip // 2][...] if flip % 2 else heads_same[flip // 2][0]
        weight[here, :] = (weight_other if flip % 2 else weight_same)[flip // 2][...]
    attention = turned[...].T
    foreign = jnp.dot(attention, weight[...], preferred_element_type=jnp.float32).astype(out_ref.dtype)
    if shards == 1:
        out_ref[0] = foreign
        return
    columns = own_ref.shape[1]
    shard = lax.axis_index("fsdp")
    own = jnp.dot(attention, own_ref[...], preferred_element_type=jnp.float32).astype(out_ref.dtype)
    out_ref[0, :, pl.ds(pl.multiple_of(shard * columns, 128), columns)] = own
    for flip in range(1, shards):
        here = pl.ds(pl.multiple_of((shard ^ flip) * columns, 128), columns)
        out_ref[0, :, here] = foreign[:, (flip - 1) * columns : flip * columns]


def project(heads_same, heads_other, weight_same, weight_other, own, shards):
    rows, frames = heads_other[0].shape
    foreign = weight_same[0].shape[1]
    width = foreign + (own[0].shape[1] if own else 0)
    features = HEADS * rows
    pieces = [*heads_same, *heads_other, *weight_same, *weight_other, *own]
    return pl.pallas_call(
        functools.partial(project_kernel, shards),
        out_shape=jax.ShapeDtypeStruct((1, frames, width), jnp.bfloat16),
        in_specs=[WHOLE] * len(pieces),
        out_specs=WHOLE,
        scratch_shapes=[pltpu.VMEM((features, frames), jnp.bfloat16), pltpu.VMEM((features, foreign), jnp.bfloat16)],
        compiler_params=params(),
        cost_estimate=pl.CostEstimate(
            flops=2 * features * frames * width, bytes_accessed=2 * features * width, transcendentals=0
        ),
        name="project_heads",
    )(*pieces)


def per_device(ctx, fsdp, queries, key_rows, value_rows, lengths, out_weight):
    def exchange(array, axis, flip):
        size = ctx if axis == "ctx" else fsdp
        return lax.ppermute(array, axis, [(i, i ^ flip) for i in range(size)])

    by_chip, share = pack(queries, key_rows, value_rows, out_weight)
    split_columns = fsdp in (2, 4)
    if split_columns:
        share = jnp.concatenate([exchange(share, "fsdp", flip) for flip in range(1, fsdp)], axis=1)
    else:
        share = lax.all_gather(share, "fsdp", axis=1, tiled=True)

    same = [exchange(array, "ctx", flip) if flip else array for flip, array in zip(FLIPS, by_chip)]
    other = [exchange(array[1], "ctx", 1) for array in same]
    weight_same = [exchange(share, "ctx", flip) if flip else share for flip in FLIPS]

    groups = ctx // HEADS
    rest = None
    if groups > 1:
        pairs = [array for two in zip([a[0, 1:] for a in same], [a[1:] for a in other]) for array in two]
        across = [[head + first for first in range(0, ctx, HEADS)] for head in range(HEADS)]
        rest = lax.all_gather(jnp.stack(pairs), "ctx", axis=0, axis_index_groups=across, tiled=True)
    mixed = attend(lengths, same, other, rest, groups)

    heads_same = [exchange(array, "ctx", flip) if flip else array for flip, array in zip(FLIPS, mixed)]
    heads_other = [exchange(array[1], "ctx", 1) for array in heads_same]
    weight_same, _ = lax.optimization_barrier((weight_same, mixed))
    weight_other = [exchange(array, "ctx", 1) for array in weight_same]
    own = [out_weight] if split_columns else []
    return project(heads_same, heads_other, weight_same, weight_other, own, fsdp if split_columns else 1)


def solution(mesh):
    return jax.shard_map(
        functools.partial(per_device, mesh.shape["ctx"], mesh.shape["fsdp"]),
        mesh=mesh,
        in_specs=(
            P("fsdp", "ctx", None),
            P("fsdp", "ctx", None),
            P("fsdp", "ctx", None),
            P("fsdp"),
            P(None, "fsdp"),
        ),
        out_specs=P("fsdp", "ctx", None),
        check_vma=False,
    )
```

```python
import functools
import math

import jax
import jax.numpy as jnp
from jax import lax
from jax.experimental import pallas as pl
from jax.experimental.pallas import tpu as pltpu
from jax.sharding import PartitionSpec as P

HEADS = 8
FLIPS = tuple(range(0, HEADS, 2))
WHOLE = pl.BlockSpec(memory_space=pltpu.VMEM)
SCALARS = pl.BlockSpec(memory_space=pltpu.SMEM)
IN_HBM = pl.BlockSpec(memory_space=pltpu.HBM)


def params(mebibytes=48):
    return pltpu.CompilerParams(vmem_limit_bytes=mebibytes * 1024 * 1024)


def place_in_group():
    return lax.axis_index("ctx") % HEADS


def pack_kernel(query_ref, key_ref, value_ref, *refs):
    outs = [refs[0:2], *([ref.at[0], ref.at[1]] for ref in refs[2 : 1 + len(FLIPS)])]
    rows, turned, sems = refs[1 + len(FLIPS) :]
    head_size = outs[0][0].shape[1]
    place = place_in_group()
    arrivals = [
        pltpu.make_async_copy(ref.at[0], rows.at[part], sems.at[part])
        for part, ref in enumerate((query_ref, key_ref, value_ref))
    ]
    for copy in arrivals:
        copy.start()
    for part, copy in enumerate(arrivals):
        copy.wait()
        turned[part] = rows[part].T
        for flip, out_ref in zip(FLIPS, outs):
            for other in range(2):
                head = pl.multiple_of((place ^ (flip + other)) * head_size, 32)
                out_ref[other][part] = turned[part, pl.ds(head, head_size), :]


def pack(queries, key_rows, value_rows):
    _, frames, features = queries.shape
    block = (3, features // HEADS, frames)
    own = jax.ShapeDtypeStruct(block, queries.dtype)
    two = jax.ShapeDtypeStruct((2, *block), queries.dtype)
    return pl.pallas_call(
        pack_kernel,
        out_shape=[own] * 2 + [two] * (len(FLIPS) - 1),
        in_specs=[IN_HBM] * 3,
        out_specs=[WHOLE] * (1 + len(FLIPS)),
        scratch_shapes=[
            pltpu.VMEM((3, frames, features), queries.dtype),
            pltpu.VMEM((3, features, frames), queries.dtype),
            pltpu.SemaphoreType.DMA((3,)),
        ],
        compiler_params=params(60),
        name="pack_heads",
    )(queries, key_rows, value_rows)


def attention_kernel(groups, lengths_ref, *refs):
    same, other = refs[: len(FLIPS)], refs[len(FLIPS) : 2 * len(FLIPS)]
    rest_ref = refs[2 * len(FLIPS)] if groups > 1 else None
    outs, (keys, values, query) = refs[-3 - len(FLIPS) : -3], refs[-3:]
    head_size, block = outs[0].shape[1:]
    place = place_in_group()
    scale = jnp.float32(math.log2(math.e) / math.sqrt(head_size))
    pad = keys.shape[1] - head_size
    at_row = lax.broadcasted_iota(jnp.int32, (pad, block), 0)
    at_frame = lax.broadcasted_iota(jnp.int32, (pad, block), 1)
    first_row = jnp.where(at_row == 0, 1.0, 0.0).astype(keys.dtype)

    def piece(flip, part):
        if flip < 2:
            return (same, other)[flip][0][part]
        return other[flip // 2][1, part] if flip % 2 else same[flip // 2][0, part]

    for at in range(groups * HEADS):
        flip = at % HEADS
        key = piece(flip, 1) if groups == 1 else rest_ref[at, 0]
        value = piece(flip, 2) if groups == 1 else rest_ref[at, 1]
        frame = (at // HEADS * HEADS + (place ^ flip)) * block + at_frame
        bias = jnp.where((at_row == 0) & (frame >= lengths_ref[0]), -1e30, 0.0).astype(keys.dtype)
        keys[at * block : (at + 1) * block, :] = jnp.concatenate([key, bias], axis=0).T
        values[:head_size, at * block : (at + 1) * block] = value
        values[head_size:, at * block : (at + 1) * block] = first_row
    for half in range(2):
        query[head_size:, half * block : (half + 1) * block] = first_row
    for flip, out_ref in zip(FLIPS, outs):
        for half in range(2):
            query[:head_size, half * block : (half + 1) * block] = piece(flip + half, 0)
        scores = jnp.dot(keys[...], query[...], preferred_element_type=jnp.float32)
        row_max = jnp.max(scores, axis=0, keepdims=True) * scale
        probs = jnp.exp2(scores * scale - row_max).astype(jnp.bfloat16)
        mixed = jnp.dot(values[...], probs, preferred_element_type=jnp.float32)
        mixed = (mixed[:head_size] / mixed[head_size : head_size + 1]).astype(jnp.bfloat16)
        for half in range(2):
            out_ref[half] = mixed[:, half * block : (half + 1) * block]


def attend(lengths, same, other, rest, groups):
    _, head_size, block = other[0].shape
    keys = groups * HEADS * block
    padded = head_size + 32
    queries = HEADS * block
    rest = [] if rest is None else [rest]
    return pl.pallas_call(
        functools.partial(attention_kernel, groups),
        out_shape=[jax.ShapeDtypeStruct((2, head_size, block), jnp.bfloat16)] * len(FLIPS),
        in_specs=[SCALARS] + [WHOLE] * (2 * len(FLIPS) + len(rest)),
        out_specs=[WHOLE] * len(FLIPS),
        scratch_shapes=[
            pltpu.VMEM((keys, padded), jnp.bfloat16),
            pltpu.VMEM((padded, keys), jnp.bfloat16),
            pltpu.VMEM((padded, 2 * block), jnp.bfloat16),
        ],
        compiler_params=params(24),
        cost_estimate=pl.CostEstimate(
            flops=4 * queries * keys * head_size,
            bytes_accessed=4 * (queries + keys) * head_size,
            transcendentals=queries * keys,
        ),
        name="attend_one_head",
    )(lengths, *same, *other, *rest)


def quarter_of(place, parity, core):
    return (((place >> 2) ^ (place >> 1) ^ parity) & 1) * 2 + ((place ^ core) & 1)


def project_kernel(shards, *refs):
    each = len(FLIPS)
    heads_same, heads_other, halves = refs[:each], refs[each : 2 * each], refs[2 * each : 2 * each + 2]
    own_ref = refs[2 * each + 2] if shards > 1 else None
    out_ref, turned, weight = refs[-3:]
    place = place_in_group()
    rows = turned.shape[0] // HEADS
    for flip in range(HEADS):
        here = pl.ds(pl.multiple_of((place ^ flip) * rows, 32), rows)
        turned[here, :] = heads_other[flip // 2][1] if flip % 2 else heads_same[flip // 2][0]
    quarter = weight.shape[0] // 4
    for core in range(2):
        for parity in range(2):
            here = pl.multiple_of(quarter_of(place, parity, core) * quarter, 32)
            weight[pl.ds(here, quarter), :] = halves[core][parity * quarter : (parity + 1) * quarter, :]
    attention = turned[...].T
    foreign = jnp.dot(attention, weight[...], preferred_element_type=jnp.float32).astype(out_ref.dtype)
    if shards == 1:
        out_ref[0] = foreign
        return
    columns = own_ref.shape[1]
    shard = lax.axis_index("fsdp")
    own = jnp.dot(attention, own_ref[...], preferred_element_type=jnp.float32).astype(out_ref.dtype)
    out_ref[0, :, pl.ds(pl.multiple_of(shard * columns, 128), columns)] = own
    for flip in range(1, shards):
        here = pl.ds(pl.multiple_of((shard ^ flip) * columns, 128), columns)
        out_ref[0, :, here] = foreign[:, (flip - 1) * columns : flip * columns]


def project(heads_same, heads_other, near, far, own, shards):
    _, rows, frames = heads_other[0].shape
    foreign = near.shape[1]
    width = foreign + (own[0].shape[1] if own else 0)
    features = HEADS * rows
    pieces = [*heads_same, *heads_other, near, far, *own]
    return pl.pallas_call(
        functools.partial(project_kernel, shards),
        out_shape=jax.ShapeDtypeStruct((1, frames, width), jnp.bfloat16),
        in_specs=[WHOLE] * len(pieces),
        out_specs=WHOLE,
        scratch_shapes=[pltpu.VMEM((features, frames), jnp.bfloat16), pltpu.VMEM((features, foreign), jnp.bfloat16)],
        compiler_params=params(24),
        cost_estimate=pl.CostEstimate(
            flops=2 * features * frames * width, bytes_accessed=2 * features * width, transcendentals=0
        ),
        name="project_heads",
    )(*pieces)


def per_device(ctx, fsdp, queries, key_rows, value_rows, lengths, out_weight):
    def exchange(array, axis, flip):
        size = ctx if axis == "ctx" else fsdp
        return lax.ppermute(array, axis, [(i, i ^ flip) for i in range(size)])

    place = place_in_group()
    rows = out_weight.shape[0] // 4
    quarter = lax.dynamic_slice_in_dim(out_weight, quarter_of(place, 0, 0) * rows, rows, 0)
    split_columns = fsdp == 4
    if split_columns:
        far = exchange(quarter, "fsdp", 2)
        near = exchange(quarter, "fsdp", 1)
        quarter = jnp.concatenate([near, far, exchange(far, "fsdp", 1)], axis=1)
    else:
        quarter = lax.all_gather(quarter, "fsdp", axis=1, tiled=True)

    own_same, own_other, *by_chip = pack(queries, key_rows, value_rows)
    same = [exchange(array, "ctx", flip) for flip, array in zip(FLIPS[1:], by_chip)]
    same = lax.optimization_barrier(same)
    other = [exchange(array, "ctx", 1) for array in (own_other, *same)]
    quarter, other = lax.optimization_barrier((quarter, other))
    first = exchange(quarter[: rows // 2], "ctx", 2)
    second = exchange(quarter[rows // 2 :], "ctx", 4)

    groups = ctx // HEADS
    rest = None
    if groups > 1:
        pairs = [own_same[1:], other[0][1:]]
        for one, two in zip(same, other[1:]):
            pairs += [one[0, 1:], two[1, 1:]]
        across = [[head + first for first in range(0, ctx, HEADS)] for head in range(HEADS)]
        rest = lax.all_gather(jnp.stack(pairs), "ctx", axis=0, axis_index_groups=across, tiled=True)
    mixed = attend(lengths, [own_same, *same], other, rest, groups)

    first, second, last = lax.optimization_barrier((first, second, mixed[-1]))
    mixed = [*mixed[:-1], last]
    heads_same = [exchange(array, "ctx", flip) if flip else array for flip, array in zip(FLIPS, mixed)]
    near = jnp.concatenate([quarter, first, second], axis=0)
    near, heads_same = lax.optimization_barrier((near, heads_same))
    heads_other = [exchange(array, "ctx", 1) for array in heads_same]
    far = exchange(near, "ctx", 1)
    own = [out_weight] if split_columns else []
    return project(heads_same, heads_other, near, far, own, fsdp if split_columns else 1)


def solution(mesh):
    return jax.shard_map(
        functools.partial(per_device, mesh.shape["ctx"], mesh.shape["fsdp"]),
        mesh=mesh,
        in_specs=(
            P("fsdp", "ctx", None),
            P("fsdp", "ctx", None),
            P("fsdp", "ctx", None),
            P("fsdp"),
            P(None, "fsdp"),
        ),
        out_specs=P("fsdp", "ctx", None),
        check_vma=False,
    )
```

```python
import functools
import math

import jax
import jax.numpy as jnp
from jax import lax
from jax.experimental import pallas as pl
from jax.experimental.pallas import tpu as pltpu
from jax.sharding import PartitionSpec as P

HEADS = 8
FLIPS = tuple(range(0, HEADS, 2))
WHOLE = pl.BlockSpec(memory_space=pltpu.VMEM)
IN_HBM = pl.BlockSpec(memory_space=pltpu.HBM)


def params(mebibytes=48):
    return pltpu.CompilerParams(vmem_limit_bytes=mebibytes * 1024 * 1024)


def place_in_group():
    return lax.axis_index("ctx") % HEADS


def pack_kernel(query_ref, key_ref, value_ref, *refs):
    outs = [refs[0:2], *([ref.at[0], ref.at[1]] for ref in refs[2 : 1 + len(FLIPS)])]
    rows, turned, sems = refs[1 + len(FLIPS) :]
    head_size = outs[0][0].shape[1]
    place = place_in_group()
    arrivals = [
        pltpu.make_async_copy(ref.at[0], rows.at[part], sems.at[part])
        for part, ref in enumerate((query_ref, key_ref, value_ref))
    ]
    for copy in arrivals:
        copy.start()
    for part, copy in enumerate(arrivals):
        copy.wait()
        turned[part] = rows[part].T
        for flip, out_ref in zip(FLIPS, outs):
            for other in range(2):
                head = pl.multiple_of((place ^ (flip + other)) * head_size, 32)
                out_ref[other][part] = turned[part, pl.ds(head, head_size), :]


def pack(queries, key_rows, value_rows):
    _, frames, features = queries.shape
    block = (3, features // HEADS, frames)
    own = pltpu.VMEM(block, queries.dtype)
    two = pltpu.VMEM((2, *block), queries.dtype)
    return pl.pallas_call(
        pack_kernel,
        out_shape=[own] * 2 + [two] * (len(FLIPS) - 1),
        in_specs=[IN_HBM] * 3,
        out_specs=[WHOLE] * (1 + len(FLIPS)),
        scratch_shapes=[
            pltpu.VMEM((3, frames, features), queries.dtype),
            pltpu.VMEM((3, features, frames), queries.dtype),
            pltpu.SemaphoreType.DMA((3,)),
        ],
        compiler_params=params(24),
        name="pack_heads",
    )(*(pltpu.with_memory_space_constraint(array, pltpu.HBM) for array in (queries, key_rows, value_rows)))


def attention_kernel(groups, lengths_ref, *refs):
    same, other = refs[: len(FLIPS)], refs[len(FLIPS) : 2 * len(FLIPS)]
    rest_ref = refs[2 * len(FLIPS)] if groups > 1 else None
    outs, (keys, values) = refs[-2 - len(FLIPS) : -2], refs[-2:]
    head_size, block = outs[0].shape[1:]
    place = place_in_group()
    scale = jnp.float32(math.log2(math.e) / math.sqrt(head_size))
    pad = keys.shape[1] - head_size

    def piece(flip, part):
        if flip < 2:
            return (same, other)[flip][0][part]
        return other[flip // 2][1, part] if flip % 2 else same[flip // 2][0, part]

    ones = jnp.where(lax.broadcasted_iota(jnp.int32, (pad, block), 0) == 0, 1.0, 0.0).astype(keys.dtype)
    for at in range(groups * HEADS):
        here = slice(at * block, (at + 1) * block)
        keys[here, :head_size] = (piece(at, 1) if groups == 1 else rest_ref[at, 0]).T
        values[:head_size, here] = piece(at, 2) if groups == 1 else rest_ref[at, 1]
        values[head_size:, here] = ones
    at_frame = lax.broadcasted_iota(jnp.int32, (block, pad), 0)
    at_feature = lax.broadcasted_iota(jnp.int32, (block, pad), 1)
    for at in range(groups * HEADS):
        frame = (at // HEADS * HEADS + (place ^ (at % HEADS))) * block + at_frame
        bias = jnp.where((at_feature == 0) & (frame >= lengths_ref[:1, :pad]), -1e30, 0.0)
        keys[at * block : (at + 1) * block, head_size:] = bias.astype(keys.dtype)

    def score(flip):
        query = [jnp.concatenate([piece(flip + half, 0), ones], axis=0) for half in range(2)]
        return jnp.dot(keys[...], jnp.concatenate(query, axis=1), preferred_element_type=jnp.float32)

    later = score(0)
    for flip, out_ref in zip(FLIPS, outs):
        scores = later
        if flip + 2 < HEADS:
            later = score(flip + 2)
        row_max = jnp.max(scores, axis=0, keepdims=True) * scale
        probs = jnp.exp2(scores * scale - row_max).astype(jnp.bfloat16)
        mixed = jnp.dot(values[...], probs, preferred_element_type=jnp.float32)
        mixed = (mixed[:head_size] / mixed[head_size : head_size + 1]).astype(jnp.bfloat16)
        for half in range(2):
            out_ref[half] = mixed[:, half * block : (half + 1) * block]


def attend(lengths, same, other, rest, groups):
    _, head_size, block = other[0].shape
    keys = groups * HEADS * block
    padded = head_size + 32
    queries = HEADS * block
    rest = [] if rest is None else [rest]
    return pl.pallas_call(
        functools.partial(attention_kernel, groups),
        out_shape=[jax.ShapeDtypeStruct((2, head_size, block), jnp.bfloat16)] * len(FLIPS),
        in_specs=[WHOLE] * (1 + 2 * len(FLIPS) + len(rest)),
        out_specs=[WHOLE] * len(FLIPS),
        scratch_shapes=[
            pltpu.VMEM((keys, padded), jnp.bfloat16),
            pltpu.VMEM((padded, keys), jnp.bfloat16),
        ],
        compiler_params=params(24),
        cost_estimate=pl.CostEstimate(
            flops=4 * queries * keys * head_size,
            bytes_accessed=4 * (queries + keys) * head_size,
            transcendentals=queries * keys,
        ),
        name="attend_one_head",
    )(lengths, *same, *other, *rest)


def quarter_of(place, parity, core):
    return (((place >> 2) ^ (place >> 1) ^ parity) & 1) * 2 + ((place ^ core) & 1)


def project_kernel(shards, *refs):
    each = len(FLIPS)
    heads_same, heads_other, pieces = refs[:each], refs[each : 2 * each], refs[2 * each : 2 * each + 6]
    own_ref = refs[2 * each + 6] if shards > 1 else None
    out_ref, turned, weight = refs[-3:]
    place = place_in_group()
    rows = turned.shape[0] // HEADS
    for flip in range(HEADS):
        here = pl.ds(pl.multiple_of((place ^ flip) * rows, 32), rows)
        turned[here, :] = heads_other[flip // 2][1] if flip % 2 else heads_same[flip // 2][0]
    rows = weight.shape[0] // 4
    for core in range(2):
        quarter, first, second = pieces[3 * core : 3 * core + 3]
        here = pl.multiple_of(quarter_of(place, 0, core) * rows, 32)
        weight[pl.ds(here, rows), :] = quarter[...]
        here = pl.multiple_of(quarter_of(place, 1, core) * rows, 32)
        weight[pl.ds(here, rows // 2), :] = first[...]
        weight[pl.ds(here + rows // 2, rows // 2), :] = second[...]
    attention = turned[...].T
    foreign = jnp.dot(attention, weight[...], preferred_element_type=jnp.float32).astype(out_ref.dtype)
    if shards == 1:
        out_ref[0] = foreign
        return
    columns = own_ref.shape[1]
    shard = lax.axis_index("fsdp")
    own = jnp.dot(attention, own_ref[...], preferred_element_type=jnp.float32).astype(out_ref.dtype)
    out_ref[0, :, pl.ds(pl.multiple_of(shard * columns, 128), columns)] = own
    for flip in range(1, shards):
        here = pl.ds(pl.multiple_of((shard ^ flip) * columns, 128), columns)
        out_ref[0, :, here] = foreign[:, (flip - 1) * columns : flip * columns]


def project(heads_same, heads_other, near, far, own, shards):
    _, rows, frames = heads_other[0].shape
    foreign = near[0].shape[1]
    width = foreign + (own[0].shape[1] if own else 0)
    features = HEADS * rows
    pieces = [*heads_same, *heads_other, *near, *far, *own]
    return pl.pallas_call(
        functools.partial(project_kernel, shards),
        out_shape=jax.ShapeDtypeStruct((1, frames, width), jnp.bfloat16),
        in_specs=[WHOLE] * len(pieces),
        out_specs=WHOLE,
        scratch_shapes=[pltpu.VMEM((features, frames), jnp.bfloat16), pltpu.VMEM((features, foreign), jnp.bfloat16)],
        compiler_params=params(24),
        cost_estimate=pl.CostEstimate(
            flops=2 * features * frames * width, bytes_accessed=2 * features * width, transcendentals=0
        ),
        name="project_heads",
    )(*pieces)


def per_device(ctx, fsdp, queries, key_rows, value_rows, lengths, out_weight):
    def exchange(array, axis, flip):
        size = ctx if axis == "ctx" else fsdp
        return lax.ppermute(array, axis, [(i, i ^ flip) for i in range(size)])

    place = place_in_group()
    rows = out_weight.shape[0] // 4
    quarter = lax.dynamic_slice_in_dim(out_weight, quarter_of(place, 0, 0) * rows, rows, 0)
    split_columns = fsdp == 4
    lengths = jnp.broadcast_to(lengths, (8, 128))
    if split_columns:
        one, two = exchange(quarter, "fsdp", 1), exchange(quarter, "fsdp", 2)
        two, lengths = lax.optimization_barrier((two, lengths))
        quarter = jnp.concatenate([one, two, exchange(two, "fsdp", 1)], axis=1)
    else:
        quarter = lax.all_gather(quarter, "fsdp", axis=1, tiled=True)

    own_same, own_other, *by_chip = pack(queries, key_rows, value_rows)
    same = [exchange(array, "ctx", flip) for flip, array in zip(FLIPS[1:], by_chip)]
    same = lax.optimization_barrier(same)
    other = [exchange(array, "ctx", 1) for array in (own_other, *same)]
    quarter, other = lax.optimization_barrier((quarter, other))
    first = exchange(quarter[: rows // 2], "ctx", 2)
    second = exchange(quarter[rows // 2 :], "ctx", 4)

    groups = ctx // HEADS
    rest = None
    if groups > 1:
        pairs = [own_same[1:], other[0][1:]]
        for one, two in zip(same, other[1:]):
            pairs += [one[0, 1:], two[1, 1:]]
        across = [[head + first for first in range(0, ctx, HEADS)] for head in range(HEADS)]
        rest = lax.all_gather(jnp.stack(pairs), "ctx", axis=0, axis_index_groups=across, tiled=True)
    mixed = attend(lengths, [own_same, *same], other, rest, groups)

    far = exchange(quarter, "ctx", 1)
    first, second, far, last = lax.optimization_barrier((first, second, far, mixed[2]))
    heads = [exchange(array, "ctx", flip) for flip, array in zip(FLIPS[1:], (mixed[1], last, mixed[3]))]
    heads, first, second = lax.optimization_barrier((heads, first, second))
    near = [quarter, first, second]
    far = [far, exchange(first, "ctx", 1), exchange(second, "ctx", 1)]
    heads_same = [mixed[0], *heads]
    heads_other = [exchange(array, "ctx", 1) for array in heads_same]
    own = [out_weight] if split_columns else []
    return project(heads_same, heads_other, near, far, own, fsdp if split_columns else 1)


def solution(mesh):
    return jax.shard_map(
        functools.partial(per_device, mesh.shape["ctx"], mesh.shape["fsdp"]),
        mesh=mesh,
        in_specs=(
            P("fsdp", "ctx", None),
            P("fsdp", "ctx", None),
            P("fsdp", "ctx", None),
            P("fsdp"),
            P(None, "fsdp"),
        ),
        out_specs=P("fsdp", "ctx", None),
        check_vma=False,
    )
```

```python
import functools
import math

import jax
import jax.numpy as jnp
from jax import lax
from jax.experimental import pallas as pl
from jax.experimental.pallas import tpu as pltpu
from jax.sharding import PartitionSpec as P

HEADS = 8
FLIPS = tuple(range(0, HEADS, 2))
WHOLE = pl.BlockSpec(memory_space=pltpu.VMEM)
IN_HBM = pl.BlockSpec(memory_space=pltpu.HBM)


def params(mebibytes=48):
    return pltpu.CompilerParams(vmem_limit_bytes=mebibytes * 1024 * 1024)


def place_in_group():
    return lax.axis_index("ctx") % HEADS


def pack_kernel(query_ref, key_ref, value_ref, *refs):
    outs = [refs[0:2], *([ref.at[0], ref.at[1]] for ref in refs[2 : 1 + len(FLIPS)])]
    rows, turned, sems = refs[1 + len(FLIPS) :]
    head_size = outs[0][0].shape[1]
    place = place_in_group()
    arrivals = [
        pltpu.make_async_copy(ref.at[0], rows.at[part], sems.at[part])
        for part, ref in enumerate((query_ref, key_ref, value_ref))
    ]
    for copy in arrivals:
        copy.start()
    for part, copy in enumerate(arrivals):
        copy.wait()
        turned[part] = rows[part].T
        for flip, out_ref in zip(FLIPS, outs):
            for other in range(2):
                head = pl.multiple_of((place ^ (flip + other)) * head_size, 32)
                out_ref[other][part] = turned[part, pl.ds(head, head_size), :]


def pack(queries, key_rows, value_rows):
    _, frames, features = queries.shape
    block = (3, features // HEADS, frames)
    own = pltpu.VMEM(block, queries.dtype)
    two = pltpu.VMEM((2, *block), queries.dtype)
    return pl.pallas_call(
        pack_kernel,
        out_shape=[own] * 2 + [two] * (len(FLIPS) - 1),
        in_specs=[IN_HBM] * 3,
        out_specs=[WHOLE] * (1 + len(FLIPS)),
        scratch_shapes=[
            pltpu.VMEM((3, frames, features), queries.dtype),
            pltpu.VMEM((3, features, frames), queries.dtype),
            pltpu.SemaphoreType.DMA((3,)),
        ],
        compiler_params=params(24),
        name="pack_heads",
    )(*(pltpu.with_memory_space_constraint(array, pltpu.HBM) for array in (queries, key_rows, value_rows)))


def attention_kernel(groups, lengths_ref, *refs):
    same, other = refs[: len(FLIPS)], refs[len(FLIPS) : 2 * len(FLIPS)]
    rest_ref = refs[2 * len(FLIPS)] if groups > 1 else None
    outs, (keys, values) = refs[-2 - len(FLIPS) : -2], refs[-2:]
    head_size, block = outs[0].shape[1:]
    place = place_in_group()
    scale = jnp.float32(math.log2(math.e) / math.sqrt(head_size))
    pad = keys.shape[1] - head_size

    def piece(flip, part):
        if flip % 2:
            return other[flip // 2][1, part] if flip > 1 else other[0][part]
        return same[flip // 2][0, part] if flip else same[0][part]

    ones = jnp.where(lax.broadcasted_iota(jnp.int32, (pad, block), 0) == 0, 1.0, 0.0).astype(keys.dtype)
    for at in range(groups * HEADS):
        here = slice(at * block, (at + 1) * block)
        keys[here, :head_size] = (piece(at, 1) if groups == 1 else rest_ref[at, 0]).T
        values[:head_size, here] = piece(at, 2) if groups == 1 else rest_ref[at, 1]
        values[head_size:, here] = ones
    at_frame = lax.broadcasted_iota(jnp.int32, (block, pad), 0)
    at_feature = lax.broadcasted_iota(jnp.int32, (block, pad), 1)
    for at in range(groups * HEADS):
        frame = (at // HEADS * HEADS + (place ^ (at % HEADS))) * block + at_frame
        bias = jnp.where((at_feature == 0) & (frame >= lengths_ref[:1, :pad]), -1e30, 0.0)
        keys[at * block : (at + 1) * block, head_size:] = bias.astype(keys.dtype)

    def score(flip):
        query = [jnp.concatenate([piece(flip + half, 0), ones], axis=0) for half in range(2)]
        return jnp.dot(keys[...], jnp.concatenate(query, axis=1), preferred_element_type=jnp.float32)

    later = score(0)
    for flip, out_ref in zip(FLIPS, outs):
        scores = later
        if flip + 2 < HEADS:
            later = score(flip + 2)
        row_max = jnp.max(scores, axis=0, keepdims=True) * scale
        probs = jnp.exp2(scores * scale - row_max).astype(jnp.bfloat16)
        mixed = jnp.dot(values[...], probs, preferred_element_type=jnp.float32)
        mixed = (mixed[:head_size] / mixed[head_size : head_size + 1]).astype(jnp.bfloat16)
        for half in range(2):
            out_ref[half] = mixed[:, half * block : (half + 1) * block]


def attend(lengths, same, other, rest, groups):
    _, head_size, block = other[0].shape
    keys = groups * HEADS * block
    padded = head_size + 32
    rest = [] if rest is None else [rest]
    return pl.pallas_call(
        functools.partial(attention_kernel, groups),
        out_shape=[jax.ShapeDtypeStruct((2, head_size, block), jnp.bfloat16)] * len(FLIPS),
        in_specs=[WHOLE] * (1 + 2 * len(FLIPS) + len(rest)),
        out_specs=[WHOLE] * len(FLIPS),
        scratch_shapes=[
            pltpu.VMEM((keys, padded), jnp.bfloat16),
            pltpu.VMEM((padded, keys), jnp.bfloat16),
        ],
        compiler_params=params(24),
        cost_estimate=pl.CostEstimate(flops=0, bytes_accessed=0, transcendentals=0),
        name="attend_one_head",
    )(lengths, *same, *other, *rest)


def second_entries_kernel(*refs):
    for at, ref in enumerate(refs[:-1]):
        refs[-1][at] = ref[1]


def second_entries(arrays):
    return pl.pallas_call(
        second_entries_kernel,
        out_shape=jax.ShapeDtypeStruct((len(arrays), *arrays[0].shape[1:]), arrays[0].dtype),
        in_specs=[WHOLE] * len(arrays),
        out_specs=WHOLE,
        compiler_params=params(16),
        name="second_entries",
    )(*arrays)


def parity_of(place):
    return ((place >> 2) ^ (place >> 1)) & 1


def project_kernel(shards, *refs):
    each = len(FLIPS)
    heads_same, heads_other, pieces = refs[:each], refs[each], refs[each + 1 : -3]
    out_ref, turned, weight = refs[-3:]
    place = place_in_group()
    core, parity = place & 1, parity_of(place)
    rows = turned.shape[0] // HEADS
    for flip in range(HEADS):
        here = pl.ds(pl.multiple_of((place ^ flip) * rows, 32), rows)
        turned[here, :] = heads_other[flip // 2] if flip % 2 else heads_same[flip // 2][0]
    half = weight.shape[0] // 2
    if shards == 1:
        for other, ref in enumerate(pieces):
            weight[pl.ds(pl.multiple_of((core ^ other) * half, 32), half), :] = ref[...]
    else:
        *pieces, own_ref = pieces
        columns = own_ref.shape[1]
        part = pieces[2].shape[0]
        for other in range(2):
            fetched, passed, third, third_passed = pieces[4 * other : 4 * other + 4]
            near = pl.ds(pl.multiple_of((1 - (core ^ other)) * columns, 128), columns)
            last = slice(2 * columns, 3 * columns)
            for flip, whole_ref, part_ref in ((0, fetched, third), (1, passed, third_passed)):
                first = (parity ^ flip) * half
                weight[pl.ds(pl.multiple_of(first, 32), half), near] = whole_ref[...]
                first = first + (core ^ other) * (half - part)
                weight[pl.ds(pl.multiple_of(first, 16), part), last] = part_ref[...]
    attention = turned[...].T
    foreign = jnp.dot(attention, weight[...], preferred_element_type=jnp.float32).astype(out_ref.dtype)
    if shards == 1:
        out_ref[0] = foreign
        return
    shard = lax.axis_index("fsdp")
    own = jnp.dot(attention, own_ref[...], preferred_element_type=jnp.float32).astype(out_ref.dtype)
    out_ref[0, :, pl.ds(pl.multiple_of(shard * columns, 128), columns)] = own
    for flip in range(1, shards):
        here = pl.ds(pl.multiple_of((shard ^ flip) * columns, 128), columns)
        out_ref[0, :, here] = foreign[:, (flip - 1) * columns : flip * columns]


def project(heads_same, heads_other, pieces, own, shards):
    _, rows, frames = heads_other.shape
    foreign = (shards - 1) * own[0].shape[1] if own else pieces[0].shape[1]
    width = foreign + (own[0].shape[1] if own else 0)
    features = HEADS * rows
    pieces = [*heads_same, heads_other, *pieces, *own]
    return pl.pallas_call(
        functools.partial(project_kernel, shards),
        out_shape=jax.ShapeDtypeStruct((1, frames, width), jnp.bfloat16),
        in_specs=[WHOLE] * len(pieces),
        out_specs=WHOLE,
        scratch_shapes=[pltpu.VMEM((features, frames), jnp.bfloat16), pltpu.VMEM((features, foreign), jnp.bfloat16)],
        compiler_params=params(24),
        cost_estimate=pl.CostEstimate(
            flops=2 * features * frames * width, bytes_accessed=2 * features * width, transcendentals=0
        ),
        name="project_heads",
    )(*pieces)


def per_device(ctx, fsdp, queries, key_rows, value_rows, lengths, out_weight):
    def exchange(array, axis, flip):
        size = ctx if axis == "ctx" else fsdp
        return lax.ppermute(array, axis, [(i, i ^ flip) for i in range(size)])

    def exchange_in_plane(array):
        return lax.ppermute(array, "ctx", [(i, i ^ (4 if i % 2 else 2)) for i in range(ctx)])

    def exchange_along(array, *flips):
        pairs = [(i * fsdp + z, i * fsdp + (z ^ flips[i % 2])) for i in range(ctx) for z in range(fsdp)]
        return lax.ppermute(array, ("ctx", "fsdp"), pairs)

    place = place_in_group()
    core = place & 1
    rows = out_weight.shape[0] // 2
    split_columns = fsdp == 4
    lengths = jnp.broadcast_to(lengths, (8, 128))
    if split_columns:
        half = lax.dynamic_slice_in_dim(out_weight, parity_of(place) * rows, rows, 0)
        fetched = exchange_along(half, 2, 1)
        part = rows // 2 + 16
        third = lax.dynamic_slice_in_dim(fetched, core * (rows - part), part, 0)
        third = exchange_along(third, 1, 2)
        passed = exchange_in_plane(fetched)
        fetched_other = exchange(fetched, "ctx", 1)
    else:
        half = lax.dynamic_slice_in_dim(out_weight, core * rows, rows, 0)
        half = lax.all_gather(half, "fsdp", axis=1, tiled=True)

    own_same, own_other, *by_chip = pack(queries, key_rows, value_rows)
    same = [exchange(array, "ctx", flip) for flip, array in zip(FLIPS[1:], by_chip)]
    same, own_other = lax.optimization_barrier((same, exchange(own_other, "ctx", 1)))
    other = [own_other, *(exchange(array, "ctx", 1) for array in same)]

    groups = ctx // HEADS
    rest = None
    if groups > 1:
        pairs = [own_same[1:], own_other[1:]]
        for one, two in zip(same, other[1:]):
            pairs += [one[0, 1:], two[1, 1:]]
        across = [[head + first for first in range(0, ctx, HEADS)] for head in range(HEADS)]
        rest = lax.all_gather(jnp.stack(pairs), "ctx", axis=0, axis_index_groups=across, tiled=True)
    mixed = attend(lengths, [own_same, *same], other, rest, groups)

    own = []
    if split_columns:
        third, passed, last = lax.optimization_barrier((third, passed, mixed[2]))
        mixed = [*mixed[:2], last, mixed[3]]
        third_passed = exchange_in_plane(third)
    heads = [exchange(array, "ctx", flip) for flip, array in zip(FLIPS[1:], mixed[1:])]
    if split_columns:
        heads, third_passed = lax.optimization_barrier((heads, third_passed))
        pieces = [fetched, passed, third, third_passed]
        pieces += [fetched_other, *(exchange(array, "ctx", 1) for array in pieces[1:])]
        own = [out_weight]
    else:
        pieces = [half, exchange(half, "ctx", 1)]
    heads_same = [mixed[0], *heads]
    heads_other = exchange(second_entries(heads_same), "ctx", 1)
    return project(heads_same, heads_other, pieces, own, fsdp if split_columns else 1)


def solution(mesh):
    return jax.shard_map(
        functools.partial(per_device, mesh.shape["ctx"], mesh.shape["fsdp"]),
        mesh=mesh,
        in_specs=(
            P("fsdp", "ctx", None),
            P("fsdp", "ctx", None),
            P("fsdp", "ctx", None),
            P("fsdp"),
            P(None, "fsdp"),
        ),
        out_specs=P("fsdp", "ctx", None),
        check_vma=False,
    )
```

```python
import functools
import math

import jax
import jax.numpy as jnp
from jax import lax
from jax.experimental import pallas as pl
from jax.experimental.pallas import tpu as pltpu
from jax.sharding import PartitionSpec as P

HEADS = 8
FLIPS = tuple(range(0, HEADS, 2))
WHOLE = pl.BlockSpec(memory_space=pltpu.VMEM)
IN_HBM = pl.BlockSpec(memory_space=pltpu.HBM)


def params(mebibytes=48):
    return pltpu.CompilerParams(vmem_limit_bytes=mebibytes * 1024 * 1024)


def place_in_group():
    return lax.axis_index("ctx") % HEADS


def pack_kernel(query_ref, key_ref, value_ref, *refs):
    outs = [refs[0:2], *([ref.at[0], ref.at[1]] for ref in refs[2 : 1 + len(FLIPS)])]
    rows, turned, sems = refs[1 + len(FLIPS) :]
    head_size = outs[0][0].shape[1]
    place = place_in_group()
    arrivals = [
        pltpu.make_async_copy(ref.at[0], rows.at[part], sems.at[part])
        for part, ref in enumerate((query_ref, key_ref, value_ref))
    ]
    for copy in arrivals:
        copy.start()
    for part, copy in enumerate(arrivals):
        copy.wait()
        turned[part] = rows[part].T
        for flip, out_ref in zip(FLIPS, outs):
            for other in range(2):
                head = pl.multiple_of((place ^ (flip + other)) * head_size, 32)
                out_ref[other][part] = turned[part, pl.ds(head, head_size), :]


def pack(queries, key_rows, value_rows):
    _, frames, features = queries.shape
    block = (3, features // HEADS, frames)
    own = pltpu.VMEM(block, queries.dtype)
    two = pltpu.VMEM((2, *block), queries.dtype)
    return pl.pallas_call(
        pack_kernel,
        out_shape=[own] * 2 + [two] * (len(FLIPS) - 1),
        in_specs=[IN_HBM] * 3,
        out_specs=[WHOLE] * (1 + len(FLIPS)),
        scratch_shapes=[
            pltpu.VMEM((3, frames, features), queries.dtype),
            pltpu.VMEM((3, features, frames), queries.dtype),
            pltpu.SemaphoreType.DMA((3,)),
        ],
        compiler_params=params(24),
        name="pack_heads",
    )(*(pltpu.with_memory_space_constraint(array, pltpu.HBM) for array in (queries, key_rows, value_rows)))


def attention_kernel(groups, lengths_ref, *refs):
    same, other = refs[: len(FLIPS)], refs[len(FLIPS) : 2 * len(FLIPS)]
    rest_ref = refs[2 * len(FLIPS)] if groups > 1 else None
    outs, (keys, values) = refs[-2 - len(FLIPS) : -2], refs[-2:]
    head_size, block = outs[0].shape[1:]
    place = place_in_group()
    scale = jnp.float32(math.log2(math.e) / math.sqrt(head_size))
    pad = keys.shape[1] - head_size

    def piece(flip, part):
        if flip % 2:
            return other[flip // 2][1, part] if flip > 1 else other[0][part]
        return same[flip // 2][0, part] if flip else same[0][part]

    ones = jnp.where(lax.broadcasted_iota(jnp.int32, (pad, block), 0) == 0, 1.0, 0.0).astype(keys.dtype)
    for at in range(groups * HEADS):
        here = slice(at * block, (at + 1) * block)
        keys[here, :head_size] = (piece(at, 1) if groups == 1 else rest_ref[at, 0]).T
        values[:head_size, here] = piece(at, 2) if groups == 1 else rest_ref[at, 1]
        values[head_size:, here] = ones
    at_frame = lax.broadcasted_iota(jnp.int32, (block, pad), 0)
    at_feature = lax.broadcasted_iota(jnp.int32, (block, pad), 1)
    for at in range(groups * HEADS):
        frame = (at // HEADS * HEADS + (place ^ (at % HEADS))) * block + at_frame
        bias = jnp.where((at_feature == 0) & (frame >= lengths_ref[:1, :pad]), -1e30, 0.0)
        keys[at * block : (at + 1) * block, head_size:] = bias.astype(keys.dtype)

    def score(flip):
        query = [jnp.concatenate([piece(flip + half, 0), ones], axis=0) for half in range(2)]
        return jnp.dot(keys[...], jnp.concatenate(query, axis=1), preferred_element_type=jnp.float32)

    later = score(0)
    for flip, out_ref in zip(FLIPS, outs):
        scores = later
        if flip + 2 < HEADS:
            later = score(flip + 2)
        row_max = jnp.max(scores, axis=0, keepdims=True) * scale
        probs = jnp.exp2(scores * scale - row_max).astype(jnp.bfloat16)
        mixed = jnp.dot(values[...], probs, preferred_element_type=jnp.float32)
        mixed = (mixed[:head_size] / mixed[head_size : head_size + 1]).astype(jnp.bfloat16)
        for half in range(2):
            out_ref[half] = mixed[:, half * block : (half + 1) * block]


def attend(lengths, same, other, rest, groups):
    _, head_size, block = other[0].shape
    keys = groups * HEADS * block
    padded = head_size + 32
    rest = [] if rest is None else [rest]
    return pl.pallas_call(
        functools.partial(attention_kernel, groups),
        out_shape=[jax.ShapeDtypeStruct((2, head_size, block), jnp.bfloat16)] * len(FLIPS),
        in_specs=[WHOLE] * (1 + 2 * len(FLIPS) + len(rest)),
        out_specs=[WHOLE] * len(FLIPS),
        scratch_shapes=[
            pltpu.VMEM((keys, padded), jnp.bfloat16),
            pltpu.VMEM((padded, keys), jnp.bfloat16),
        ],
        compiler_params=params(24),
        cost_estimate=pl.CostEstimate(flops=0, bytes_accessed=0, transcendentals=0),
        name="attend_one_head",
    )(lengths, *same, *other, *rest)


def second_entries_kernel(*refs):
    for at, ref in enumerate(refs[:-1]):
        refs[-1][at] = ref[1]


def second_entries(arrays):
    return pl.pallas_call(
        second_entries_kernel,
        out_shape=jax.ShapeDtypeStruct((len(arrays), *arrays[0].shape[1:]), arrays[0].dtype),
        in_specs=[WHOLE] * len(arrays),
        out_specs=WHOLE,
        compiler_params=params(16),
        name="second_entries",
    )(*arrays)


def parity_of(place):
    return ((place >> 2) ^ (place >> 1)) & 1


def project_kernel(shards, *refs):
    each = len(FLIPS)
    heads_same, heads_other, pieces = refs[:each], refs[each], refs[each + 1 : -3]
    out_ref, turned, weight = refs[-3:]
    place = place_in_group()
    core, parity = place & 1, parity_of(place)
    rows = turned.shape[0] // HEADS
    for flip in range(HEADS):
        here = pl.ds(pl.multiple_of((place ^ flip) * rows, 32), rows)
        turned[here, :] = heads_other[flip // 2] if flip % 2 else heads_same[flip // 2][0]
    half = weight.shape[0] // 2
    if shards == 1:
        for other, ref in enumerate(pieces):
            weight[pl.ds(pl.multiple_of((core ^ other) * half, 32), half), :] = ref[...]
    else:
        *pieces, own_ref = pieces
        columns = own_ref.shape[1]
        part = pieces[2].shape[0]
        for other in range(2):
            fetched, passed, third, third_passed = pieces[4 * other : 4 * other + 4]
            near = pl.ds(pl.multiple_of((1 - (core ^ other)) * columns, 128), columns)
            last = slice(2 * columns, 3 * columns)
            for flip, whole_ref, part_ref in ((0, fetched, third), (1, passed, third_passed)):
                first = (parity ^ flip) * half
                weight[pl.ds(pl.multiple_of(first, 32), half), near] = whole_ref[...]
                first = first + (core ^ other) * (half - part)
                weight[pl.ds(pl.multiple_of(first, 16), part), last] = part_ref[...]
    attention = turned[...].T
    foreign = jnp.dot(attention, weight[...], preferred_element_type=jnp.float32).astype(out_ref.dtype)
    if shards == 1:
        out_ref[0] = foreign
        return
    shard = lax.axis_index("fsdp")
    own = jnp.dot(attention, own_ref[...], preferred_element_type=jnp.float32).astype(out_ref.dtype)
    out_ref[0, :, pl.ds(pl.multiple_of(shard * columns, 128), columns)] = own
    for flip in range(1, shards):
        here = pl.ds(pl.multiple_of((shard ^ flip) * columns, 128), columns)
        out_ref[0, :, here] = foreign[:, (flip - 1) * columns : flip * columns]


def project(heads_same, heads_other, pieces, own, shards):
    _, rows, frames = heads_other.shape
    foreign = (shards - 1) * own[0].shape[1] if own else pieces[0].shape[1]
    width = foreign + (own[0].shape[1] if own else 0)
    features = HEADS * rows
    pieces = [*heads_same, heads_other, *pieces, *own]
    return pl.pallas_call(
        functools.partial(project_kernel, shards),
        out_shape=jax.ShapeDtypeStruct((1, frames, width), jnp.bfloat16),
        in_specs=[WHOLE] * len(pieces),
        out_specs=WHOLE,
        scratch_shapes=[pltpu.VMEM((features, frames), jnp.bfloat16), pltpu.VMEM((features, foreign), jnp.bfloat16)],
        compiler_params=params(24),
        cost_estimate=pl.CostEstimate(
            flops=2 * features * frames * width, bytes_accessed=2 * features * width, transcendentals=0
        ),
        name="project_heads",
    )(*pieces)


def per_device(ctx, fsdp, queries, key_rows, value_rows, lengths, out_weight):
    def exchange(array, axis, flip):
        size = ctx if axis == "ctx" else fsdp
        return lax.ppermute(array, axis, [(i, i ^ flip) for i in range(size)])

    def exchange_in_plane(array):
        return lax.ppermute(array, "ctx", [(i, i ^ (4 if i % 2 else 2)) for i in range(ctx)])

    def exchange_along(array, *flips):
        pairs = [(i * fsdp + z, i * fsdp + (z ^ flips[i % 2])) for i in range(ctx) for z in range(fsdp)]
        return lax.ppermute(array, ("ctx", "fsdp"), pairs)

    place = place_in_group()
    core = place & 1
    rows = out_weight.shape[0] // 2
    split_columns = fsdp == 4
    lengths = jnp.broadcast_to(lengths, (8, 128))
    if split_columns:
        half = lax.dynamic_slice_in_dim(out_weight, parity_of(place) * rows, rows, 0)
        fetched = exchange_along(half, 2, 1)
    else:
        half = lax.dynamic_slice_in_dim(out_weight, core * rows, rows, 0)
        half = lax.all_gather(half, "fsdp", axis=1, tiled=True)

    own_same, own_other, *by_chip = pack(queries, key_rows, value_rows)
    same = [exchange(array, "ctx", flip) for flip, array in zip(FLIPS[1:], by_chip)]
    own_other = exchange(own_other, "ctx", 1)
    if split_columns:
        fetched, own_other = lax.optimization_barrier((fetched, own_other))
        passed = exchange_in_plane(fetched)
        part = rows // 2 + 16
        third = lax.dynamic_slice_in_dim(fetched, core * (rows - part), part, 0)
        third = exchange_along(third, 1, 2)
        third_passed = exchange_in_plane(third)
    same, own_other = lax.optimization_barrier((same, own_other))
    other = [own_other, *(exchange(array, "ctx", 1) for array in same)]

    groups = ctx // HEADS
    rest = None
    if groups > 1:
        pairs = [own_same[1:], own_other[1:]]
        for one, two in zip(same, other[1:]):
            pairs += [one[0, 1:], two[1, 1:]]
        across = [[head + first for first in range(0, ctx, HEADS)] for head in range(HEADS)]
        rest = lax.all_gather(jnp.stack(pairs), "ctx", axis=0, axis_index_groups=across, tiled=True)
    mixed = attend(lengths, [own_same, *same], other, rest, groups)

    heads = [exchange(array, "ctx", flip) for flip, array in zip(FLIPS[1:], mixed[1:])]
    own = []
    if split_columns:
        heads, fetched, passed, third = lax.optimization_barrier((heads, fetched, passed, third))
        pieces = [fetched, passed, third]
        others = [exchange(array, "ctx", 1) for array in pieces]
    heads_same = [mixed[0], *heads]
    heads_other = exchange(second_entries(heads_same), "ctx", 1)
    if split_columns:
        third_passed, heads_other = lax.optimization_barrier((third_passed, heads_other))
        pieces += [third_passed, *others, exchange(third_passed, "ctx", 1)]
        own = [out_weight]
    else:
        pieces = [half, exchange(half, "ctx", 1)]
    return project(heads_same, heads_other, pieces, own, fsdp if split_columns else 1)


def solution(mesh):
    return jax.shard_map(
        functools.partial(per_device, mesh.shape["ctx"], mesh.shape["fsdp"]),
        mesh=mesh,
        in_specs=(
            P("fsdp", "ctx", None),
            P("fsdp", "ctx", None),
            P("fsdp", "ctx", None),
            P("fsdp"),
            P(None, "fsdp"),
        ),
        out_specs=P("fsdp", "ctx", None),
        check_vma=False,
    )
```

```python
import functools
import math

import jax
import jax.numpy as jnp
from jax import lax
from jax.experimental import pallas as pl
from jax.experimental.pallas import tpu as pltpu
from jax.sharding import PartitionSpec as P

HEADS = 8
FLIPS = tuple(range(0, HEADS, 2))
WHOLE = pl.BlockSpec(memory_space=pltpu.VMEM)
IN_HBM = pl.BlockSpec(memory_space=pltpu.HBM)


def params(mebibytes=48):
    return pltpu.CompilerParams(vmem_limit_bytes=mebibytes * 1024 * 1024)


def place_in_group():
    return lax.axis_index("ctx") % HEADS


def pack_kernel(query_ref, key_ref, value_ref, *refs):
    outs = [refs[0:2], *([ref.at[0], ref.at[1]] for ref in refs[2 : 1 + len(FLIPS)])]
    rows, turned, sems = refs[1 + len(FLIPS) :]
    head_size = outs[0][0].shape[1]
    place = place_in_group()
    arrivals = [
        pltpu.make_async_copy(ref.at[0], rows.at[part], sems.at[part])
        for part, ref in enumerate((query_ref, key_ref, value_ref))
    ]
    for copy in arrivals:
        copy.start()
    for part, copy in enumerate(arrivals):
        copy.wait()
        turned[part] = rows[part].T
        for flip, out_ref in zip(FLIPS, outs):
            for other in range(2):
                head = pl.multiple_of((place ^ (flip + other)) * head_size, 32)
                out_ref[other][part] = turned[part, pl.ds(head, head_size), :]


def pack(queries, key_rows, value_rows):
    _, frames, features = queries.shape
    block = (3, features // HEADS, frames)
    own = pltpu.VMEM(block, queries.dtype)
    two = pltpu.VMEM((2, *block), queries.dtype)
    return pl.pallas_call(
        pack_kernel,
        out_shape=[own] * 2 + [two] * (len(FLIPS) - 1),
        in_specs=[IN_HBM] * 3,
        out_specs=[WHOLE] * (1 + len(FLIPS)),
        scratch_shapes=[
            pltpu.VMEM((3, frames, features), queries.dtype),
            pltpu.VMEM((3, features, frames), queries.dtype),
            pltpu.SemaphoreType.DMA((3,)),
        ],
        compiler_params=params(24),
        name="pack_heads",
    )(*(pltpu.with_memory_space_constraint(array, pltpu.HBM) for array in (queries, key_rows, value_rows)))


def attention_kernel(groups, lengths_ref, *refs):
    same, other = refs[: len(FLIPS)], refs[len(FLIPS) : 2 * len(FLIPS)]
    rest_ref = refs[2 * len(FLIPS)] if groups > 1 else None
    outs, (keys, values) = refs[-2 - len(FLIPS) : -2], refs[-2:]
    head_size, block = outs[0].shape[1:]
    place = place_in_group()
    scale = jnp.float32(math.log2(math.e) / math.sqrt(head_size))
    pad = keys.shape[1] - head_size

    def piece(flip, part):
        if flip % 2:
            return other[flip // 2][1, part] if flip > 1 else other[0][part]
        return same[flip // 2][0, part] if flip else same[0][part]

    ones = jnp.where(lax.broadcasted_iota(jnp.int32, (pad, block), 0) == 0, 1.0, 0.0).astype(keys.dtype)
    for at in range(groups * HEADS):
        here = slice(at * block, (at + 1) * block)
        keys[here, :head_size] = (piece(at, 1) if groups == 1 else rest_ref[at, 0]).T
        values[:head_size, here] = piece(at, 2) if groups == 1 else rest_ref[at, 1]
        values[head_size:, here] = ones
    at_frame = lax.broadcasted_iota(jnp.int32, (block, pad), 0)
    at_feature = lax.broadcasted_iota(jnp.int32, (block, pad), 1)
    for at in range(groups * HEADS):
        frame = (at // HEADS * HEADS + (place ^ (at % HEADS))) * block + at_frame
        bias = jnp.where((at_feature == 0) & (frame >= lengths_ref[:1, :pad]), -1e30, 0.0)
        keys[at * block : (at + 1) * block, head_size:] = bias.astype(keys.dtype)

    def score(flip):
        query = [jnp.concatenate([piece(flip + half, 0), ones], axis=0) for half in range(2)]
        return jnp.dot(keys[...], jnp.concatenate(query, axis=1), preferred_element_type=jnp.float32)

    later = score(0)
    for flip, out_ref in zip(FLIPS, outs):
        scores = later
        if flip + 2 < HEADS:
            later = score(flip + 2)
        row_max = jnp.max(scores, axis=0, keepdims=True) * scale
        probs = jnp.exp2(scores * scale - row_max).astype(jnp.bfloat16)
        mixed = jnp.dot(values[...], probs, preferred_element_type=jnp.float32)
        mixed = (mixed[:head_size] / mixed[head_size : head_size + 1]).astype(jnp.bfloat16)
        for half in range(2):
            out_ref[half] = mixed[:, half * block : (half + 1) * block]


def attend(lengths, same, other, rest, groups):
    _, head_size, block = other[0].shape
    keys = groups * HEADS * block
    padded = head_size + 32
    rest = [] if rest is None else [rest]
    return pl.pallas_call(
        functools.partial(attention_kernel, groups),
        out_shape=[jax.ShapeDtypeStruct((2, head_size, block), jnp.bfloat16)] * len(FLIPS),
        in_specs=[WHOLE] * (1 + 2 * len(FLIPS) + len(rest)),
        out_specs=[WHOLE] * len(FLIPS),
        scratch_shapes=[
            pltpu.VMEM((keys, padded), jnp.bfloat16),
            pltpu.VMEM((padded, keys), jnp.bfloat16),
        ],
        compiler_params=params(24),
        cost_estimate=pl.CostEstimate(flops=0, bytes_accessed=0, transcendentals=0),
        name="attend_one_head",
    )(lengths, *same, *other, *rest)


def second_entries_kernel(*refs):
    for at, ref in enumerate(refs[:-1]):
        refs[-1][at] = ref[1]


def second_entries(arrays):
    return pl.pallas_call(
        second_entries_kernel,
        out_shape=jax.ShapeDtypeStruct((len(arrays), *arrays[0].shape[1:]), arrays[0].dtype),
        in_specs=[WHOLE] * len(arrays),
        out_specs=WHOLE,
        compiler_params=params(16),
        name="second_entries",
    )(*arrays)


def parity_of(place):
    return ((place >> 2) ^ (place >> 1)) & 1


def gather_heads(heads_same, heads_other, turned):
    place = place_in_group()
    rows = turned.shape[0] // HEADS
    for flip in range(HEADS):
        here = pl.ds(pl.multiple_of((place ^ flip) * rows, 32), rows)
        turned[here, :] = heads_other[flip // 2] if flip % 2 else heads_same[flip // 2][0]


def project_kernel(*refs):
    each = len(FLIPS)
    heads_same, heads_other, halves = refs[:each], refs[each], refs[each + 1 : each + 3]
    out_ref, turned, weight = refs[each + 3 :]
    gather_heads(heads_same, heads_other, turned)
    half = weight.shape[0] // 2
    for other, ref in enumerate(halves):
        weight[pl.ds(pl.multiple_of(((place_in_group() & 1) ^ other) * half, 32), half), :] = ref[...]
    out_ref[0] = jnp.dot(turned[...].T, weight[...], preferred_element_type=jnp.float32).astype(out_ref.dtype)


def project_near_kernel(*refs):
    each = len(FLIPS)
    heads_same, heads_other, own_ref, pieces = refs[:each], refs[each], refs[each + 1], refs[each + 2 : each + 6]
    out_ref, attention_ref, turned, weight, blocks, sems = refs[each + 6 :]
    gather_heads(heads_same, heads_other, turned)
    attention_ref[...] = turned[...].T
    place, shard = place_in_group(), lax.axis_index("fsdp")
    half, columns = pieces[0].shape
    beside = (place & 1) ^ 1
    copies = []
    for at, flip in enumerate((0, 1, 2)):
        if flip == 0:
            block = own_ref[...]
        else:
            mine = beside == flip - 1
            for other in range(2):
                here = pl.ds(pl.multiple_of((parity_of(place) ^ other) * half, 32), half)
                weight[flip - 1, here, :] = jnp.where(mine, pieces[other][...], pieces[2 + other][...])
            block = weight[flip - 1]
        blocks[at] = jnp.dot(attention_ref[...], block, preferred_element_type=jnp.float32).astype(blocks.dtype)
        here = pl.ds(pl.multiple_of((shard ^ flip) * columns, 128), columns)
        copies.append(pltpu.make_async_copy(blocks.at[at], out_ref.at[0, :, here], sems.at[at]))
        copies[-1].start()
    for copy in copies:
        copy.wait()


def project_third_kernel(so_far_ref, attention_ref, *refs):
    pieces, (out_ref, weight, block, sem) = refs[:4], refs[4:]
    place, shard = place_in_group(), lax.axis_index("fsdp")
    part, columns = pieces[0].shape
    half = weight.shape[0] // 2
    for other in range(2):
        for flip in range(2):
            first = (parity_of(place) ^ flip) * half + ((place & 1) ^ other) * (half - part)
            weight[pl.ds(pl.multiple_of(first, 16), part), :] = pieces[2 * other + flip][...]
    block[...] = jnp.dot(attention_ref[...], weight[...], preferred_element_type=jnp.float32).astype(block.dtype)
    here = pl.ds(pl.multiple_of((shard ^ 3) * columns, 128), columns)
    copy = pltpu.make_async_copy(block, out_ref.at[0, :, here], sem)
    copy.start()
    copy.wait()


def projection_cost(frames, features, columns):
    return pl.CostEstimate(
        flops=2 * features * frames * columns, bytes_accessed=2 * features * columns, transcendentals=0
    )


def project(heads_same, heads_other, halves):
    _, rows, frames = heads_other.shape
    features, width = HEADS * rows, halves[0].shape[1]
    return pl.pallas_call(
        project_kernel,
        out_shape=jax.ShapeDtypeStruct((1, frames, width), jnp.bfloat16),
        in_specs=[WHOLE] * (len(FLIPS) + 3),
        out_specs=WHOLE,
        scratch_shapes=[pltpu.VMEM((features, frames), jnp.bfloat16), pltpu.VMEM((features, width), jnp.bfloat16)],
        compiler_params=params(24),
        cost_estimate=projection_cost(frames, features, width),
        name="project_heads",
    )(*heads_same, heads_other, *halves)


def project_near(heads_same, heads_other, own, pieces):
    _, rows, frames = heads_other.shape
    features, columns = own.shape
    return pl.pallas_call(
        project_near_kernel,
        out_shape=[jax.ShapeDtypeStruct((1, frames, 4 * columns), jnp.bfloat16), pltpu.VMEM((frames, features), jnp.bfloat16)],
        in_specs=[WHOLE] * (len(FLIPS) + 6),
        out_specs=[IN_HBM, WHOLE],
        scratch_shapes=[
            pltpu.VMEM((features, frames), jnp.bfloat16),
            pltpu.VMEM((2, features, columns), jnp.bfloat16),
            pltpu.VMEM((3, frames, columns), jnp.bfloat16),
            pltpu.SemaphoreType.DMA((3,)),
        ],
        compiler_params=params(24),
        cost_estimate=projection_cost(frames, features, 3 * columns),
        name="project_near_shards",
    )(*heads_same, heads_other, own, *pieces)


def project_third(so_far, attention, pieces):
    frames, features = attention.shape
    columns = pieces[0].shape[1]
    return pl.pallas_call(
        project_third_kernel,
        out_shape=jax.ShapeDtypeStruct(so_far.shape, so_far.dtype),
        in_specs=[IN_HBM] + [WHOLE] * 5,
        out_specs=IN_HBM,
        input_output_aliases={0: 0},
        scratch_shapes=[
            pltpu.VMEM((features, columns), jnp.bfloat16),
            pltpu.VMEM((frames, columns), jnp.bfloat16),
            pltpu.SemaphoreType.DMA,
        ],
        compiler_params=params(24),
        cost_estimate=projection_cost(frames, features, columns),
        name="project_third_shard",
    )(so_far, attention, *pieces)


def per_device(ctx, fsdp, queries, key_rows, value_rows, lengths, out_weight):
    def exchange(array, axis, flip):
        size = ctx if axis == "ctx" else fsdp
        return lax.ppermute(array, axis, [(i, i ^ flip) for i in range(size)])

    def exchange_chips(arrays):
        return [exchange(array, "ctx", flip) for flip, array in zip(FLIPS[1:], arrays)]

    def exchange_in_plane(array):
        return lax.ppermute(array, "ctx", [(i, i ^ (4 if i % 2 else 2)) for i in range(ctx)])

    def exchange_along(array, *flips):
        pairs = [(i * fsdp + z, i * fsdp + (z ^ flips[i % 2])) for i in range(ctx) for z in range(fsdp)]
        return lax.ppermute(array, ("ctx", "fsdp"), pairs)

    place = place_in_group()
    core = place & 1
    rows = out_weight.shape[0] // 2
    split_columns = fsdp == 4
    lengths = jnp.broadcast_to(lengths, (8, 128))
    if split_columns:
        half = lax.dynamic_slice_in_dim(out_weight, parity_of(place) * rows, rows, 0)
        fetched = exchange_along(half, 2, 1)
    else:
        half = lax.dynamic_slice_in_dim(out_weight, core * rows, rows, 0)
        half = lax.all_gather(half, "fsdp", axis=1, tiled=True)

    own_same, own_other, *by_chip = pack(queries, key_rows, value_rows)
    same = exchange_chips(by_chip)
    own_other = exchange(own_other, "ctx", 1)
    if split_columns:
        fetched, own_other, lengths = lax.optimization_barrier((fetched, own_other, lengths))
        passed = exchange_in_plane(fetched)
        part = rows // 2 + 16
        third = lax.dynamic_slice_in_dim(fetched, core * (rows - part), part, 0)
        third = exchange_along(third, 1, 2)
        third_passed = exchange_in_plane(third)
    same, own_other = lax.optimization_barrier((same, own_other))
    other = [own_other, *(exchange(array, "ctx", 1) for array in same)]

    groups = ctx // HEADS
    rest = None
    if groups > 1:
        pairs = [own_same[1:], own_other[1:]]
        for one, two in zip(same, other[1:]):
            pairs += [one[0, 1:], two[1, 1:]]
        across = [[head + first for first in range(0, ctx, HEADS)] for head in range(HEADS)]
        rest = lax.all_gather(jnp.stack(pairs), "ctx", axis=0, axis_index_groups=across, tiled=True)
    mixed = attend(lengths, [own_same, *same], other, rest, groups)

    heads = exchange_chips(mixed[1:])
    if split_columns:
        heads, *arrived = lax.optimization_barrier((heads, fetched, passed, third))
        fetched, passed, third = arrived
        fetched_other, passed_other, third_other = (exchange(array, "ctx", 1) for array in arrived)
    heads_same = [mixed[0], *heads]
    heads_other = exchange(second_entries(heads_same), "ctx", 1)
    if not split_columns:
        return project(heads_same, heads_other, [half, exchange(half, "ctx", 1)])
    third_passed, heads_other = lax.optimization_barrier((third_passed, heads_other))
    third_passed_other = exchange(third_passed, "ctx", 1)
    near = [fetched, passed, fetched_other, passed_other]
    so_far, attention = project_near(heads_same, heads_other, out_weight, near)
    return project_third(so_far, attention, [third, third_passed, third_other, third_passed_other])


def solution(mesh):
    return jax.shard_map(
        functools.partial(per_device, mesh.shape["ctx"], mesh.shape["fsdp"]),
        mesh=mesh,
        in_specs=(
            P("fsdp", "ctx", None),
            P("fsdp", "ctx", None),
            P("fsdp", "ctx", None),
            P("fsdp"),
            P(None, "fsdp"),
        ),
        out_specs=P("fsdp", "ctx", None),
        check_vma=False,
    )
```

```python
import functools
import math

import jax
import jax.numpy as jnp
from jax import lax
from jax.experimental import pallas as pl
from jax.experimental.pallas import tpu as pltpu
from jax.sharding import PartitionSpec as P

HEADS = 8
FLIPS = tuple(range(0, HEADS, 2))
WHOLE = pl.BlockSpec(memory_space=pltpu.VMEM)
IN_HBM = pl.BlockSpec(memory_space=pltpu.HBM)


def params(mebibytes=48):
    return pltpu.CompilerParams(vmem_limit_bytes=mebibytes * 1024 * 1024)


def place_in_group():
    return lax.axis_index("ctx") % HEADS


def parity_of(place):
    return ((place >> 2) ^ (place >> 1)) & 1


def copy_in_kernel(by_parity, query_ref, key_ref, value_ref, weight_ref, rows_ref, half_ref, sems):
    place = place_in_group()
    first = (parity_of(place) if by_parity else place & 1) * half_ref.shape[0]
    copies = [pltpu.make_async_copy(weight_ref.at[pl.ds(pl.multiple_of(first, 32), half_ref.shape[0])], half_ref, sems.at[3])]
    for part, ref in enumerate((query_ref, key_ref, value_ref)):
        copies.append(pltpu.make_async_copy(ref.at[0], rows_ref.at[part], sems.at[part]))
    for copy in copies:
        copy.start()
    for copy in copies:
        copy.wait()


def copy_in(queries, key_rows, value_rows, out_weight, by_parity):
    _, frames, features = queries.shape
    half = (out_weight.shape[0] // 2, out_weight.shape[1])
    arrays = [pltpu.with_memory_space_constraint(array, pltpu.HBM) for array in (queries, key_rows, value_rows, out_weight)]
    return pl.pallas_call(
        functools.partial(copy_in_kernel, by_parity),
        out_shape=[pltpu.VMEM((3, frames, features), queries.dtype), pltpu.VMEM(half, out_weight.dtype)],
        in_specs=[IN_HBM] * 4,
        out_specs=[WHOLE] * 2,
        scratch_shapes=[pltpu.SemaphoreType.DMA((4,))],
        compiler_params=params(16),
        name="copy_in",
    )(*arrays)


def turn_kernel(rows_ref, *refs):
    outs, turned = refs[:-1], refs[-1]
    features = outs[0].shape[1]
    chip = place_in_group() >> 1
    for part in range(3):
        turned[part] = rows_ref[part].T
        for flip, out_ref in zip(FLIPS, outs):
            first = pl.multiple_of((chip ^ (flip >> 1)) * features, 32)
            out_ref[part] = turned[part, pl.ds(first, features), :]


def turn(rows):
    _, frames, features = rows.shape
    return pl.pallas_call(
        turn_kernel,
        out_shape=[pltpu.VMEM((3, features // len(FLIPS), frames), rows.dtype)] * len(FLIPS),
        in_specs=[WHOLE],
        out_specs=[WHOLE] * len(FLIPS),
        scratch_shapes=[pltpu.VMEM((3, features, frames), rows.dtype)],
        compiler_params=params(16),
        name="turn_heads",
    )(rows)


def attention_kernel(groups, lengths_ref, *refs):
    each = len(FLIPS)
    same, other = refs[:each], refs[each : 2 * each]
    rest_ref = refs[2 * each] if groups > 1 else None
    outs, (keys, values) = refs[-2 - each : -2], refs[-2:]
    block = outs[0].shape[1]
    head_size = outs[0].shape[0] // 2
    place = place_in_group()
    scale = jnp.float32(math.log2(math.e) / math.sqrt(head_size))
    pad = keys.shape[2] - head_size

    def piece(at, head, part):
        rows = slice(head * head_size, (head + 1) * head_size)
        if groups > 1:
            return rest_ref[at, part - 1, rows, :]
        return other[at // 2][part - 1, rows, :] if at % 2 else same[at // 2][part, rows, :]

    ones = jnp.where(lax.broadcasted_iota(jnp.int32, (pad, block), 0) == 0, 1.0, 0.0).astype(keys.dtype)
    at_frame = lax.broadcasted_iota(jnp.int32, (block, pad), 0)
    at_feature = lax.broadcasted_iota(jnp.int32, (block, pad), 1)
    for at in range(groups * HEADS):
        here = slice(at * block, (at + 1) * block)
        frame = (at // HEADS * HEADS + (place ^ (at % HEADS))) * block + at_frame
        bias = jnp.where((at_feature == 0) & (frame >= lengths_ref[:1, :pad]), -1e30, 0.0).astype(keys.dtype)
        for head in range(2):
            keys[head, here, :head_size] = piece(at, head, 1).T
            keys[head, here, head_size:] = bias
            values[head, :head_size, here] = piece(at, head, 2)
            values[head, head_size:, here] = ones

    def score(head, flips):
        rows = slice(head * head_size, (head + 1) * head_size)
        query = [jnp.concatenate([same[flip // 2][0, rows, :], ones], axis=0) for flip in flips]
        return jnp.dot(keys[head], jnp.concatenate(query, axis=1), preferred_element_type=jnp.float32)

    chunks = [(head, flips) for head in range(2) for flips in (FLIPS[:2], FLIPS[2:])]
    later = score(*chunks[0])
    for at, (head, flips) in enumerate(chunks):
        scores = later
        if at + 1 < len(chunks):
            later = score(*chunks[at + 1])
        row_max = jnp.max(scores, axis=0, keepdims=True) * scale
        probs = jnp.exp2(scores * scale - row_max).astype(jnp.bfloat16)
        mixed = jnp.dot(values[head], probs, preferred_element_type=jnp.float32)
        mixed = (mixed[:head_size] / mixed[head_size : head_size + 1]).astype(jnp.bfloat16)
        for half, flip in enumerate(flips):
            outs[flip // 2][head * head_size : (head + 1) * head_size, :] = mixed[:, half * block : (half + 1) * block]


def attend(lengths, same, other, rest, groups):
    _, features, block = same[0].shape
    keys = groups * HEADS * block
    padded = features // 2 + 32
    rest = [] if rest is None else [rest]
    return pl.pallas_call(
        functools.partial(attention_kernel, groups),
        out_shape=[pltpu.VMEM((features, block), jnp.bfloat16)] * len(FLIPS),
        in_specs=[WHOLE] * (1 + 2 * len(FLIPS) + len(rest)),
        out_specs=[WHOLE] * len(FLIPS),
        scratch_shapes=[pltpu.VMEM((2, keys, padded), jnp.bfloat16), pltpu.VMEM((2, padded, keys), jnp.bfloat16)],
        compiler_params=params(32),
        cost_estimate=pl.CostEstimate(flops=8 * keys * keys * features, bytes_accessed=0, transcendentals=0),
        name="attend_two_heads",
    )(lengths, *same, *other, *rest)


def gather_heads(heads, turned):
    rows = heads[0].shape[0]
    for flip, ref in zip(FLIPS, heads):
        first = pl.multiple_of(((place_in_group() ^ flip) >> 1) * rows, 32)
        turned[pl.ds(first, rows), :] = ref[...]


def project_kernel(*refs):
    each = len(FLIPS)
    heads, halves, (out_ref, turned, weight) = refs[:each], refs[each : each + 2], refs[each + 2 :]
    gather_heads(heads, turned)
    half = weight.shape[0] // 2
    for other, ref in enumerate(halves):
        weight[pl.ds(pl.multiple_of(((place_in_group() & 1) ^ other) * half, 32), half), :] = ref[...]
    out_ref[0] = jnp.dot(turned[...].T, weight[...], preferred_element_type=jnp.float32).astype(out_ref.dtype)


def project_near_kernel(*refs):
    each = len(FLIPS)
    heads, own_ref, pieces = refs[:each], refs[each], refs[each + 1 : each + 5]
    out_ref, attention_ref, turned, weight, blocks, sems = refs[each + 5 :]
    gather_heads(heads, turned)
    attention_ref[...] = turned[...].T
    place, shard = place_in_group(), lax.axis_index("fsdp")
    half, columns = pieces[0].shape
    beside = (place & 1) ^ 1
    copies = []
    for at, flip in enumerate((0, 1, 2)):
        if flip == 0:
            block = own_ref[...]
        else:
            mine = beside == flip - 1
            for other in range(2):
                here = pl.ds(pl.multiple_of((parity_of(place) ^ other) * half, 32), half)
                weight[flip - 1, here, :] = jnp.where(mine, pieces[other][...], pieces[2 + other][...])
            block = weight[flip - 1]
        blocks[at] = jnp.dot(attention_ref[...], block, preferred_element_type=jnp.float32).astype(blocks.dtype)
        here = pl.ds(pl.multiple_of((shard ^ flip) * columns, 128), columns)
        copies.append(pltpu.make_async_copy(blocks.at[at], out_ref.at[0, :, here], sems.at[at]))
        copies[-1].start()
    for copy in copies:
        copy.wait()


def project_third_kernel(so_far_ref, attention_ref, *refs):
    pieces, (out_ref, weight, block, sem) = refs[:4], refs[4:]
    place, shard = place_in_group(), lax.axis_index("fsdp")
    part, columns = pieces[0].shape
    half = weight.shape[0] // 2
    for other in range(2):
        for flip in range(2):
            first = (parity_of(place) ^ flip) * half + ((place & 1) ^ other) * (half - part)
            weight[pl.ds(pl.multiple_of(first, 16), part), :] = pieces[2 * other + flip][...]
    block[...] = jnp.dot(attention_ref[...], weight[...], preferred_element_type=jnp.float32).astype(block.dtype)
    here = pl.ds(pl.multiple_of((shard ^ 3) * columns, 128), columns)
    copy = pltpu.make_async_copy(block, out_ref.at[0, :, here], sem)
    copy.start()
    copy.wait()


def projection_cost(frames, features, columns):
    return pl.CostEstimate(
        flops=2 * features * frames * columns, bytes_accessed=2 * features * columns, transcendentals=0
    )


def project(heads, halves):
    rows, frames = heads[0].shape
    features, width = len(FLIPS) * rows, halves[0].shape[1]
    return pl.pallas_call(
        project_kernel,
        out_shape=jax.ShapeDtypeStruct((1, frames, width), jnp.bfloat16),
        in_specs=[WHOLE] * (len(FLIPS) + 2),
        out_specs=WHOLE,
        scratch_shapes=[pltpu.VMEM((features, frames), jnp.bfloat16), pltpu.VMEM((features, width), jnp.bfloat16)],
        compiler_params=params(24),
        cost_estimate=projection_cost(frames, features, width),
        name="project_heads",
    )(*heads, *halves)


def project_near(heads, own, pieces):
    frames = heads[0].shape[1]
    features, columns = own.shape
    return pl.pallas_call(
        project_near_kernel,
        out_shape=[jax.ShapeDtypeStruct((1, frames, 4 * columns), jnp.bfloat16), pltpu.VMEM((frames, features), jnp.bfloat16)],
        in_specs=[WHOLE] * (len(FLIPS) + 5),
        out_specs=[IN_HBM, WHOLE],
        scratch_shapes=[
            pltpu.VMEM((features, frames), jnp.bfloat16),
            pltpu.VMEM((2, features, columns), jnp.bfloat16),
            pltpu.VMEM((3, frames, columns), jnp.bfloat16),
            pltpu.SemaphoreType.DMA((3,)),
        ],
        compiler_params=params(24),
        cost_estimate=projection_cost(frames, features, 3 * columns),
        name="project_near_shards",
    )(*heads, own, *pieces)


def project_third(so_far, attention, pieces):
    frames, features = attention.shape
    columns = pieces[0].shape[1]
    return pl.pallas_call(
        project_third_kernel,
        out_shape=jax.ShapeDtypeStruct(so_far.shape, so_far.dtype),
        in_specs=[IN_HBM] + [WHOLE] * 5,
        out_specs=IN_HBM,
        input_output_aliases={0: 0},
        scratch_shapes=[
            pltpu.VMEM((features, columns), jnp.bfloat16),
            pltpu.VMEM((frames, columns), jnp.bfloat16),
            pltpu.SemaphoreType.DMA,
        ],
        compiler_params=params(24),
        cost_estimate=projection_cost(frames, features, columns),
        name="project_third_shard",
    )(so_far, attention, *pieces)


def per_device(ctx, fsdp, queries, key_rows, value_rows, lengths, out_weight):
    def exchange(array, axis, flip):
        size = ctx if axis == "ctx" else fsdp
        return lax.ppermute(array, axis, [(i, i ^ flip) for i in range(size)])

    def exchange_chips(arrays):
        return [exchange(array, "ctx", flip) for flip, array in zip(FLIPS[1:], arrays)]

    def exchange_in_plane(array):
        return lax.ppermute(array, "ctx", [(i, i ^ (4 if i % 2 else 2)) for i in range(ctx)])

    def exchange_along(array, *flips):
        pairs = [(i * fsdp + z, i * fsdp + (z ^ flips[i % 2])) for i in range(ctx) for z in range(fsdp)]
        return lax.ppermute(array, ("ctx", "fsdp"), pairs)

    core = place_in_group() & 1
    split_columns = fsdp == 4
    lengths = jnp.broadcast_to(lengths, (8, 128))
    rows, half = copy_in(queries, key_rows, value_rows, out_weight, split_columns)
    if split_columns:
        fetched = exchange_along(half, 2, 1)
    else:
        half = lax.all_gather(half, "fsdp", axis=1, tiled=True)

    own, *by_chip = turn(rows)
    same = exchange_chips(by_chip)
    own_other = exchange(own[1:], "ctx", 1)
    if split_columns:
        fetched, own_other, lengths = lax.optimization_barrier((fetched, own_other, lengths))
        passed = exchange_in_plane(fetched)
        depth = half.shape[0]
        part = depth // 2 + 16
        third = lax.dynamic_slice_in_dim(fetched, core * (depth - part), part, 0)
        third = exchange_along(third, 1, 2)
    same, own_other = lax.optimization_barrier((same, own_other))
    other = [own_other, *(exchange(array[1:], "ctx", 1) for array in same)]
    same = [own, *same]

    groups = ctx // HEADS
    rest = None
    if groups > 1:
        pairs = [array for one, two in zip(same, other) for array in (one[1:], two)]
        across = [[head + first for first in range(0, ctx, HEADS)] for head in range(HEADS)]
        rest = lax.all_gather(jnp.stack(pairs), "ctx", axis=0, axis_index_groups=across, tiled=True)
    mixed = attend(lengths, same, other, rest, groups)

    heads = [mixed[0], *exchange_chips(mixed[1:])]
    if not split_columns:
        return project(heads, [half, exchange(half, "ctx", 1)])
    third_passed = exchange_in_plane(third)
    heads, fetched, passed, third = lax.optimization_barrier((heads, fetched, passed, third))
    fetched_other, passed_other, third_other, third_passed_other = (
        exchange(array, "ctx", 1) for array in (fetched, passed, third, third_passed)
    )
    so_far, attention = project_near(heads, out_weight, [fetched, passed, fetched_other, passed_other])
    return project_third(so_far, attention, [third, third_passed, third_other, third_passed_other])


def solution(mesh):
    return jax.shard_map(
        functools.partial(per_device, mesh.shape["ctx"], mesh.shape["fsdp"]),
        mesh=mesh,
        in_specs=(
            P("fsdp", "ctx", None),
            P("fsdp", "ctx", None),
            P("fsdp", "ctx", None),
            P("fsdp"),
            P(None, "fsdp"),
        ),
        out_specs=P("fsdp", "ctx", None),
        check_vma=False,
    )
```

```python
import functools
import math

import jax
import jax.numpy as jnp
from jax import lax
from jax.experimental import pallas as pl
from jax.experimental.pallas import tpu as pltpu
from jax.sharding import PartitionSpec as P

HEADS = 8
FLIPS = tuple(range(0, HEADS, 2))
WHOLE = pl.BlockSpec(memory_space=pltpu.VMEM)
IN_HBM = pl.BlockSpec(memory_space=pltpu.HBM)


def params(mebibytes=48):
    return pltpu.CompilerParams(vmem_limit_bytes=mebibytes * 1024 * 1024)


def place_in_group():
    return lax.axis_index("ctx") % HEADS


def parity_of(place):
    return ((place >> 2) ^ (place >> 1)) & 1


def copy_in_kernel(by_parity, query_ref, key_ref, value_ref, weight_ref, rows_ref, half_ref, sems):
    place = place_in_group()
    first = (parity_of(place) if by_parity else place & 1) * half_ref.shape[0]
    copies = [pltpu.make_async_copy(weight_ref.at[pl.ds(pl.multiple_of(first, 32), half_ref.shape[0])], half_ref, sems.at[3])]
    for part, ref in enumerate((query_ref, key_ref, value_ref)):
        copies.append(pltpu.make_async_copy(ref.at[0], rows_ref.at[part], sems.at[part]))
    for copy in copies:
        copy.start()
    for copy in copies:
        copy.wait()


def copy_in(queries, key_rows, value_rows, out_weight, by_parity):
    _, frames, features = queries.shape
    half = (out_weight.shape[0] // 2, out_weight.shape[1])
    arrays = [pltpu.with_memory_space_constraint(array, pltpu.HBM) for array in (queries, key_rows, value_rows, out_weight)]
    return pl.pallas_call(
        functools.partial(copy_in_kernel, by_parity),
        out_shape=[pltpu.VMEM((3, frames, features), queries.dtype), pltpu.VMEM(half, out_weight.dtype)],
        in_specs=[IN_HBM] * 4,
        out_specs=[WHOLE] * 2,
        scratch_shapes=[pltpu.SemaphoreType.DMA((4,))],
        compiler_params=params(16),
        name="copy_in",
    )(*arrays)


def turn_kernel(rows_ref, *refs):
    outs, turned = refs[:-1], refs[-1]
    features = outs[0].shape[1]
    chip = place_in_group() >> 1
    for part in range(3):
        turned[part] = rows_ref[part].T
        for flip, out_ref in zip(FLIPS, outs):
            first = pl.multiple_of((chip ^ (flip >> 1)) * features, 32)
            out_ref[part] = turned[part, pl.ds(first, features), :]


def turn(rows):
    _, frames, features = rows.shape
    return pl.pallas_call(
        turn_kernel,
        out_shape=[pltpu.VMEM((3, features // len(FLIPS), frames), rows.dtype)] * len(FLIPS),
        in_specs=[WHOLE],
        out_specs=[WHOLE] * len(FLIPS),
        scratch_shapes=[pltpu.VMEM((3, features, frames), rows.dtype)],
        compiler_params=params(16),
        name="turn_heads",
    )(rows)


def attention_kernel(groups, lengths_ref, *refs):
    each = len(FLIPS)
    same, other = refs[:each], refs[each : 2 * each]
    rest_ref = refs[2 * each] if groups > 1 else None
    outs, (keys, values) = refs[-2 - each : -2], refs[-2:]
    block = outs[0].shape[1]
    head_size = outs[0].shape[0] // 2
    place = place_in_group()
    scale = jnp.float32(math.log2(math.e) / math.sqrt(head_size))
    pad = keys.shape[2] - head_size

    def piece(at, head, part):
        rows = slice(head * head_size, (head + 1) * head_size)
        if groups > 1:
            return rest_ref[at, part - 1, rows, :]
        return other[at // 2][part - 1, rows, :] if at % 2 else same[at // 2][part, rows, :]

    ones = jnp.where(lax.broadcasted_iota(jnp.int32, (pad, block), 0) == 0, 1.0, 0.0).astype(keys.dtype)
    at_feature = lax.broadcasted_iota(jnp.int32, (pad, block), 0)
    at_frame = lax.broadcasted_iota(jnp.int32, (pad, block), 1)
    for at in range(groups * HEADS):
        here = slice(at * block, (at + 1) * block)
        frame = (at // HEADS * HEADS + (place ^ (at % HEADS))) * block + at_frame
        bias = jnp.where((at_feature == 0) & (frame >= lengths_ref[:1, :]), -1e30, 0.0).astype(keys.dtype)
        for head in range(2):
            keys[head, here, :] = jnp.concatenate([piece(at, head, 1), bias], axis=0).T
            values[head, :, here] = jnp.concatenate([piece(at, head, 2), ones], axis=0)

    def score(head, flips):
        rows = slice(head * head_size, (head + 1) * head_size)
        query = [jnp.concatenate([same[flip // 2][0, rows, :], ones], axis=0) for flip in flips]
        return jnp.dot(keys[head], jnp.concatenate(query, axis=1), preferred_element_type=jnp.float32)

    chunks = [(head, flips) for head in range(2) for flips in (FLIPS[:2], FLIPS[2:])]
    later = score(*chunks[0])
    for at, (head, flips) in enumerate(chunks):
        scores = later
        if at + 1 < len(chunks):
            later = score(*chunks[at + 1])
        row_max = jnp.max(scores, axis=0, keepdims=True) * scale
        probs = jnp.exp2(scores * scale - row_max).astype(jnp.bfloat16)
        mixed = jnp.dot(values[head], probs, preferred_element_type=jnp.float32)
        mixed = (mixed[:head_size] / mixed[head_size : head_size + 1]).astype(jnp.bfloat16)
        for half, flip in enumerate(flips):
            outs[flip // 2][head * head_size : (head + 1) * head_size, :] = mixed[:, half * block : (half + 1) * block]


def attend(lengths, same, other, rest, groups):
    _, features, block = same[0].shape
    keys = groups * HEADS * block
    padded = features // 2 + 32
    rest = [] if rest is None else [rest]
    return pl.pallas_call(
        functools.partial(attention_kernel, groups),
        out_shape=[pltpu.VMEM((features, block), jnp.bfloat16)] * len(FLIPS),
        in_specs=[WHOLE] * (1 + 2 * len(FLIPS) + len(rest)),
        out_specs=[WHOLE] * len(FLIPS),
        scratch_shapes=[pltpu.VMEM((2, keys, padded), jnp.bfloat16), pltpu.VMEM((2, padded, keys), jnp.bfloat16)],
        compiler_params=params(32),
        cost_estimate=pl.CostEstimate(flops=8 * keys * keys * features, bytes_accessed=0, transcendentals=0),
        name="attend_two_heads",
    )(lengths, *same, *other, *rest)


def gather_heads(heads, turned):
    rows = heads[0].shape[0]
    for flip, ref in zip(FLIPS, heads):
        first = pl.multiple_of(((place_in_group() ^ flip) >> 1) * rows, 32)
        turned[pl.ds(first, rows), :] = ref[...]


def project_kernel(*refs):
    each = len(FLIPS)
    heads, halves, (out_ref, turned, weight) = refs[:each], refs[each : each + 2], refs[each + 2 :]
    gather_heads(heads, turned)
    half = weight.shape[0] // 2
    for other, ref in enumerate(halves):
        weight[pl.ds(pl.multiple_of(((place_in_group() & 1) ^ other) * half, 32), half), :] = ref[...]
    out_ref[0] = jnp.dot(turned[...].T, weight[...], preferred_element_type=jnp.float32).astype(out_ref.dtype)


def project_near_kernel(*refs):
    each = len(FLIPS)
    heads, own_ref, pieces = refs[:each], refs[each], refs[each + 1 : each + 5]
    blocks_ref, attention_ref, turned, weight = refs[each + 5 :]
    gather_heads(heads, turned)
    attention = turned[...].T
    attention_ref[...] = attention
    place = place_in_group()
    half = pieces[0].shape[0]
    for flip in (1, 2):
        mine = (place & 1) == 2 - flip
        for other in range(2):
            here = pl.ds(pl.multiple_of((parity_of(place) ^ other) * half, 32), half)
            weight[flip - 1, here, :] = jnp.where(mine, pieces[other][...], pieces[2 + other][...])
    for flip, block in enumerate((own_ref[...], weight[0], weight[1])):
        blocks_ref[flip] = jnp.dot(attention, block, preferred_element_type=jnp.float32).astype(blocks_ref.dtype)


def project_third_kernel(blocks_ref, attention_ref, *refs):
    pieces, (out_ref, weight, last, sems) = refs[:4], refs[4:]
    place, shard = place_in_group(), lax.axis_index("fsdp")
    part, columns = pieces[0].shape
    half = weight.shape[0] // 2

    def copy_out(flip, block_ref):
        here = pl.ds(pl.multiple_of((shard ^ flip) * columns, 128), columns)
        copy = pltpu.make_async_copy(block_ref, out_ref.at[0, :, here], sems.at[flip])
        copy.start()
        return copy

    copies = [copy_out(flip, blocks_ref.at[flip]) for flip in range(3)]
    for other in range(2):
        for flip in range(2):
            first = (parity_of(place) ^ flip) * half + ((place & 1) ^ other) * (half - part)
            weight[pl.ds(pl.multiple_of(first, 16), part), :] = pieces[2 * other + flip][...]
    last[...] = jnp.dot(attention_ref[...], weight[...], preferred_element_type=jnp.float32).astype(last.dtype)
    copies.append(copy_out(3, last))
    for copy in copies:
        copy.wait()


def projection_cost(frames, features, columns):
    return pl.CostEstimate(
        flops=2 * features * frames * columns, bytes_accessed=2 * features * columns, transcendentals=0
    )


def project(heads, halves):
    rows, frames = heads[0].shape
    features, width = len(FLIPS) * rows, halves[0].shape[1]
    return pl.pallas_call(
        project_kernel,
        out_shape=jax.ShapeDtypeStruct((1, frames, width), jnp.bfloat16),
        in_specs=[WHOLE] * (len(FLIPS) + 2),
        out_specs=WHOLE,
        scratch_shapes=[pltpu.VMEM((features, frames), jnp.bfloat16), pltpu.VMEM((features, width), jnp.bfloat16)],
        compiler_params=params(24),
        cost_estimate=projection_cost(frames, features, width),
        name="project_heads",
    )(*heads, *halves)


def project_near(heads, own, pieces):
    frames = heads[0].shape[1]
    features, columns = own.shape
    return pl.pallas_call(
        project_near_kernel,
        out_shape=[pltpu.VMEM((3, frames, columns), jnp.bfloat16), pltpu.VMEM((frames, features), jnp.bfloat16)],
        in_specs=[WHOLE] * (len(FLIPS) + 5),
        out_specs=[WHOLE] * 2,
        scratch_shapes=[
            pltpu.VMEM((features, frames), jnp.bfloat16),
            pltpu.VMEM((2, features, columns), jnp.bfloat16),
        ],
        compiler_params=params(24),
        cost_estimate=projection_cost(frames, features, 3 * columns),
        name="project_near_shards",
    )(*heads, own, *pieces)


def project_third(blocks, attention, pieces):
    frames, features = attention.shape
    columns = pieces[0].shape[1]
    return pl.pallas_call(
        project_third_kernel,
        out_shape=jax.ShapeDtypeStruct((1, frames, 4 * columns), blocks.dtype),
        in_specs=[WHOLE] * 6,
        out_specs=IN_HBM,
        scratch_shapes=[
            pltpu.VMEM((features, columns), jnp.bfloat16),
            pltpu.VMEM((frames, columns), jnp.bfloat16),
            pltpu.SemaphoreType.DMA((4,)),
        ],
        compiler_params=params(24),
        cost_estimate=projection_cost(frames, features, columns),
        name="project_third_shard",
    )(blocks, attention, *pieces)


def per_device(ctx, fsdp, queries, key_rows, value_rows, lengths, out_weight):
    def exchange(array, axis, flip):
        size = ctx if axis == "ctx" else fsdp
        return lax.ppermute(array, axis, [(i, i ^ flip) for i in range(size)])

    def exchange_chips(arrays):
        return [exchange(array, "ctx", flip) for flip, array in zip(FLIPS[1:], arrays)]

    def exchange_in_plane(array):
        return lax.ppermute(array, "ctx", [(i, i ^ (4 if i % 2 else 2)) for i in range(ctx)])

    def exchange_along(array, *flips):
        pairs = [(i * fsdp + z, i * fsdp + (z ^ flips[i % 2])) for i in range(ctx) for z in range(fsdp)]
        return lax.ppermute(array, ("ctx", "fsdp"), pairs)

    core = place_in_group() & 1
    split_columns = fsdp == 4
    lengths = jnp.broadcast_to(lengths, (8, 128))
    rows, half = copy_in(queries, key_rows, value_rows, out_weight, split_columns)
    if split_columns:
        fetched = exchange_along(half, 2, 1)
    else:
        half = lax.all_gather(half, "fsdp", axis=1, tiled=True)

    own, *by_chip = turn(rows)
    same = exchange_chips(by_chip)
    own_other = exchange(own[1:], "ctx", 1)
    if split_columns:
        fetched, own_other, lengths = lax.optimization_barrier((fetched, own_other, lengths))
        passed = exchange_in_plane(fetched)
        depth = half.shape[0]
        part = depth // 2 + 16
        third = lax.dynamic_slice_in_dim(fetched, core * (depth - part), part, 0)
        third = exchange_along(third, 1, 2)
    same, own_other = lax.optimization_barrier((same, own_other))
    other = [own_other, *(exchange(array[1:], "ctx", 1) for array in same)]
    same = [own, *same]

    groups = ctx // HEADS
    rest = None
    if groups > 1:
        pairs = [array for one, two in zip(same, other) for array in (one[1:], two)]
        across = [[head + first for first in range(0, ctx, HEADS)] for head in range(HEADS)]
        rest = lax.all_gather(jnp.stack(pairs), "ctx", axis=0, axis_index_groups=across, tiled=True)
    mixed = attend(lengths, same, other, rest, groups)

    heads = [mixed[0], *exchange_chips(mixed[1:])]
    if not split_columns:
        return project(heads, [half, exchange(half, "ctx", 1)])
    third_passed = exchange_in_plane(third)
    heads, fetched, passed, third = lax.optimization_barrier((heads, fetched, passed, third))
    fetched_other, passed_other, third_other, third_passed_other = (
        exchange(array, "ctx", 1) for array in (fetched, passed, third, third_passed)
    )
    blocks, attention = project_near(heads, out_weight, [fetched, passed, fetched_other, passed_other])
    return project_third(blocks, attention, [third, third_passed, third_other, third_passed_other])


def solution(mesh):
    return jax.shard_map(
        functools.partial(per_device, mesh.shape["ctx"], mesh.shape["fsdp"]),
        mesh=mesh,
        in_specs=(
            P("fsdp", "ctx", None),
            P("fsdp", "ctx", None),
            P("fsdp", "ctx", None),
            P("fsdp"),
            P(None, "fsdp"),
        ),
        out_specs=P("fsdp", "ctx", None),
        check_vma=False,
    )
```

```python
import functools
import math

import jax
import jax.numpy as jnp
from jax import lax
from jax.experimental import pallas as pl
from jax.experimental.pallas import tpu as pltpu
from jax.sharding import PartitionSpec as P

HEADS = 8
FLIPS = tuple(range(0, HEADS, 2))
WHOLE = pl.BlockSpec(memory_space=pltpu.VMEM)
IN_HBM = pl.BlockSpec(memory_space=pltpu.HBM)


def params(mebibytes=48):
    return pltpu.CompilerParams(vmem_limit_bytes=mebibytes * 1024 * 1024)


def place_in_group():
    return lax.axis_index("ctx") % HEADS


def parity_of(place):
    return ((place >> 2) ^ (place >> 1)) & 1


def copy_in_kernel(by_parity, query_ref, key_ref, value_ref, weight_ref, rows_ref, half_ref, sems):
    place = place_in_group()
    first = (parity_of(place) if by_parity else place & 1) * half_ref.shape[0]
    copies = [pltpu.make_async_copy(weight_ref.at[pl.ds(pl.multiple_of(first, 32), half_ref.shape[0])], half_ref, sems.at[3])]
    for part, ref in enumerate((query_ref, key_ref, value_ref)):
        copies.append(pltpu.make_async_copy(ref.at[0], rows_ref.at[part], sems.at[part]))
    for copy in copies:
        copy.start()
    for copy in copies:
        copy.wait()


def copy_in(queries, key_rows, value_rows, out_weight, by_parity):
    _, frames, features = queries.shape
    half = (out_weight.shape[0] // 2, out_weight.shape[1])
    arrays = [pltpu.with_memory_space_constraint(array, pltpu.HBM) for array in (queries, key_rows, value_rows, out_weight)]
    return pl.pallas_call(
        functools.partial(copy_in_kernel, by_parity),
        out_shape=[pltpu.VMEM((3, frames, features), queries.dtype), pltpu.VMEM(half, out_weight.dtype)],
        in_specs=[IN_HBM] * 4,
        out_specs=[WHOLE] * 2,
        scratch_shapes=[pltpu.SemaphoreType.DMA((4,))],
        compiler_params=params(16),
        name="copy_in",
    )(*arrays)


def turn_kernel(rows_ref, *refs):
    outs, turned = refs[:-1], refs[-1]
    features = outs[0].shape[1]
    chip = place_in_group() >> 1
    for part in range(3):
        turned[part] = rows_ref[part].T
        for flip, out_ref in zip(FLIPS, outs):
            first = pl.multiple_of((chip ^ (flip >> 1)) * features, 32)
            out_ref[part] = turned[part, pl.ds(first, features), :]


def turn(rows):
    _, frames, features = rows.shape
    return pl.pallas_call(
        turn_kernel,
        out_shape=[pltpu.VMEM((3, features // len(FLIPS), frames), rows.dtype)] * len(FLIPS),
        in_specs=[WHOLE],
        out_specs=[WHOLE] * len(FLIPS),
        scratch_shapes=[pltpu.VMEM((3, features, frames), rows.dtype)],
        compiler_params=params(16),
        name="turn_heads",
    )(rows)


def attention_kernel(groups, lengths_ref, *refs):
    each = len(FLIPS)
    same, own_other, other = refs[:each], refs[each], refs[each + 1]
    rest_ref = refs[each + 2] if groups > 1 else None
    outs, (keys, values) = refs[-2 - each : -2], refs[-2:]
    block = outs[0].shape[1]
    head_size = outs[0].shape[0] // 2
    place = place_in_group()
    scale = jnp.float32(math.log2(math.e) / math.sqrt(head_size))
    pad = keys.shape[2] - head_size

    def piece(at, head, part):
        rows = slice(head * head_size, (head + 1) * head_size)
        if groups > 1:
            return rest_ref[at, part - 1, rows, :]
        if at % 2 == 0:
            return same[at // 2][part, rows, :]
        return other[at // 2 - 1, part - 1, rows, :] if at > 1 else own_other[part - 1, rows, :]

    ones = jnp.where(lax.broadcasted_iota(jnp.int32, (pad, block), 0) == 0, 1.0, 0.0).astype(keys.dtype)
    at_feature = lax.broadcasted_iota(jnp.int32, (pad, block), 0)
    at_frame = lax.broadcasted_iota(jnp.int32, (pad, block), 1)
    for at in range(groups * HEADS):
        here = slice(at * block, (at + 1) * block)
        frame = (at // HEADS * HEADS + (place ^ (at % HEADS))) * block + at_frame
        bias = jnp.where((at_feature == 0) & (frame >= lengths_ref[:1, :]), -1e30, 0.0).astype(keys.dtype)
        for head in range(2):
            keys[head, here, :] = jnp.concatenate([piece(at, head, 1), bias], axis=0).T
            values[head, :, here] = jnp.concatenate([piece(at, head, 2), ones], axis=0)

    def score(head, flips):
        rows = slice(head * head_size, (head + 1) * head_size)
        query = [jnp.concatenate([same[flip // 2][0, rows, :], ones], axis=0) for flip in flips]
        return jnp.dot(keys[head], jnp.concatenate(query, axis=1), preferred_element_type=jnp.float32)

    chunks = [(head, flips) for head in range(2) for flips in (FLIPS[:2], FLIPS[2:])]
    later = score(*chunks[0])
    for at, (head, flips) in enumerate(chunks):
        scores = later
        if at + 1 < len(chunks):
            later = score(*chunks[at + 1])
        row_max = jnp.max(scores, axis=0, keepdims=True) * scale
        probs = jnp.exp2(scores * scale - row_max).astype(jnp.bfloat16)
        mixed = jnp.dot(values[head], probs, preferred_element_type=jnp.float32)
        mixed = (mixed[:head_size] / mixed[head_size : head_size + 1]).astype(jnp.bfloat16)
        for half, flip in enumerate(flips):
            outs[flip // 2][head * head_size : (head + 1) * head_size, :] = mixed[:, half * block : (half + 1) * block]


def stack_kernel(*refs):
    for at, ref in enumerate(refs[:-1]):
        refs[-1][at] = ref[1:]


def stack_keys_and_values(arrays):
    parts, features, frames = arrays[0].shape
    return pl.pallas_call(
        stack_kernel,
        out_shape=pltpu.VMEM((len(arrays), parts - 1, features, frames), arrays[0].dtype),
        in_specs=[WHOLE] * len(arrays),
        out_specs=WHOLE,
        compiler_params=params(16),
        name="stack_keys_and_values",
    )(*arrays)


def attend(lengths, same, own_other, other, rest, groups):
    _, features, block = same[0].shape
    keys = groups * HEADS * block
    padded = features // 2 + 32
    rest = [] if rest is None else [rest]
    return pl.pallas_call(
        functools.partial(attention_kernel, groups),
        out_shape=[pltpu.VMEM((features, block), jnp.bfloat16)] * len(FLIPS),
        in_specs=[WHOLE] * (3 + len(FLIPS) + len(rest)),
        out_specs=[WHOLE] * len(FLIPS),
        scratch_shapes=[pltpu.VMEM((2, keys, padded), jnp.bfloat16), pltpu.VMEM((2, padded, keys), jnp.bfloat16)],
        compiler_params=params(32),
        cost_estimate=pl.CostEstimate(flops=2 * keys * keys * features, bytes_accessed=0, transcendentals=0),
        name="attend_two_heads",
    )(lengths, *same, own_other, other, *rest)


def gather_heads(heads, turned):
    rows = heads[0].shape[0]
    for flip, ref in zip(FLIPS, heads):
        first = pl.multiple_of(((place_in_group() ^ flip) >> 1) * rows, 32)
        turned[pl.ds(first, rows), :] = ref[...]


def project_kernel(*refs):
    each = len(FLIPS)
    heads, halves, (out_ref, turned, weight) = refs[:each], refs[each : each + 2], refs[each + 2 :]
    gather_heads(heads, turned)
    half = weight.shape[0] // 2
    for other, ref in enumerate(halves):
        weight[pl.ds(pl.multiple_of(((place_in_group() & 1) ^ other) * half, 32), half), :] = ref[...]
    out_ref[0] = jnp.dot(turned[...].T, weight[...], preferred_element_type=jnp.float32).astype(out_ref.dtype)


def project_near_kernel(*refs):
    each = len(FLIPS)
    heads, own_ref, pieces = refs[:each], refs[each], refs[each + 1 : each + 5]
    blocks_ref, attention_ref, turned, weight = refs[each + 5 :]
    gather_heads(heads, turned)
    attention = turned[...].T
    attention_ref[...] = attention
    place = place_in_group()
    half = pieces[0].shape[0]
    for flip in (1, 2):
        mine = (place & 1) == 2 - flip
        for other in range(2):
            here = pl.ds(pl.multiple_of((parity_of(place) ^ other) * half, 32), half)
            weight[flip - 1, here, :] = jnp.where(mine, pieces[other][...], pieces[2 + other][...])
    for flip, block in enumerate((own_ref[...], weight[0], weight[1])):
        blocks_ref[flip] = jnp.dot(attention, block, preferred_element_type=jnp.float32).astype(blocks_ref.dtype)


def project_third_kernel(blocks_ref, attention_ref, *refs):
    pieces, (out_ref, weight, last, sems) = refs[:4], refs[4:]
    place, shard = place_in_group(), lax.axis_index("fsdp")
    part, columns = pieces[0].shape
    half = weight.shape[0] // 2

    def copy_out(flip, block_ref):
        here = pl.ds(pl.multiple_of((shard ^ flip) * columns, 128), columns)
        copy = pltpu.make_async_copy(block_ref, out_ref.at[0, :, here], sems.at[flip])
        copy.start()
        return copy

    copies = [copy_out(flip, blocks_ref.at[flip]) for flip in range(3)]
    for other in range(2):
        for flip in range(2):
            first = (parity_of(place) ^ flip) * half + ((place & 1) ^ other) * (half - part)
            weight[pl.ds(pl.multiple_of(first, 16), part), :] = pieces[2 * other + flip][...]
    last[...] = jnp.dot(attention_ref[...], weight[...], preferred_element_type=jnp.float32).astype(last.dtype)
    copies.append(copy_out(3, last))
    for copy in copies:
        copy.wait()


def projection_cost(frames, features, columns):
    return pl.CostEstimate(
        flops=2 * features * frames * columns, bytes_accessed=2 * features * columns, transcendentals=0
    )


def project(heads, halves):
    rows, frames = heads[0].shape
    features, width = len(FLIPS) * rows, halves[0].shape[1]
    return pl.pallas_call(
        project_kernel,
        out_shape=jax.ShapeDtypeStruct((1, frames, width), jnp.bfloat16),
        in_specs=[WHOLE] * (len(FLIPS) + 2),
        out_specs=WHOLE,
        scratch_shapes=[pltpu.VMEM((features, frames), jnp.bfloat16), pltpu.VMEM((features, width), jnp.bfloat16)],
        compiler_params=params(24),
        cost_estimate=projection_cost(frames, features, width),
        name="project_heads",
    )(*heads, *halves)


def project_near(heads, own, pieces):
    frames = heads[0].shape[1]
    features, columns = own.shape
    return pl.pallas_call(
        project_near_kernel,
        out_shape=[pltpu.VMEM((3, frames, columns), jnp.bfloat16), pltpu.VMEM((frames, features), jnp.bfloat16)],
        in_specs=[WHOLE] * (len(FLIPS) + 5),
        out_specs=[WHOLE] * 2,
        scratch_shapes=[
            pltpu.VMEM((features, frames), jnp.bfloat16),
            pltpu.VMEM((2, features, columns), jnp.bfloat16),
        ],
        compiler_params=params(24),
        cost_estimate=pl.CostEstimate(flops=0, bytes_accessed=0, transcendentals=0),
        name="project_near_shards",
    )(*heads, own, *pieces)


def project_third(blocks, attention, pieces):
    frames, features = attention.shape
    columns = pieces[0].shape[1]
    return pl.pallas_call(
        project_third_kernel,
        out_shape=jax.ShapeDtypeStruct((1, frames, 4 * columns), blocks.dtype),
        in_specs=[WHOLE] * 6,
        out_specs=IN_HBM,
        scratch_shapes=[
            pltpu.VMEM((features, columns), jnp.bfloat16),
            pltpu.VMEM((frames, columns), jnp.bfloat16),
            pltpu.SemaphoreType.DMA((4,)),
        ],
        compiler_params=params(24),
        cost_estimate=projection_cost(frames, features, columns),
        name="project_third_shard",
    )(blocks, attention, *pieces)


def per_device(ctx, fsdp, queries, key_rows, value_rows, lengths, out_weight):
    def exchange(array, axis, flip):
        size = ctx if axis == "ctx" else fsdp
        return lax.ppermute(array, axis, [(i, i ^ flip) for i in range(size)])

    def exchange_chips(arrays):
        return [exchange(array, "ctx", flip) for flip, array in zip(FLIPS[1:], arrays)]

    def exchange_in_plane(array):
        return lax.ppermute(array, "ctx", [(i, i ^ (4 if i % 2 else 2)) for i in range(ctx)])

    def exchange_along(array, *flips):
        pairs = [(i * fsdp + z, i * fsdp + (z ^ flips[i % 2])) for i in range(ctx) for z in range(fsdp)]
        return lax.ppermute(array, ("ctx", "fsdp"), pairs)

    core = place_in_group() & 1
    split_columns = fsdp == 4
    lengths = jnp.broadcast_to(lengths, (8, 128))
    rows, half = copy_in(queries, key_rows, value_rows, out_weight, split_columns)
    if split_columns:
        fetched = exchange_along(half, 2, 1)
    else:
        half = lax.all_gather(half, "fsdp", axis=1, tiled=True)

    own, *by_chip = turn(rows)
    same = exchange_chips(by_chip)
    own_other = exchange(own[1:], "ctx", 1)
    if split_columns:
        fetched, own_other, lengths = lax.optimization_barrier((fetched, own_other, lengths))
        passed = [exchange_in_plane(rows) for rows in (fetched[: half.shape[0] // 2], fetched[half.shape[0] // 2 :])]
        depth = half.shape[0]
        part = depth // 2 + 16
        third = lax.dynamic_slice_in_dim(fetched, core * (depth - part), part, 0)
        third = exchange_along(third, 1, 2)
    same, own_other = lax.optimization_barrier((same, own_other))
    other = exchange(stack_keys_and_values(same), "ctx", 1)
    same = [own, *same]

    groups = ctx // HEADS
    rest = None
    if groups > 1:
        pairs = [own[1:], own_other]
        for at, array in enumerate(same[1:]):
            pairs += [array[1:], other[at]]
        across = [[head + first for first in range(0, ctx, HEADS)] for head in range(HEADS)]
        rest = lax.all_gather(jnp.stack(pairs), "ctx", axis=0, axis_index_groups=across, tiled=True)
    mixed = attend(lengths, same, own_other, other, rest, groups)

    if split_columns:
        third, own_heads = lax.optimization_barrier((third, mixed[0]))
        mixed = [own_heads, *mixed[1:]]
    heads = [mixed[0], *exchange_chips(mixed[1:])]
    if not split_columns:
        return project(heads, [half, exchange(half, "ctx", 1)])
    third_passed = exchange_in_plane(third)
    heads[3], fetched, passed = lax.optimization_barrier((heads[3], fetched, jnp.concatenate(passed, axis=0)))
    heads[1], heads[2], third = lax.optimization_barrier((heads[1], heads[2], third))
    fetched_other, passed_other, third_other, third_passed_other = (
        exchange(array, "ctx", 1) for array in (fetched, passed, third, third_passed)
    )
    blocks, attention = project_near(heads, out_weight, [fetched, passed, fetched_other, passed_other])
    return project_third(blocks, attention, [third, third_passed, third_other, third_passed_other])


def solution(mesh):
    return jax.shard_map(
        functools.partial(per_device, mesh.shape["ctx"], mesh.shape["fsdp"]),
        mesh=mesh,
        in_specs=(
            P("fsdp", "ctx", None),
            P("fsdp", "ctx", None),
            P("fsdp", "ctx", None),
            P("fsdp"),
            P(None, "fsdp"),
        ),
        out_specs=P("fsdp", "ctx", None),
        check_vma=False,
    )
```

```python
import functools
import math

import jax
import jax.numpy as jnp
from jax import lax
from jax.experimental import pallas as pl
from jax.experimental.pallas import tpu as pltpu
from jax.sharding import PartitionSpec as P

HEADS = 8
FLIPS = tuple(range(0, HEADS, 2))
WHOLE = pl.BlockSpec(memory_space=pltpu.VMEM)
IN_HBM = pl.BlockSpec(memory_space=pltpu.HBM)


def params(mebibytes=48):
    return pltpu.CompilerParams(vmem_limit_bytes=mebibytes * 1024 * 1024)


def place_in_group():
    return lax.axis_index("ctx") % HEADS


def parity_of(place):
    return ((place >> 2) ^ (place >> 1)) & 1


def copy_in_kernel(by_parity, query_ref, key_ref, value_ref, weight_ref, rows_ref, half_ref, sems):
    place = place_in_group()
    first = (parity_of(place) if by_parity else place & 1) * half_ref.shape[0]
    copies = [pltpu.make_async_copy(weight_ref.at[pl.ds(pl.multiple_of(first, 32), half_ref.shape[0])], half_ref, sems.at[3])]
    for part, ref in enumerate((query_ref, key_ref, value_ref)):
        copies.append(pltpu.make_async_copy(ref.at[0], rows_ref.at[part], sems.at[part]))
    for copy in copies:
        copy.start()
    for copy in copies:
        copy.wait()


def copy_in(queries, key_rows, value_rows, out_weight, by_parity):
    _, frames, features = queries.shape
    half = (out_weight.shape[0] // 2, out_weight.shape[1])
    arrays = [pltpu.with_memory_space_constraint(array, pltpu.HBM) for array in (queries, key_rows, value_rows, out_weight)]
    return pl.pallas_call(
        functools.partial(copy_in_kernel, by_parity),
        out_shape=[pltpu.VMEM((3, frames, features), queries.dtype), pltpu.VMEM(half, out_weight.dtype)],
        in_specs=[IN_HBM] * 4,
        out_specs=[WHOLE] * 2,
        scratch_shapes=[pltpu.SemaphoreType.DMA((4,))],
        compiler_params=params(16),
        name="copy_in",
    )(*arrays)


def turn_kernel(rows_ref, *refs):
    outs, turned = refs[:-1], refs[-1]
    features = outs[0].shape[1]
    chip = place_in_group() >> 1
    for part in range(3):
        turned[part] = rows_ref[part].T
        for flip, out_ref in zip(FLIPS, outs):
            first = pl.multiple_of((chip ^ (flip >> 1)) * features, 32)
            out_ref[part] = turned[part, pl.ds(first, features), :]


def turn(rows):
    _, frames, features = rows.shape
    return pl.pallas_call(
        turn_kernel,
        out_shape=[pltpu.VMEM((3, features // len(FLIPS), frames), rows.dtype)] * len(FLIPS),
        in_specs=[WHOLE],
        out_specs=[WHOLE] * len(FLIPS),
        scratch_shapes=[pltpu.VMEM((3, features, frames), rows.dtype)],
        compiler_params=params(16),
        name="turn_heads",
    )(rows)


def attention_kernel(groups, lengths_ref, *refs):
    each = len(FLIPS)
    same, own_other, other = refs[:each], refs[each], refs[each + 1]
    rest_ref = refs[each + 2] if groups > 1 else None
    outs, (keys, values) = refs[-2 - each : -2], refs[-2:]
    block = outs[0].shape[1]
    head_size = outs[0].shape[0] // 2
    place = place_in_group()
    scale = jnp.float32(math.log2(math.e) / math.sqrt(head_size))
    pad = keys.shape[2] - head_size

    def piece(at, head, part):
        rows = slice(head * head_size, (head + 1) * head_size)
        if groups > 1:
            return rest_ref[at, part - 1, rows, :]
        if at % 2 == 0:
            return same[at // 2][part, rows, :]
        return other[at // 2 - 1, part - 1, rows, :] if at > 1 else own_other[part - 1, rows, :]

    ones = jnp.where(lax.broadcasted_iota(jnp.int32, (pad, block), 0) == 0, 1.0, 0.0).astype(keys.dtype)
    at_feature = lax.broadcasted_iota(jnp.int32, (pad, block), 0)
    at_frame = lax.broadcasted_iota(jnp.int32, (pad, block), 1)

    def prepare(head):
        for at in range(groups * HEADS):
            here = slice(at * block, (at + 1) * block)
            frame = (at // HEADS * HEADS + (place ^ (at % HEADS))) * block + at_frame
            bias = jnp.where((at_feature == 0) & (frame >= lengths_ref[:1, :]), -1e30, 0.0).astype(keys.dtype)
            keys[head, here, :] = jnp.concatenate([piece(at, head, 1), bias], axis=0).T
            values[head, :, here] = jnp.concatenate([piece(at, head, 2), ones], axis=0)

    def score(head, flips):
        rows = slice(head * head_size, (head + 1) * head_size)
        query = [jnp.concatenate([same[flip // 2][0, rows, :], ones], axis=0) for flip in flips]
        return jnp.dot(keys[head], jnp.concatenate(query, axis=1), preferred_element_type=jnp.float32)

    chunks = [(head, flips) for head in range(2) for flips in (FLIPS[:2], FLIPS[2:])]
    prepare(0)
    later = score(*chunks[0])
    prepare(1)
    for at, (head, flips) in enumerate(chunks):
        scores = later
        if at + 1 < len(chunks):
            later = score(*chunks[at + 1])
        row_max = jnp.max(scores, axis=0, keepdims=True) * scale
        probs = jnp.exp2(scores * scale - row_max).astype(jnp.bfloat16)
        mixed = jnp.dot(values[head], probs, preferred_element_type=jnp.float32)
        mixed = (mixed[:head_size] / mixed[head_size : head_size + 1]).astype(jnp.bfloat16)
        for half, flip in enumerate(flips):
            outs[flip // 2][head * head_size : (head + 1) * head_size, :] = mixed[:, half * block : (half + 1) * block]


def stack_kernel(*refs):
    for at, ref in enumerate(refs[:-1]):
        refs[-1][at] = ref[1:]


def stack_keys_and_values(arrays):
    parts, features, frames = arrays[0].shape
    return pl.pallas_call(
        stack_kernel,
        out_shape=pltpu.VMEM((len(arrays), parts - 1, features, frames), arrays[0].dtype),
        in_specs=[WHOLE] * len(arrays),
        out_specs=WHOLE,
        compiler_params=params(16),
        name="stack_keys_and_values",
    )(*arrays)


def attend(lengths, same, own_other, other, rest, groups):
    _, features, block = same[0].shape
    keys = groups * HEADS * block
    padded = features // 2 + 32
    rest = [] if rest is None else [rest]
    return pl.pallas_call(
        functools.partial(attention_kernel, groups),
        out_shape=[pltpu.VMEM((features, block), jnp.bfloat16)] * len(FLIPS),
        in_specs=[WHOLE] * (3 + len(FLIPS) + len(rest)),
        out_specs=[WHOLE] * len(FLIPS),
        scratch_shapes=[pltpu.VMEM((2, keys, padded), jnp.bfloat16), pltpu.VMEM((2, padded, keys), jnp.bfloat16)],
        compiler_params=params(32),
        cost_estimate=pl.CostEstimate(flops=8 * keys * keys * features, bytes_accessed=0, transcendentals=0),
        name="attend_two_heads",
    )(lengths, *same, own_other, other, *rest)


def gather_heads(heads, turned):
    rows = heads[0].shape[0]
    for flip, ref in zip(FLIPS, heads):
        first = pl.multiple_of(((place_in_group() ^ flip) >> 1) * rows, 32)
        turned[pl.ds(first, rows), :] = ref[...]


def project_kernel(*refs):
    each = len(FLIPS)
    heads, halves, (out_ref, turned, weight) = refs[:each], refs[each : each + 2], refs[each + 2 :]
    gather_heads(heads, turned)
    half = weight.shape[0] // 2
    for other, ref in enumerate(halves):
        weight[pl.ds(pl.multiple_of(((place_in_group() & 1) ^ other) * half, 32), half), :] = ref[...]
    out_ref[0] = jnp.dot(turned[...].T, weight[...], preferred_element_type=jnp.float32).astype(out_ref.dtype)


def project_near_kernel(*refs):
    each = len(FLIPS)
    heads, own_ref, pieces = refs[:each], refs[each], refs[each + 1 : each + 5]
    blocks_ref, attention_ref, turned, weight = refs[each + 5 :]
    gather_heads(heads, turned)
    attention = turned[...].T
    attention_ref[...] = attention
    place = place_in_group()
    half = pieces[0].shape[0]
    for flip in (1, 2):
        mine = (place & 1) == 2 - flip
        for other in range(2):
            here = pl.ds(pl.multiple_of((parity_of(place) ^ other) * half, 32), half)
            weight[flip - 1, here, :] = jnp.where(mine, pieces[other][...], pieces[2 + other][...])
    for flip, block in enumerate((own_ref[...], weight[0], weight[1])):
        blocks_ref[flip] = jnp.dot(attention, block, preferred_element_type=jnp.float32).astype(blocks_ref.dtype)


def project_third_kernel(blocks_ref, attention_ref, *refs):
    pieces, (out_ref, weight, last, sems) = refs[:4], refs[4:]
    place, shard = place_in_group(), lax.axis_index("fsdp")
    part, columns = pieces[0].shape
    half = weight.shape[0] // 2

    def copy_out(flip, block_ref):
        here = pl.ds(pl.multiple_of((shard ^ flip) * columns, 128), columns)
        copy = pltpu.make_async_copy(block_ref, out_ref.at[0, :, here], sems.at[flip])
        copy.start()
        return copy

    copies = [copy_out(flip, blocks_ref.at[flip]) for flip in range(3)]
    for other in range(2):
        for flip in range(2):
            first = (parity_of(place) ^ flip) * half + ((place & 1) ^ other) * (half - part)
            weight[pl.ds(pl.multiple_of(first, 16), part), :] = pieces[2 * other + flip][...]
    last[...] = jnp.dot(attention_ref[...], weight[...], preferred_element_type=jnp.float32).astype(last.dtype)
    copies.append(copy_out(3, last))
    for copy in copies:
        copy.wait()


def projection_cost(frames, features, columns):
    return pl.CostEstimate(
        flops=2 * features * frames * columns, bytes_accessed=2 * features * columns, transcendentals=0
    )


def project(heads, halves):
    rows, frames = heads[0].shape
    features, width = len(FLIPS) * rows, halves[0].shape[1]
    return pl.pallas_call(
        project_kernel,
        out_shape=jax.ShapeDtypeStruct((1, frames, width), jnp.bfloat16),
        in_specs=[WHOLE] * (len(FLIPS) + 2),
        out_specs=WHOLE,
        scratch_shapes=[pltpu.VMEM((features, frames), jnp.bfloat16), pltpu.VMEM((features, width), jnp.bfloat16)],
        compiler_params=params(24),
        cost_estimate=projection_cost(frames, features, width),
        name="project_heads",
    )(*heads, *halves)


def project_near(heads, own, pieces):
    frames = heads[0].shape[1]
    features, columns = own.shape
    return pl.pallas_call(
        project_near_kernel,
        out_shape=[pltpu.VMEM((3, frames, columns), jnp.bfloat16), pltpu.VMEM((frames, features), jnp.bfloat16)],
        in_specs=[WHOLE] * (len(FLIPS) + 5),
        out_specs=[WHOLE] * 2,
        scratch_shapes=[
            pltpu.VMEM((features, frames), jnp.bfloat16),
            pltpu.VMEM((2, features, columns), jnp.bfloat16),
        ],
        compiler_params=params(24),
        cost_estimate=projection_cost(frames, features, 3 * columns),
        name="project_near_shards",
    )(*heads, own, *pieces)


def project_third(blocks, attention, pieces):
    frames, features = attention.shape
    columns = pieces[0].shape[1]
    return pl.pallas_call(
        project_third_kernel,
        out_shape=jax.ShapeDtypeStruct((1, frames, 4 * columns), blocks.dtype),
        in_specs=[WHOLE] * 6,
        out_specs=IN_HBM,
        scratch_shapes=[
            pltpu.VMEM((features, columns), jnp.bfloat16),
            pltpu.VMEM((frames, columns), jnp.bfloat16),
            pltpu.SemaphoreType.DMA((4,)),
        ],
        compiler_params=params(24),
        cost_estimate=projection_cost(frames, features, columns),
        name="project_third_shard",
    )(blocks, attention, *pieces)


def per_device(ctx, fsdp, queries, key_rows, value_rows, lengths, out_weight):
    def exchange(array, axis, flip):
        size = ctx if axis == "ctx" else fsdp
        return lax.ppermute(array, axis, [(i, i ^ flip) for i in range(size)])

    def exchange_chips(arrays):
        return [exchange(array, "ctx", flip) for flip, array in zip(FLIPS[1:], arrays)]

    def exchange_in_plane(array):
        return lax.ppermute(array, "ctx", [(i, i ^ (4 if i % 2 else 2)) for i in range(ctx)])

    def exchange_along(array, *flips):
        pairs = [(i * fsdp + z, i * fsdp + (z ^ flips[i % 2])) for i in range(ctx) for z in range(fsdp)]
        return lax.ppermute(array, ("ctx", "fsdp"), pairs)

    core = place_in_group() & 1
    split_columns = fsdp == 4
    lengths = jnp.broadcast_to(lengths, (8, 128))
    rows, half = copy_in(queries, key_rows, value_rows, out_weight, split_columns)
    if split_columns:
        fetched = exchange_along(half, 2, 1)
    else:
        half = lax.all_gather(half, "fsdp", axis=1, tiled=True)

    own, *by_chip = turn(rows)
    same = exchange_chips(by_chip)
    own_other = exchange(own[1:], "ctx", 1)
    if split_columns:
        fetched, own_other, lengths = lax.optimization_barrier((fetched, own_other, lengths))
        passed = exchange_in_plane(fetched)
        depth = half.shape[0]
        part = depth // 2 + 16
        third = lax.dynamic_slice_in_dim(fetched, core * (depth - part), part, 0)
        third = exchange_along(third, 1, 2)
    same, own_other = lax.optimization_barrier((same, own_other))
    other = exchange(stack_keys_and_values(same), "ctx", 1)
    same = [own, *same]

    groups = ctx // HEADS
    rest = None
    if groups > 1:
        pairs = [own[1:], own_other]
        for at, array in enumerate(same[1:]):
            pairs += [array[1:], other[at]]
        across = [[head + first for first in range(0, ctx, HEADS)] for head in range(HEADS)]
        rest = lax.all_gather(jnp.stack(pairs), "ctx", axis=0, axis_index_groups=across, tiled=True)
    mixed = attend(lengths, same, own_other, other, rest, groups)

    heads = [mixed[0], *exchange_chips(mixed[1:])]
    if not split_columns:
        return project(heads, [half, exchange(half, "ctx", 1)])
    third_passed = exchange_in_plane(third)
    heads[3], fetched = lax.optimization_barrier((heads[3], fetched))
    heads[1], heads[2], passed, third = lax.optimization_barrier((heads[1], heads[2], passed, third))
    fetched_other, passed_other, third_other, third_passed_other = (
        exchange(array, "ctx", 1) for array in (fetched, passed, third, third_passed)
    )
    blocks, attention = project_near(heads, out_weight, [fetched, passed, fetched_other, passed_other])
    return project_third(blocks, attention, [third, third_passed, third_other, third_passed_other])


def solution(mesh):
    return jax.shard_map(
        functools.partial(per_device, mesh.shape["ctx"], mesh.shape["fsdp"]),
        mesh=mesh,
        in_specs=(
            P("fsdp", "ctx", None),
            P("fsdp", "ctx", None),
            P("fsdp", "ctx", None),
            P("fsdp"),
            P(None, "fsdp"),
        ),
        out_specs=P("fsdp", "ctx", None),
        check_vma=False,
    )
```

```python
import functools
import math

import jax
import jax.numpy as jnp
from jax import lax
from jax.experimental import pallas as pl
from jax.experimental.pallas import tpu as pltpu
from jax.sharding import PartitionSpec as P

HEADS = 8
FLIPS = tuple(range(0, HEADS, 2))
WHOLE = pl.BlockSpec(memory_space=pltpu.VMEM)
IN_HBM = pl.BlockSpec(memory_space=pltpu.HBM)


def params(mebibytes=48):
    return pltpu.CompilerParams(vmem_limit_bytes=mebibytes * 1024 * 1024)


def place_in_group():
    return lax.axis_index("ctx") % HEADS


def parity_of(place):
    return ((place >> 2) ^ (place >> 1)) & 1


def copy_in_kernel(by_parity, query_ref, key_ref, value_ref, weight_ref, rows_ref, half_ref, sems):
    place = place_in_group()
    first = (parity_of(place) if by_parity else place & 1) * half_ref.shape[0]
    copies = [pltpu.make_async_copy(weight_ref.at[pl.ds(pl.multiple_of(first, 32), half_ref.shape[0])], half_ref, sems.at[3])]
    for part, ref in enumerate((query_ref, key_ref, value_ref)):
        copies.append(pltpu.make_async_copy(ref.at[0], rows_ref.at[part], sems.at[part]))
    for copy in copies:
        copy.start()
    for copy in copies:
        copy.wait()


def copy_in(queries, key_rows, value_rows, out_weight, by_parity):
    _, frames, features = queries.shape
    half = (out_weight.shape[0] // 2, out_weight.shape[1])
    arrays = [pltpu.with_memory_space_constraint(array, pltpu.HBM) for array in (queries, key_rows, value_rows, out_weight)]
    return pl.pallas_call(
        functools.partial(copy_in_kernel, by_parity),
        out_shape=[pltpu.VMEM((3, frames, features), queries.dtype), pltpu.VMEM(half, out_weight.dtype)],
        in_specs=[IN_HBM] * 4,
        out_specs=[WHOLE] * 2,
        scratch_shapes=[pltpu.SemaphoreType.DMA((4,))],
        compiler_params=params(16),
        name="copy_in",
    )(*arrays)


def turn_kernel(rows_ref, *refs):
    outs, turned = refs[:-1], refs[-1]
    features = outs[0].shape[1]
    chip = place_in_group() >> 1
    for part in range(3):
        turned[part] = rows_ref[part].T
        for flip, out_ref in zip(FLIPS, outs):
            first = pl.multiple_of((chip ^ (flip >> 1)) * features, 32)
            out_ref[part] = turned[part, pl.ds(first, features), :]


def turn(rows):
    _, frames, features = rows.shape
    return pl.pallas_call(
        turn_kernel,
        out_shape=[pltpu.VMEM((3, features // len(FLIPS), frames), rows.dtype)] * len(FLIPS),
        in_specs=[WHOLE],
        out_specs=[WHOLE] * len(FLIPS),
        scratch_shapes=[pltpu.VMEM((3, features, frames), rows.dtype)],
        compiler_params=params(16),
        name="turn_heads",
    )(rows)


def attention_kernel(groups, lengths_ref, *refs):
    each = len(FLIPS)
    same, own_other, other = refs[:each], refs[each], refs[each + 1]
    rest_ref = refs[each + 2] if groups > 1 else None
    outs, (keys, values) = refs[-2 - each : -2], refs[-2:]
    block = outs[0].shape[1]
    head_size = outs[0].shape[0] // 2
    place = place_in_group()
    scale = jnp.float32(math.log2(math.e) / math.sqrt(head_size))
    pad = keys.shape[2] - head_size

    def piece(at, head, part):
        rows = slice(head * head_size, (head + 1) * head_size)
        if groups > 1:
            return rest_ref[at, part - 1, rows, :]
        if at % 2 == 0:
            return same[at // 2][part, rows, :]
        return other[at // 2 - 1, part - 1, rows, :] if at > 1 else own_other[part - 1, rows, :]

    ones = jnp.where(lax.broadcasted_iota(jnp.int32, (pad, block), 0) == 0, 1.0, 0.0).astype(keys.dtype)
    at_feature = lax.broadcasted_iota(jnp.int32, (pad, block), 0)
    at_frame = lax.broadcasted_iota(jnp.int32, (pad, block), 1)

    def prepare(head):
        for at in range(groups * HEADS):
            here = slice(at * block, (at + 1) * block)
            frame = (at // HEADS * HEADS + (place ^ (at % HEADS))) * block + at_frame
            bias = jnp.where((at_feature == 0) & (frame >= lengths_ref[:1, :]), -1e30, 0.0).astype(keys.dtype)
            keys[head, here, :] = jnp.concatenate([piece(at, head, 1), bias], axis=0).T
            values[head, :, here] = jnp.concatenate([piece(at, head, 2), ones], axis=0)

    def score(head, flips):
        rows = slice(head * head_size, (head + 1) * head_size)
        query = [jnp.concatenate([same[flip // 2][0, rows, :], ones], axis=0) for flip in flips]
        return jnp.dot(keys[head], jnp.concatenate(query, axis=1), preferred_element_type=jnp.float32)

    chunks = [(head, flips) for head in range(2) for flips in (FLIPS[:2], FLIPS[2:])]
    prepare(0)
    later = score(*chunks[0])
    prepare(1)
    for at, (head, flips) in enumerate(chunks):
        scores = later
        if at + 1 < len(chunks):
            later = score(*chunks[at + 1])
        row_max = jnp.max(scores, axis=0, keepdims=True) * scale
        probs = jnp.exp2(scores * scale - row_max).astype(jnp.bfloat16)
        mixed = jnp.dot(values[head], probs, preferred_element_type=jnp.float32)
        mixed = (mixed[:head_size] / mixed[head_size : head_size + 1]).astype(jnp.bfloat16)
        for half, flip in enumerate(flips):
            outs[flip // 2][head * head_size : (head + 1) * head_size, :] = mixed[:, half * block : (half + 1) * block]


def stack_kernel(*refs):
    for at, ref in enumerate(refs[:-1]):
        refs[-1][at] = ref[1:]


def stack_keys_and_values(arrays):
    parts, features, frames = arrays[0].shape
    return pl.pallas_call(
        stack_kernel,
        out_shape=pltpu.VMEM((len(arrays), parts - 1, features, frames), arrays[0].dtype),
        in_specs=[WHOLE] * len(arrays),
        out_specs=WHOLE,
        compiler_params=params(16),
        name="stack_keys_and_values",
    )(*arrays)


def attend(lengths, same, own_other, other, rest, groups):
    _, features, block = same[0].shape
    keys = groups * HEADS * block
    padded = features // 2 + 32
    rest = [] if rest is None else [rest]
    return pl.pallas_call(
        functools.partial(attention_kernel, groups),
        out_shape=[pltpu.VMEM((features, block), jnp.bfloat16)] * len(FLIPS),
        in_specs=[WHOLE] * (3 + len(FLIPS) + len(rest)),
        out_specs=[WHOLE] * len(FLIPS),
        scratch_shapes=[pltpu.VMEM((2, keys, padded), jnp.bfloat16), pltpu.VMEM((2, padded, keys), jnp.bfloat16)],
        compiler_params=params(32),
        cost_estimate=pl.CostEstimate(flops=8 * keys * keys * features, bytes_accessed=0, transcendentals=0),
        name="attend_two_heads",
    )(lengths, *same, own_other, other, *rest)


def gather_heads(heads, turned):
    rows = heads[0].shape[0]
    for flip, ref in zip(FLIPS, heads):
        first = pl.multiple_of(((place_in_group() ^ flip) >> 1) * rows, 32)
        turned[pl.ds(first, rows), :] = ref[...]


def project_kernel(*refs):
    each = len(FLIPS)
    heads, halves, (out_ref, turned, weight) = refs[:each], refs[each : each + 2], refs[each + 2 :]
    gather_heads(heads, turned)
    half = weight.shape[0] // 2
    for other, ref in enumerate(halves):
        weight[pl.ds(pl.multiple_of(((place_in_group() & 1) ^ other) * half, 32), half), :] = ref[...]
    out_ref[0] = jnp.dot(turned[...].T, weight[...], preferred_element_type=jnp.float32).astype(out_ref.dtype)


def project_near_kernel(*refs):
    each = len(FLIPS)
    heads, own_ref, pieces = refs[:each], refs[each], refs[each + 1 : each + 5]
    blocks_ref, attention_ref, turned, weight = refs[each + 5 :]
    gather_heads(heads, turned)
    attention = turned[...].T
    attention_ref[...] = attention
    place = place_in_group()
    half = pieces[0].shape[0]
    for flip in (1, 2):
        mine = (place & 1) == 2 - flip
        for other in range(2):
            here = pl.ds(pl.multiple_of((parity_of(place) ^ other) * half, 32), half)
            weight[flip - 1, here, :] = jnp.where(mine, pieces[other][...], pieces[2 + other][...])
    for flip, block in enumerate((own_ref[...], weight[0], weight[1])):
        blocks_ref[flip] = jnp.dot(attention, block, preferred_element_type=jnp.float32).astype(blocks_ref.dtype)


def project_third_kernel(blocks_ref, attention_ref, *refs):
    pieces, (out_ref, weight, last, sems) = refs[:4], refs[4:]
    place, shard = place_in_group(), lax.axis_index("fsdp")
    part, columns = pieces[0].shape
    half = weight.shape[0] // 2

    def copy_out(flip, block_ref):
        here = pl.ds(pl.multiple_of((shard ^ flip) * columns, 128), columns)
        copy = pltpu.make_async_copy(block_ref, out_ref.at[0, :, here], sems.at[flip])
        copy.start()
        return copy

    copies = [copy_out(flip, blocks_ref.at[flip]) for flip in range(3)]
    for other in range(2):
        for flip in range(2):
            first = (parity_of(place) ^ flip) * half + ((place & 1) ^ other) * (half - part)
            weight[pl.ds(pl.multiple_of(first, 16), part), :] = pieces[2 * other + flip][...]
    last[...] = jnp.dot(attention_ref[...], weight[...], preferred_element_type=jnp.float32).astype(last.dtype)
    copies.append(copy_out(3, last))
    for copy in copies:
        copy.wait()


def projection_cost(frames, features, columns):
    return pl.CostEstimate(
        flops=2 * features * frames * columns, bytes_accessed=2 * features * columns, transcendentals=0
    )


def project(heads, halves):
    rows, frames = heads[0].shape
    features, width = len(FLIPS) * rows, halves[0].shape[1]
    return pl.pallas_call(
        project_kernel,
        out_shape=jax.ShapeDtypeStruct((1, frames, width), jnp.bfloat16),
        in_specs=[WHOLE] * (len(FLIPS) + 2),
        out_specs=WHOLE,
        scratch_shapes=[pltpu.VMEM((features, frames), jnp.bfloat16), pltpu.VMEM((features, width), jnp.bfloat16)],
        compiler_params=params(24),
        cost_estimate=projection_cost(frames, features, width),
        name="project_heads",
    )(*heads, *halves)


def project_near(heads, own, pieces):
    frames = heads[0].shape[1]
    features, columns = own.shape
    return pl.pallas_call(
        project_near_kernel,
        out_shape=[pltpu.VMEM((3, frames, columns), jnp.bfloat16), pltpu.VMEM((frames, features), jnp.bfloat16)],
        in_specs=[WHOLE] * (len(FLIPS) + 5),
        out_specs=[WHOLE] * 2,
        scratch_shapes=[
            pltpu.VMEM((features, frames), jnp.bfloat16),
            pltpu.VMEM((2, features, columns), jnp.bfloat16),
        ],
        compiler_params=params(24),
        cost_estimate=projection_cost(frames, features, 3 * columns),
        name="project_near_shards",
    )(*heads, own, *pieces)


def project_third(blocks, attention, pieces):
    frames, features = attention.shape
    columns = pieces[0].shape[1]
    return pl.pallas_call(
        project_third_kernel,
        out_shape=jax.ShapeDtypeStruct((1, frames, 4 * columns), blocks.dtype),
        in_specs=[WHOLE] * 6,
        out_specs=IN_HBM,
        scratch_shapes=[
            pltpu.VMEM((features, columns), jnp.bfloat16),
            pltpu.VMEM((frames, columns), jnp.bfloat16),
            pltpu.SemaphoreType.DMA((4,)),
        ],
        compiler_params=params(24),
        cost_estimate=projection_cost(frames, features, columns),
        name="project_third_shard",
    )(blocks, attention, *pieces)


def per_device(ctx, fsdp, queries, key_rows, value_rows, lengths, out_weight):
    def exchange(array, axis, flip):
        size = ctx if axis == "ctx" else fsdp
        return lax.ppermute(array, axis, [(i, i ^ flip) for i in range(size)])

    def exchange_chips(arrays):
        return [exchange(array, "ctx", flip) for flip, array in zip(FLIPS[1:], arrays)]

    def exchange_in_plane(array):
        return lax.ppermute(array, "ctx", [(i, i ^ (4 if i % 2 else 2)) for i in range(ctx)])

    def exchange_along(array, *flips):
        pairs = [(i * fsdp + z, i * fsdp + (z ^ flips[i % 2])) for i in range(ctx) for z in range(fsdp)]
        return lax.ppermute(array, ("ctx", "fsdp"), pairs)

    core = place_in_group() & 1
    split_columns = fsdp == 4
    lengths = jnp.broadcast_to(lengths, (8, 128))
    rows, half = copy_in(queries, key_rows, value_rows, out_weight, split_columns)
    if split_columns:
        fetched = exchange_along(half, 2, 1)
    else:
        half = lax.all_gather(half, "fsdp", axis=1, tiled=True)

    own, *by_chip = turn(rows)
    same = exchange_chips(by_chip)
    own_other = exchange(own[1:], "ctx", 1)
    if split_columns:
        fetched, own_other, lengths = lax.optimization_barrier((fetched, own_other, lengths))
        passed = exchange_in_plane(fetched)
        depth = half.shape[0]
        part = depth // 2 + 16
        third = lax.dynamic_slice_in_dim(fetched, core * (depth - part), part, 0)
        third = exchange_along(third, 1, 2)
    same, own_other = lax.optimization_barrier((same, own_other))
    other = exchange(stack_keys_and_values(same), "ctx", 1)
    same = [own, *same]

    groups = ctx // HEADS
    rest = None
    if groups > 1:
        pairs = [own[1:], own_other]
        for at, array in enumerate(same[1:]):
            pairs += [array[1:], other[at]]
        across = [[head + first for first in range(0, ctx, HEADS)] for head in range(HEADS)]
        rest = lax.all_gather(jnp.stack(pairs), "ctx", axis=0, axis_index_groups=across, tiled=True)
    mixed = attend(lengths, same, own_other, other, rest, groups)

    heads = [mixed[0], *exchange_chips(mixed[1:])]
    if not split_columns:
        return project(heads, [half, exchange(half, "ctx", 1)])
    third_passed = exchange_in_plane(third)
    heads[3], fetched, third = lax.optimization_barrier((heads[3], fetched, third))
    heads[1], heads[2], passed = lax.optimization_barrier((heads[1], heads[2], passed))
    fetched_other, passed_other, third_other, third_passed_other = (
        exchange(array, "ctx", 1) for array in (fetched, passed, third, third_passed)
    )
    third_other, passed_other = lax.optimization_barrier((third_other, passed_other))
    blocks, attention = project_near(heads, out_weight, [fetched, passed, fetched_other, passed_other])
    return project_third(blocks, attention, [third, third_passed, third_other, third_passed_other])


def solution(mesh):
    return jax.shard_map(
        functools.partial(per_device, mesh.shape["ctx"], mesh.shape["fsdp"]),
        mesh=mesh,
        in_specs=(
            P("fsdp", "ctx", None),
            P("fsdp", "ctx", None),
            P("fsdp", "ctx", None),
            P("fsdp"),
            P(None, "fsdp"),
        ),
        out_specs=P("fsdp", "ctx", None),
        check_vma=False,
    )
```

```python
import functools
import math

import jax
import jax.numpy as jnp
from jax import lax
from jax.experimental import pallas as pl
from jax.experimental.pallas import tpu as pltpu
from jax.sharding import PartitionSpec as P

HEADS = 8
FLIPS = tuple(range(0, HEADS, 2))
WHOLE = pl.BlockSpec(memory_space=pltpu.VMEM)
IN_HBM = pl.BlockSpec(memory_space=pltpu.HBM)


def params(mebibytes=48):
    return pltpu.CompilerParams(vmem_limit_bytes=mebibytes * 1024 * 1024)


def place_in_group():
    return lax.axis_index("ctx") % HEADS


def parity_of(place):
    return ((place >> 2) ^ (place >> 1)) & 1


def copy_in_kernel(by_parity, query_ref, key_ref, value_ref, weight_ref, rows_ref, half_ref, sems):
    place = place_in_group()
    first = (parity_of(place) if by_parity else place & 1) * half_ref.shape[0]
    copies = [pltpu.make_async_copy(weight_ref.at[pl.ds(pl.multiple_of(first, 32), half_ref.shape[0])], half_ref, sems.at[3])]
    for part, ref in enumerate((query_ref, key_ref, value_ref)):
        copies.append(pltpu.make_async_copy(ref.at[0], rows_ref.at[part], sems.at[part]))
    for copy in copies:
        copy.start()
    for copy in copies:
        copy.wait()


def copy_in(queries, key_rows, value_rows, out_weight, by_parity):
    _, frames, features = queries.shape
    half = (out_weight.shape[0] // 2, out_weight.shape[1])
    arrays = [pltpu.with_memory_space_constraint(array, pltpu.HBM) for array in (queries, key_rows, value_rows, out_weight)]
    return pl.pallas_call(
        functools.partial(copy_in_kernel, by_parity),
        out_shape=[pltpu.VMEM((3, frames, features), queries.dtype), pltpu.VMEM(half, out_weight.dtype)],
        in_specs=[IN_HBM] * 4,
        out_specs=[WHOLE] * 2,
        scratch_shapes=[pltpu.SemaphoreType.DMA((4,))],
        compiler_params=params(16),
        name="copy_in",
    )(*arrays)


def turn_kernel(rows_ref, *refs):
    outs, turned = refs[:-1], refs[-1]
    features = outs[0].shape[1]
    chip = place_in_group() >> 1
    for part in range(3):
        turned[part] = rows_ref[part].T
        for flip, out_ref in zip(FLIPS, outs):
            first = pl.multiple_of((chip ^ (flip >> 1)) * features, 32)
            out_ref[part] = turned[part, pl.ds(first, features), :]


def turn(rows):
    _, frames, features = rows.shape
    return pl.pallas_call(
        turn_kernel,
        out_shape=[pltpu.VMEM((3, features // len(FLIPS), frames), rows.dtype)] * len(FLIPS),
        in_specs=[WHOLE],
        out_specs=[WHOLE] * len(FLIPS),
        scratch_shapes=[pltpu.VMEM((3, features, frames), rows.dtype)],
        compiler_params=params(16),
        name="turn_heads",
    )(rows)


def attention_kernel(groups, lengths_ref, *refs):
    each = len(FLIPS)
    same, own_other, other = refs[:each], refs[each], refs[each + 1]
    rest_ref = refs[each + 2] if groups > 1 else None
    outs, (keys, values) = refs[-2 - each : -2], refs[-2:]
    block = outs[0].shape[1]
    head_size = outs[0].shape[0] // 2
    place = place_in_group()
    scale = jnp.float32(math.log2(math.e) / math.sqrt(head_size))
    pad = keys.shape[2] - head_size

    def piece(at, head, part):
        rows = slice(head * head_size, (head + 1) * head_size)
        if groups > 1:
            return rest_ref[at, part - 1, rows, :]
        if at % 2 == 0:
            return same[at // 2][part, rows, :]
        return other[at // 2 - 1, part - 1, rows, :] if at > 1 else own_other[part - 1, rows, :]

    ones = jnp.where(lax.broadcasted_iota(jnp.int32, (pad, block), 0) == 0, 1.0, 0.0).astype(keys.dtype)
    at_feature = lax.broadcasted_iota(jnp.int32, (pad, block), 0)
    at_frame = lax.broadcasted_iota(jnp.int32, (pad, block), 1)

    def prepare(head):
        for at in range(groups * HEADS):
            here = slice(at * block, (at + 1) * block)
            frame = (at // HEADS * HEADS + (place ^ (at % HEADS))) * block + at_frame
            bias = jnp.where((at_feature == 0) & (frame >= lengths_ref[:1, :]), -1e30, 0.0).astype(keys.dtype)
            keys[head, here, :] = jnp.concatenate([piece(at, head, 1), bias], axis=0).T
            values[head, :, here] = jnp.concatenate([piece(at, head, 2), ones], axis=0)

    def score(head, flips):
        rows = slice(head * head_size, (head + 1) * head_size)
        query = [jnp.concatenate([same[flip // 2][0, rows, :], ones], axis=0) for flip in flips]
        return jnp.dot(keys[head], jnp.concatenate(query, axis=1), preferred_element_type=jnp.float32)

    chunks = [(head, flips) for head in range(2) for flips in (FLIPS[:2], FLIPS[2:])]
    prepare(0)
    later = score(*chunks[0])
    prepare(1)
    for at, (head, flips) in enumerate(chunks):
        scores = later
        if at + 1 < len(chunks):
            later = score(*chunks[at + 1])
        row_max = jnp.max(scores, axis=0, keepdims=True) * scale
        probs = jnp.exp2(scores * scale - row_max).astype(jnp.bfloat16)
        mixed = jnp.dot(values[head], probs, preferred_element_type=jnp.float32)
        mixed = (mixed[:head_size] / mixed[head_size : head_size + 1]).astype(jnp.bfloat16)
        for half, flip in enumerate(flips):
            outs[flip // 2][head * head_size : (head + 1) * head_size, :] = mixed[:, half * block : (half + 1) * block]


def stack_kernel(*refs):
    for at, ref in enumerate(refs[:-1]):
        refs[-1][at] = ref[1:]


def stack_keys_and_values(arrays):
    parts, features, frames = arrays[0].shape
    return pl.pallas_call(
        stack_kernel,
        out_shape=pltpu.VMEM((len(arrays), parts - 1, features, frames), arrays[0].dtype),
        in_specs=[WHOLE] * len(arrays),
        out_specs=WHOLE,
        compiler_params=params(16),
        name="stack_keys_and_values",
    )(*arrays)


def attend(lengths, same, own_other, other, rest, groups):
    _, features, block = same[0].shape
    keys = groups * HEADS * block
    padded = features // 2 + 32
    rest = [] if rest is None else [rest]
    return pl.pallas_call(
        functools.partial(attention_kernel, groups),
        out_shape=[pltpu.VMEM((features, block), jnp.bfloat16)] * len(FLIPS),
        in_specs=[WHOLE] * (3 + len(FLIPS) + len(rest)),
        out_specs=[WHOLE] * len(FLIPS),
        scratch_shapes=[pltpu.VMEM((2, keys, padded), jnp.bfloat16), pltpu.VMEM((2, padded, keys), jnp.bfloat16)],
        compiler_params=params(32),
        cost_estimate=pl.CostEstimate(flops=8 * keys * keys * features, bytes_accessed=0, transcendentals=0),
        name="attend_two_heads",
    )(lengths, *same, own_other, other, *rest)


def gather_heads(heads, turned):
    rows = heads[0].shape[0]
    for flip, ref in zip(FLIPS, heads):
        first = pl.multiple_of(((place_in_group() ^ flip) >> 1) * rows, 32)
        turned[pl.ds(first, rows), :] = ref[...]


def project_kernel(*refs):
    each = len(FLIPS)
    heads, halves, (out_ref, turned, weight) = refs[:each], refs[each : each + 2], refs[each + 2 :]
    gather_heads(heads, turned)
    half = weight.shape[0] // 2
    for other, ref in enumerate(halves):
        weight[pl.ds(pl.multiple_of(((place_in_group() & 1) ^ other) * half, 32), half), :] = ref[...]
    out_ref[0] = jnp.dot(turned[...].T, weight[...], preferred_element_type=jnp.float32).astype(out_ref.dtype)


def project_near_kernel(*refs):
    each = len(FLIPS)
    heads, own_ref, pieces = refs[:each], refs[each], refs[each + 1 : each + 5]
    blocks_ref, attention_ref, turned, weight = refs[each + 5 :]
    gather_heads(heads, turned)
    attention = turned[...].T
    attention_ref[...] = attention
    place = place_in_group()
    half = pieces[0].shape[0]
    for flip in (1, 2):
        mine = (place & 1) == 2 - flip
        for other in range(2):
            here = pl.ds(pl.multiple_of((parity_of(place) ^ other) * half, 32), half)
            weight[flip - 1, here, :] = jnp.where(mine, pieces[other][...], pieces[2 + other][...])
    for flip, block in enumerate((own_ref[...], weight[0], weight[1])):
        blocks_ref[flip] = jnp.dot(attention, block, preferred_element_type=jnp.float32).astype(blocks_ref.dtype)


def project_third_kernel(blocks_ref, attention_ref, *refs):
    pieces, (out_ref, weight, last, sems) = refs[:4], refs[4:]
    place, shard = place_in_group(), lax.axis_index("fsdp")
    part, columns = pieces[0].shape
    half = weight.shape[0] // 2

    def copy_out(flip, block_ref):
        here = pl.ds(pl.multiple_of((shard ^ flip) * columns, 128), columns)
        copy = pltpu.make_async_copy(block_ref, out_ref.at[0, :, here], sems.at[flip])
        copy.start()
        return copy

    copies = [copy_out(flip, blocks_ref.at[flip]) for flip in range(3)]
    for other in range(2):
        for flip in range(2):
            first = (parity_of(place) ^ flip) * half + ((place & 1) ^ other) * (half - part) // 2
            ref = pieces[2 * other + flip]
            for rest in range(2):
                here = pl.ds(pl.multiple_of(first + rest * (half // 2), 16), part // 2)
                weight[here, :] = ref[rest * (part // 2) : (rest + 1) * (part // 2), :]
    last[...] = jnp.dot(attention_ref[...], weight[...], preferred_element_type=jnp.float32).astype(last.dtype)
    copies.append(copy_out(3, last))
    for copy in copies:
        copy.wait()


def projection_cost(frames, features, columns):
    return pl.CostEstimate(
        flops=2 * features * frames * columns, bytes_accessed=2 * features * columns, transcendentals=0
    )


def project(heads, halves):
    rows, frames = heads[0].shape
    features, width = len(FLIPS) * rows, halves[0].shape[1]
    return pl.pallas_call(
        project_kernel,
        out_shape=jax.ShapeDtypeStruct((1, frames, width), jnp.bfloat16),
        in_specs=[WHOLE] * (len(FLIPS) + 2),
        out_specs=WHOLE,
        scratch_shapes=[pltpu.VMEM((features, frames), jnp.bfloat16), pltpu.VMEM((features, width), jnp.bfloat16)],
        compiler_params=params(24),
        cost_estimate=projection_cost(frames, features, width),
        name="project_heads",
    )(*heads, *halves)


def project_near(heads, own, pieces):
    frames = heads[0].shape[1]
    features, columns = own.shape
    return pl.pallas_call(
        project_near_kernel,
        out_shape=[pltpu.VMEM((3, frames, columns), jnp.bfloat16), pltpu.VMEM((frames, features), jnp.bfloat16)],
        in_specs=[WHOLE] * (len(FLIPS) + 5),
        out_specs=[WHOLE] * 2,
        scratch_shapes=[
            pltpu.VMEM((features, frames), jnp.bfloat16),
            pltpu.VMEM((2, features, columns), jnp.bfloat16),
        ],
        compiler_params=params(24),
        cost_estimate=projection_cost(frames, features, 3 * columns),
        name="project_near_shards",
    )(*heads, own, *pieces)


def project_third(blocks, attention, pieces):
    frames, features = attention.shape
    columns = pieces[0].shape[1]
    return pl.pallas_call(
        project_third_kernel,
        out_shape=jax.ShapeDtypeStruct((1, frames, 4 * columns), blocks.dtype),
        in_specs=[WHOLE] * 6,
        out_specs=IN_HBM,
        scratch_shapes=[
            pltpu.VMEM((features, columns), jnp.bfloat16),
            pltpu.VMEM((frames, columns), jnp.bfloat16),
            pltpu.SemaphoreType.DMA((4,)),
        ],
        compiler_params=params(24),
        cost_estimate=projection_cost(frames, features, columns),
        name="project_third_shard",
    )(blocks, attention, *pieces)


def per_device(ctx, fsdp, queries, key_rows, value_rows, lengths, out_weight):
    def exchange(array, axis, flip):
        size = ctx if axis == "ctx" else fsdp
        return lax.ppermute(array, axis, [(i, i ^ flip) for i in range(size)])

    def exchange_chips(arrays):
        return [exchange(array, "ctx", flip) for flip, array in zip(FLIPS[1:], arrays)]

    def exchange_in_plane(array):
        return lax.ppermute(array, "ctx", [(i, i ^ (4 if i % 2 else 2)) for i in range(ctx)])

    def exchange_along(array, *flips):
        pairs = [(i * fsdp + z, i * fsdp + (z ^ flips[i % 2])) for i in range(ctx) for z in range(fsdp)]
        return lax.ppermute(array, ("ctx", "fsdp"), pairs)

    core = place_in_group() & 1
    split_columns = fsdp == 4
    lengths = jnp.broadcast_to(lengths, (8, 128))
    rows, half = copy_in(queries, key_rows, value_rows, out_weight, split_columns)
    if split_columns:
        depth = half.shape[0]
        fetched_first = exchange_along(half[: depth // 2], 2, 1)
    else:
        half = lax.all_gather(half, "fsdp", axis=1, tiled=True)

    own, *by_chip = turn(rows)
    same = exchange_chips(by_chip)
    own_other = exchange(own[1:], "ctx", 1)
    if split_columns:
        fetched_first, own_other, lengths, rest = lax.optimization_barrier(
            (fetched_first, own_other, lengths, half[depth // 2 :])
        )
        fetched_second = exchange_along(rest, 2, 1)

        def forward(rows):
            part = depth // 4 + 16
            rows = lax.dynamic_slice_in_dim(rows, core * (depth // 2 - part), part, 0)
            return exchange_along(rows, 1, 2)

        third_first = forward(fetched_first)
        fetched_second, third_first = lax.optimization_barrier((fetched_second, third_first))
        fetched = jnp.concatenate([fetched_first, fetched_second], axis=0)
        passed = exchange_in_plane(fetched)
        third = jnp.concatenate([third_first, forward(fetched_second)], axis=0)
    same, own_other = lax.optimization_barrier((same, own_other))
    other = exchange(stack_keys_and_values(same), "ctx", 1)
    same = [own, *same]

    groups = ctx // HEADS
    rest = None
    if groups > 1:
        pairs = [own[1:], own_other]
        for at, array in enumerate(same[1:]):
            pairs += [array[1:], other[at]]
        across = [[head + first for first in range(0, ctx, HEADS)] for head in range(HEADS)]
        rest = lax.all_gather(jnp.stack(pairs), "ctx", axis=0, axis_index_groups=across, tiled=True)
    mixed = attend(lengths, same, own_other, other, rest, groups)

    heads = [mixed[0], *exchange_chips(mixed[1:])]
    if not split_columns:
        return project(heads, [half, exchange(half, "ctx", 1)])
    third_passed = exchange_in_plane(third)
    heads[3], fetched, third = lax.optimization_barrier((heads[3], fetched, third))
    heads[1], heads[2], passed = lax.optimization_barrier((heads[1], heads[2], passed))
    fetched_other, passed_other, third_other, third_passed_other = (
        exchange(array, "ctx", 1) for array in (fetched, passed, third, third_passed)
    )
    third_other, passed_other = lax.optimization_barrier((third_other, passed_other))
    blocks, attention = project_near(heads, out_weight, [fetched, passed, fetched_other, passed_other])
    return project_third(blocks, attention, [third, third_passed, third_other, third_passed_other])


def solution(mesh):
    return jax.shard_map(
        functools.partial(per_device, mesh.shape["ctx"], mesh.shape["fsdp"]),
        mesh=mesh,
        in_specs=(
            P("fsdp", "ctx", None),
            P("fsdp", "ctx", None),
            P("fsdp", "ctx", None),
            P("fsdp"),
            P(None, "fsdp"),
        ),
        out_specs=P("fsdp", "ctx", None),
        check_vma=False,
    )
```

```python
import functools
import math

import jax
import jax.numpy as jnp
from jax import lax
from jax.experimental import pallas as pl
from jax.experimental.pallas import tpu as pltpu
from jax.sharding import PartitionSpec as P

HEADS = 8
FLIPS = tuple(range(0, HEADS, 2))
WHOLE = pl.BlockSpec(memory_space=pltpu.VMEM)
IN_HBM = pl.BlockSpec(memory_space=pltpu.HBM)


def params(mebibytes=48):
    return pltpu.CompilerParams(vmem_limit_bytes=mebibytes * 1024 * 1024)


def place_in_group():
    return lax.axis_index("ctx") % HEADS


def parity_of(place):
    return ((place >> 2) ^ (place >> 1)) & 1


def copy_in_kernel(by_parity, query_ref, key_ref, value_ref, weight_ref, rows_ref, half_ref, sems):
    place = place_in_group()
    first = (parity_of(place) if by_parity else place & 1) * half_ref.shape[0]
    copies = [pltpu.make_async_copy(weight_ref.at[pl.ds(pl.multiple_of(first, 32), half_ref.shape[0])], half_ref, sems.at[3])]
    for part, ref in enumerate((query_ref, key_ref, value_ref)):
        copies.append(pltpu.make_async_copy(ref.at[0], rows_ref.at[part], sems.at[part]))
    for copy in copies:
        copy.start()
    for copy in copies:
        copy.wait()


def copy_in(queries, key_rows, value_rows, out_weight, by_parity):
    _, frames, features = queries.shape
    half = (out_weight.shape[0] // 2, out_weight.shape[1])
    arrays = [pltpu.with_memory_space_constraint(array, pltpu.HBM) for array in (queries, key_rows, value_rows, out_weight)]
    return pl.pallas_call(
        functools.partial(copy_in_kernel, by_parity),
        out_shape=[pltpu.VMEM((3, frames, features), queries.dtype), pltpu.VMEM(half, out_weight.dtype)],
        in_specs=[IN_HBM] * 4,
        out_specs=[WHOLE] * 2,
        scratch_shapes=[pltpu.SemaphoreType.DMA((4,))],
        compiler_params=params(16),
        name="copy_in",
    )(*arrays)


def turn_kernel(rows_ref, *refs):
    outs, turned = refs[:-1], refs[-1]
    features = outs[0].shape[1]
    chip = place_in_group() >> 1
    for part in range(3):
        turned[part] = rows_ref[part].T
        for flip, out_ref in zip(FLIPS, outs):
            first = pl.multiple_of((chip ^ (flip >> 1)) * features, 32)
            out_ref[part] = turned[part, pl.ds(first, features), :]


def turn(rows):
    _, frames, features = rows.shape
    return pl.pallas_call(
        turn_kernel,
        out_shape=[pltpu.VMEM((3, features // len(FLIPS), frames), rows.dtype)] * len(FLIPS),
        in_specs=[WHOLE],
        out_specs=[WHOLE] * len(FLIPS),
        scratch_shapes=[pltpu.VMEM((3, features, frames), rows.dtype)],
        compiler_params=params(16),
        name="turn_heads",
    )(rows)


def attention_kernel(groups, lengths_ref, *refs):
    each = len(FLIPS)
    same, own_other, other = refs[:each], refs[each], refs[each + 1]
    rest_ref = refs[each + 2] if groups > 1 else None
    outs, (keys, values) = refs[-2 - each : -2], refs[-2:]
    block = outs[0].shape[1]
    head_size = outs[0].shape[0] // 2
    place = place_in_group()
    scale = jnp.float32(math.log2(math.e) / math.sqrt(head_size))
    pad = keys.shape[2] - head_size

    def piece(at, head, part):
        rows = slice(head * head_size, (head + 1) * head_size)
        if groups > 1:
            return rest_ref[at, part - 1, rows, :]
        if at % 2 == 0:
            return same[at // 2][part, rows, :]
        return other[at // 2 - 1, part - 1, rows, :] if at > 1 else own_other[part - 1, rows, :]

    ones = jnp.where(lax.broadcasted_iota(jnp.int32, (pad, block), 0) == 0, 1.0, 0.0).astype(keys.dtype)
    at_feature = lax.broadcasted_iota(jnp.int32, (pad, block), 0)
    at_frame = lax.broadcasted_iota(jnp.int32, (pad, block), 1)

    def prepare(head):
        for at in range(groups * HEADS):
            here = slice(at * block, (at + 1) * block)
            frame = (at // HEADS * HEADS + (place ^ (at % HEADS))) * block + at_frame
            bias = jnp.where((at_feature == 0) & (frame >= lengths_ref[:1, :]), -1e30, 0.0).astype(keys.dtype)
            keys[head, here, :] = jnp.concatenate([piece(at, head, 1), bias], axis=0).T
            values[head, :, here] = jnp.concatenate([piece(at, head, 2), ones], axis=0)

    def score(head, flips):
        rows = slice(head * head_size, (head + 1) * head_size)
        query = jnp.concatenate([jnp.concatenate([same[flip // 2][0, rows, :], ones], axis=0) for flip in flips], axis=1)
        return [jnp.dot(keys[head, part, :], query, preferred_element_type=jnp.float32) for part in parts]

    parts = [slice(first, first + keys.shape[1] // 4) for first in range(0, keys.shape[1], keys.shape[1] // 4)]
    chunks = [(head, flips) for head in range(2) for flips in (FLIPS[:2], FLIPS[2:])]
    prepare(0)
    later = score(*chunks[0])
    prepare(1)
    for at, (head, flips) in enumerate(chunks):
        scores = later
        if at + 1 < len(chunks):
            later = score(*chunks[at + 1])
        row_max = functools.reduce(jnp.maximum, (jnp.max(part, axis=0, keepdims=True) for part in scores)) * scale
        mixed = jnp.zeros((values.shape[1], scores[0].shape[1]), jnp.float32)
        for part, part_scores in zip(parts, scores):
            probs = jnp.exp2(part_scores * scale - row_max).astype(jnp.bfloat16)
            mixed = mixed + jnp.dot(values[head, :, part], probs, preferred_element_type=jnp.float32)
        mixed = (mixed[:head_size] / mixed[head_size : head_size + 1]).astype(jnp.bfloat16)
        for half, flip in enumerate(flips):
            outs[flip // 2][head * head_size : (head + 1) * head_size, :] = mixed[:, half * block : (half + 1) * block]


def stack_kernel(*refs):
    for at, ref in enumerate(refs[:-1]):
        refs[-1][at] = ref[1:]


def stack_keys_and_values(arrays):
    parts, features, frames = arrays[0].shape
    return pl.pallas_call(
        stack_kernel,
        out_shape=pltpu.VMEM((len(arrays), parts - 1, features, frames), arrays[0].dtype),
        in_specs=[WHOLE] * len(arrays),
        out_specs=WHOLE,
        compiler_params=params(16),
        name="stack_keys_and_values",
    )(*arrays)


def attend(lengths, same, own_other, other, rest, groups):
    _, features, block = same[0].shape
    keys = groups * HEADS * block
    padded = features // 2 + 32
    rest = [] if rest is None else [rest]
    return pl.pallas_call(
        functools.partial(attention_kernel, groups),
        out_shape=[pltpu.VMEM((features, block), jnp.bfloat16)] * len(FLIPS),
        in_specs=[WHOLE] * (3 + len(FLIPS) + len(rest)),
        out_specs=[WHOLE] * len(FLIPS),
        scratch_shapes=[pltpu.VMEM((2, keys, padded), jnp.bfloat16), pltpu.VMEM((2, padded, keys), jnp.bfloat16)],
        compiler_params=params(32),
        cost_estimate=pl.CostEstimate(flops=8 * keys * keys * features, bytes_accessed=0, transcendentals=0),
        name="attend_two_heads",
    )(lengths, *same, own_other, other, *rest)


def gather_heads(heads, turned):
    rows = heads[0].shape[0]
    for flip, ref in zip(FLIPS, heads):
        first = pl.multiple_of(((place_in_group() ^ flip) >> 1) * rows, 32)
        turned[pl.ds(first, rows), :] = ref[...]


def project_kernel(*refs):
    each = len(FLIPS)
    heads, halves, (out_ref, turned, weight) = refs[:each], refs[each : each + 2], refs[each + 2 :]
    gather_heads(heads, turned)
    half = weight.shape[0] // 2
    for other, ref in enumerate(halves):
        weight[pl.ds(pl.multiple_of(((place_in_group() & 1) ^ other) * half, 32), half), :] = ref[...]
    out_ref[0] = jnp.dot(turned[...].T, weight[...], preferred_element_type=jnp.float32).astype(out_ref.dtype)


def project_near_kernel(*refs):
    each = len(FLIPS)
    heads, own_ref, pieces = refs[:each], refs[each], refs[each + 1 : each + 5]
    blocks_ref, attention_ref, turned, weight = refs[each + 5 :]
    gather_heads(heads, turned)
    attention = turned[...].T
    attention_ref[...] = attention
    place = place_in_group()
    half = pieces[0].shape[0]
    for flip in (1, 2):
        mine = (place & 1) == 2 - flip
        for other in range(2):
            here = pl.ds(pl.multiple_of((parity_of(place) ^ other) * half, 32), half)
            weight[flip - 1, here, :] = jnp.where(mine, pieces[other][...], pieces[2 + other][...])
    for flip, block in enumerate((own_ref[...], weight[0], weight[1])):
        blocks_ref[flip] = jnp.dot(attention, block, preferred_element_type=jnp.float32).astype(blocks_ref.dtype)


def project_third_kernel(blocks_ref, attention_ref, *refs):
    pieces, (out_ref, weight, last, sems) = refs[:4], refs[4:]
    place, shard = place_in_group(), lax.axis_index("fsdp")
    part, columns = pieces[0].shape
    half = weight.shape[0] // 2

    def copy_out(flip, block_ref):
        here = pl.ds(pl.multiple_of((shard ^ flip) * columns, 128), columns)
        copy = pltpu.make_async_copy(block_ref, out_ref.at[0, :, here], sems.at[flip])
        copy.start()
        return copy

    copies = [copy_out(flip, blocks_ref.at[flip]) for flip in range(3)]
    for other in range(2):
        for flip in range(2):
            first = (parity_of(place) ^ flip) * half + ((place & 1) ^ other) * (half - part)
            weight[pl.ds(pl.multiple_of(first, 16), part), :] = pieces[2 * other + flip][...]
    last[...] = jnp.dot(attention_ref[...], weight[...], preferred_element_type=jnp.float32).astype(last.dtype)
    copies.append(copy_out(3, last))
    for copy in copies:
        copy.wait()


def projection_cost(frames, features, columns):
    return pl.CostEstimate(
        flops=2 * features * frames * columns, bytes_accessed=2 * features * columns, transcendentals=0
    )


def project(heads, halves):
    rows, frames = heads[0].shape
    features, width = len(FLIPS) * rows, halves[0].shape[1]
    return pl.pallas_call(
        project_kernel,
        out_shape=jax.ShapeDtypeStruct((1, frames, width), jnp.bfloat16),
        in_specs=[WHOLE] * (len(FLIPS) + 2),
        out_specs=WHOLE,
        scratch_shapes=[pltpu.VMEM((features, frames), jnp.bfloat16), pltpu.VMEM((features, width), jnp.bfloat16)],
        compiler_params=params(24),
        cost_estimate=projection_cost(frames, features, width),
        name="project_heads",
    )(*heads, *halves)


def project_near(heads, own, pieces):
    frames = heads[0].shape[1]
    features, columns = own.shape
    return pl.pallas_call(
        project_near_kernel,
        out_shape=[pltpu.VMEM((3, frames, columns), jnp.bfloat16), pltpu.VMEM((frames, features), jnp.bfloat16)],
        in_specs=[WHOLE] * (len(FLIPS) + 5),
        out_specs=[WHOLE] * 2,
        scratch_shapes=[
            pltpu.VMEM((features, frames), jnp.bfloat16),
            pltpu.VMEM((2, features, columns), jnp.bfloat16),
        ],
        compiler_params=params(24),
        cost_estimate=projection_cost(frames, features, 3 * columns),
        name="project_near_shards",
    )(*heads, own, *pieces)


def project_third(blocks, attention, pieces):
    frames, features = attention.shape
    columns = pieces[0].shape[1]
    return pl.pallas_call(
        project_third_kernel,
        out_shape=jax.ShapeDtypeStruct((1, frames, 4 * columns), blocks.dtype),
        in_specs=[WHOLE] * 6,
        out_specs=IN_HBM,
        scratch_shapes=[
            pltpu.VMEM((features, columns), jnp.bfloat16),
            pltpu.VMEM((frames, columns), jnp.bfloat16),
            pltpu.SemaphoreType.DMA((4,)),
        ],
        compiler_params=params(24),
        cost_estimate=projection_cost(frames, features, columns),
        name="project_third_shard",
    )(blocks, attention, *pieces)


def per_device(ctx, fsdp, queries, key_rows, value_rows, lengths, out_weight):
    def exchange(array, axis, flip):
        size = ctx if axis == "ctx" else fsdp
        return lax.ppermute(array, axis, [(i, i ^ flip) for i in range(size)])

    def exchange_chips(arrays):
        return [exchange(array, "ctx", flip) for flip, array in zip(FLIPS[1:], arrays)]

    def exchange_in_plane(array):
        return lax.ppermute(array, "ctx", [(i, i ^ (4 if i % 2 else 2)) for i in range(ctx)])

    def exchange_along(array, *flips):
        pairs = [(i * fsdp + z, i * fsdp + (z ^ flips[i % 2])) for i in range(ctx) for z in range(fsdp)]
        return lax.ppermute(array, ("ctx", "fsdp"), pairs)

    core = place_in_group() & 1
    split_columns = fsdp == 4
    lengths = jnp.broadcast_to(lengths, (8, 128))
    rows, half = copy_in(queries, key_rows, value_rows, out_weight, split_columns)
    if split_columns:
        fetched = exchange_along(half, 2, 1)
    else:
        half = lax.all_gather(half, "fsdp", axis=1, tiled=True)

    own, *by_chip = turn(rows)
    same = exchange_chips(by_chip)
    own_other = exchange(own[1:], "ctx", 1)
    if split_columns:
        fetched, own_other, lengths = lax.optimization_barrier((fetched, own_other, lengths))
        passed = exchange_in_plane(fetched)
        depth = half.shape[0]
        part = depth // 2 + 16
        third = lax.dynamic_slice_in_dim(fetched, core * (depth - part), part, 0)
        third = exchange_along(third, 1, 2)
    same, own_other = lax.optimization_barrier((same, own_other))
    other = exchange(stack_keys_and_values(same), "ctx", 1)
    same = [own, *same]

    groups = ctx // HEADS
    rest = None
    if groups > 1:
        pairs = [own[1:], own_other]
        for at, array in enumerate(same[1:]):
            pairs += [array[1:], other[at]]
        across = [[head + first for first in range(0, ctx, HEADS)] for head in range(HEADS)]
        rest = lax.all_gather(jnp.stack(pairs), "ctx", axis=0, axis_index_groups=across, tiled=True)
    mixed = attend(lengths, same, own_other, other, rest, groups)

    heads = [mixed[0], *exchange_chips(mixed[1:])]
    if not split_columns:
        return project(heads, [half, exchange(half, "ctx", 1)])
    third_passed = exchange_in_plane(third)
    heads[3], fetched, third = lax.optimization_barrier((heads[3], fetched, third))
    heads[1], heads[2], passed = lax.optimization_barrier((heads[1], heads[2], passed))
    fetched_other, passed_other, third_other, third_passed_other = (
        exchange(array, "ctx", 1) for array in (fetched, passed, third, third_passed)
    )
    third_other, passed_other = lax.optimization_barrier((third_other, passed_other))
    blocks, attention = project_near(heads, out_weight, [fetched, passed, fetched_other, passed_other])
    return project_third(blocks, attention, [third, third_passed, third_other, third_passed_other])


def solution(mesh):
    return jax.shard_map(
        functools.partial(per_device, mesh.shape["ctx"], mesh.shape["fsdp"]),
        mesh=mesh,
        in_specs=(
            P("fsdp", "ctx", None),
            P("fsdp", "ctx", None),
            P("fsdp", "ctx", None),
            P("fsdp"),
            P(None, "fsdp"),
        ),
        out_specs=P("fsdp", "ctx", None),
        check_vma=False,
    )
```

```python
import functools
import math

import jax
import jax.numpy as jnp
from jax import lax
from jax.experimental import pallas as pl
from jax.experimental.pallas import tpu as pltpu
from jax.sharding import PartitionSpec as P

HEADS = 8
FLIPS = tuple(range(0, HEADS, 2))
WHOLE = pl.BlockSpec(memory_space=pltpu.VMEM)
IN_HBM = pl.BlockSpec(memory_space=pltpu.HBM)


def params(mebibytes=48):
    return pltpu.CompilerParams(vmem_limit_bytes=mebibytes * 1024 * 1024)


def place_in_group():
    return lax.axis_index("ctx") % HEADS


def parity_of(place):
    return ((place >> 2) ^ (place >> 1)) & 1


def copy_in_kernel(by_parity, query_ref, key_ref, value_ref, weight_ref, rows_ref, half_ref, sems):
    place = place_in_group()
    first = (parity_of(place) if by_parity else place & 1) * half_ref.shape[0]
    copies = [pltpu.make_async_copy(weight_ref.at[pl.ds(pl.multiple_of(first, 32), half_ref.shape[0])], half_ref, sems.at[3])]
    for part, ref in enumerate((query_ref, key_ref, value_ref)):
        copies.append(pltpu.make_async_copy(ref.at[0], rows_ref.at[part], sems.at[part]))
    for copy in copies:
        copy.start()
    for copy in copies:
        copy.wait()


def copy_in(queries, key_rows, value_rows, out_weight, by_parity):
    _, frames, features = queries.shape
    half = (out_weight.shape[0] // 2, out_weight.shape[1])
    arrays = [pltpu.with_memory_space_constraint(array, pltpu.HBM) for array in (queries, key_rows, value_rows, out_weight)]
    return pl.pallas_call(
        functools.partial(copy_in_kernel, by_parity),
        out_shape=[pltpu.VMEM((3, frames, features), queries.dtype), pltpu.VMEM(half, out_weight.dtype)],
        in_specs=[IN_HBM] * 4,
        out_specs=[WHOLE] * 2,
        scratch_shapes=[pltpu.SemaphoreType.DMA((4,))],
        compiler_params=params(16),
        name="copy_in",
    )(*arrays)


def turn_kernel(rows_ref, *refs):
    outs, turned = refs[:-1], refs[-1]
    features = outs[0].shape[1]
    chip = place_in_group() >> 1
    for part in range(3):
        turned[part] = rows_ref[part].T
        for flip, out_ref in zip(FLIPS, outs):
            first = pl.multiple_of((chip ^ (flip >> 1)) * features, 32)
            out_ref[part] = turned[part, pl.ds(first, features), :]


def turn(rows):
    _, frames, features = rows.shape
    return pl.pallas_call(
        turn_kernel,
        out_shape=[pltpu.VMEM((3, features // len(FLIPS), frames), rows.dtype)] * len(FLIPS),
        in_specs=[WHOLE],
        out_specs=[WHOLE] * len(FLIPS),
        scratch_shapes=[pltpu.VMEM((3, features, frames), rows.dtype)],
        compiler_params=params(16),
        name="turn_heads",
    )(rows)


def attention_kernel(groups, lengths_ref, *refs):
    each = len(FLIPS)
    same, own_other, other = refs[:each], refs[each], refs[each + 1]
    rest_ref = refs[each + 2] if groups > 1 else None
    outs, (keys, values) = refs[-2 - each : -2], refs[-2:]
    block = outs[0].shape[1]
    head_size = outs[0].shape[0] // 2
    place = place_in_group()
    scale = jnp.float32(math.log2(math.e) / math.sqrt(head_size))
    pad = keys.shape[2] - head_size

    def piece(at, head, part):
        rows = slice(head * head_size, (head + 1) * head_size)
        if groups > 1:
            return rest_ref[at, part - 1, rows, :]
        if at % 2 == 0:
            return same[at // 2][part, rows, :]
        return other[at // 2 - 1, part - 1, rows, :] if at > 1 else own_other[part - 1, rows, :]

    ones = jnp.where(lax.broadcasted_iota(jnp.int32, (pad, block), 0) == 0, 1.0, 0.0).astype(keys.dtype)
    at_feature = lax.broadcasted_iota(jnp.int32, (pad, block), 0)
    at_frame = lax.broadcasted_iota(jnp.int32, (pad, block), 1)

    def prepare(head):
        for at in range(groups * HEADS):
            here = slice(at * block, (at + 1) * block)
            frame = (at // HEADS * HEADS + (place ^ (at % HEADS))) * block + at_frame
            bias = jnp.where((at_feature == 0) & (frame >= lengths_ref[:1, :]), -1e30, 0.0).astype(keys.dtype)
            keys[head, here, :] = jnp.concatenate([piece(at, head, 1), bias], axis=0).T
            values[head, :, here] = jnp.concatenate([piece(at, head, 2), ones], axis=0)

    def score(head, flips):
        rows = slice(head * head_size, (head + 1) * head_size)
        query = jnp.concatenate([jnp.concatenate([same[flip // 2][0, rows, :], ones], axis=0) for flip in flips], axis=1)
        return [jnp.dot(keys[head, part, :], query, preferred_element_type=jnp.float32) for part in parts]

    parts = [slice(first, first + keys.shape[1] // 4) for first in range(0, keys.shape[1], keys.shape[1] // 4)]
    chunks = [(head, flips) for head in range(2) for flips in (FLIPS[:2], FLIPS[2:])]
    prepare(0)
    later = score(*chunks[0])
    prepare(1)
    for at, (head, flips) in enumerate(chunks):
        scores = later
        if at + 1 < len(chunks):
            later = score(*chunks[at + 1])
        row_max = functools.reduce(jnp.maximum, (jnp.max(part, axis=0, keepdims=True) for part in scores)) * scale
        mixed = jnp.zeros((values.shape[1], scores[0].shape[1]), jnp.float32)
        for part, part_scores in zip(parts, scores):
            probs = jnp.exp2(part_scores * scale - row_max).astype(jnp.bfloat16)
            mixed = mixed + jnp.dot(values[head, :, part], probs, preferred_element_type=jnp.float32)
        mixed = (mixed[:head_size] / mixed[head_size : head_size + 1]).astype(jnp.bfloat16)
        for half, flip in enumerate(flips):
            outs[flip // 2][head * head_size : (head + 1) * head_size, :] = mixed[:, half * block : (half + 1) * block]


def stack_kernel(*refs):
    for at, ref in enumerate(refs[:-1]):
        refs[-1][at] = ref[1:]


def stack_keys_and_values(arrays):
    parts, features, frames = arrays[0].shape
    return pl.pallas_call(
        stack_kernel,
        out_shape=pltpu.VMEM((len(arrays), parts - 1, features, frames), arrays[0].dtype),
        in_specs=[WHOLE] * len(arrays),
        out_specs=WHOLE,
        compiler_params=params(16),
        name="stack_keys_and_values",
    )(*arrays)


def attend(lengths, same, own_other, other, rest, groups):
    _, features, block = same[0].shape
    keys = groups * HEADS * block
    padded = features // 2 + 32
    rest = [] if rest is None else [rest]
    return pl.pallas_call(
        functools.partial(attention_kernel, groups),
        out_shape=[pltpu.VMEM((features, block), jnp.bfloat16)] * len(FLIPS),
        in_specs=[WHOLE] * (3 + len(FLIPS) + len(rest)),
        out_specs=[WHOLE] * len(FLIPS),
        scratch_shapes=[pltpu.VMEM((2, keys, padded), jnp.bfloat16), pltpu.VMEM((2, padded, keys), jnp.bfloat16)],
        compiler_params=params(32),
        cost_estimate=pl.CostEstimate(flops=8 * keys * keys * features, bytes_accessed=0, transcendentals=0),
        name="attend_two_heads",
    )(lengths, *same, own_other, other, *rest)


def gather_heads(heads, turned):
    rows = heads[0].shape[0]
    for flip, ref in zip(FLIPS, heads):
        first = pl.multiple_of(((place_in_group() ^ flip) >> 1) * rows, 32)
        turned[pl.ds(first, rows), :] = ref[...]


def project_kernel(*refs):
    each = len(FLIPS)
    heads, halves, (out_ref, turned, weight) = refs[:each], refs[each : each + 2], refs[each + 2 :]
    gather_heads(heads, turned)
    half = weight.shape[0] // 2
    for other, ref in enumerate(halves):
        weight[pl.ds(pl.multiple_of(((place_in_group() & 1) ^ other) * half, 32), half), :] = ref[...]
    out_ref[0] = jnp.dot(turned[...].T, weight[...], preferred_element_type=jnp.float32).astype(out_ref.dtype)


def project_near_kernel(*refs):
    each = len(FLIPS)
    heads, own_ref, pieces, thirds = refs[:each], refs[each], refs[each + 1 : each + 5], refs[each + 5 : each + 8]
    blocks_ref, sum_ref, rest_ref, turned, weight, third = refs[each + 8 :]
    gather_heads(heads, turned)
    attention = turned[...].T
    place = place_in_group()
    core, parity = place & 1, parity_of(place)
    half = pieces[0].shape[0]
    for flip in (1, 2):
        mine = core == 2 - flip
        for other in range(2):
            here = pl.ds(pl.multiple_of((parity ^ other) * half, 32), half)
            weight[flip - 1, here, :] = jnp.where(mine, pieces[other][...], pieces[2 + other][...])
    for flip, block in enumerate((own_ref[...], weight[0], weight[1])):
        blocks_ref[flip] = jnp.dot(attention, block, preferred_element_type=jnp.float32).astype(blocks_ref.dtype)

    part, quarter = thirds[0].shape[0], half // 2
    for other in range(2):
        third[pl.ds(pl.multiple_of((core ^ other) * (half - part), 16), part), :] = thirds[other][...]
    fitting = turned[pl.ds(pl.multiple_of(parity * half, 32), half), :].T
    total = jnp.dot(fitting, third[...], preferred_element_type=jnp.float32)
    for other in range(2):
        first = (1 - parity) * half + (core ^ other) * quarter
        fitting = turned[pl.ds(pl.multiple_of(first, 32), quarter), :].T
        if other:
            rest_ref[...] = fitting
        else:
            rows = thirds[2][pl.ds(pl.multiple_of(core * (part - quarter), 16), quarter), :]
            total = total + jnp.dot(fitting, rows, preferred_element_type=jnp.float32)
    sum_ref[...] = total


def project_third_kernel(blocks_ref, sum_ref, rest_ref, part_ref, out_ref, last, sems):
    shard = lax.axis_index("fsdp")
    quarter, columns = rest_ref.shape[1], last.shape[1]

    def copy_out(flip, block_ref):
        here = pl.ds(pl.multiple_of((shard ^ flip) * columns, 128), columns)
        copy = pltpu.make_async_copy(block_ref, out_ref.at[0, :, here], sems.at[flip])
        copy.start()
        return copy

    copies = [copy_out(flip, blocks_ref.at[flip]) for flip in range(3)]
    first = (1 - (place_in_group() & 1)) * (part_ref.shape[0] - quarter)
    rows = part_ref[pl.ds(pl.multiple_of(first, 16), quarter), :]
    total = sum_ref[...] + jnp.dot(rest_ref[...], rows, preferred_element_type=jnp.float32)
    last[...] = total.astype(last.dtype)
    copies.append(copy_out(3, last))
    for copy in copies:
        copy.wait()


def projection_cost(frames, features, columns):
    return pl.CostEstimate(
        flops=2 * features * frames * columns, bytes_accessed=2 * features * columns, transcendentals=0
    )


def project(heads, halves):
    rows, frames = heads[0].shape
    features, width = len(FLIPS) * rows, halves[0].shape[1]
    return pl.pallas_call(
        project_kernel,
        out_shape=jax.ShapeDtypeStruct((1, frames, width), jnp.bfloat16),
        in_specs=[WHOLE] * (len(FLIPS) + 2),
        out_specs=WHOLE,
        scratch_shapes=[pltpu.VMEM((features, frames), jnp.bfloat16), pltpu.VMEM((features, width), jnp.bfloat16)],
        compiler_params=params(24),
        cost_estimate=projection_cost(frames, features, width),
        name="project_heads",
    )(*heads, *halves)


def project_near(heads, own, pieces, thirds):
    frames = heads[0].shape[1]
    features, columns = own.shape
    return pl.pallas_call(
        project_near_kernel,
        out_shape=[
            pltpu.VMEM((3, frames, columns), jnp.bfloat16),
            pltpu.VMEM((frames, columns), jnp.float32),
            pltpu.VMEM((frames, features // 4), jnp.bfloat16),
        ],
        in_specs=[WHOLE] * (len(FLIPS) + 8),
        out_specs=[WHOLE] * 3,
        scratch_shapes=[
            pltpu.VMEM((features, frames), jnp.bfloat16),
            pltpu.VMEM((2, features, columns), jnp.bfloat16),
            pltpu.VMEM((features // 2, columns), jnp.bfloat16),
        ],
        compiler_params=params(24),
        cost_estimate=projection_cost(frames, features, 3 * columns),
        name="project_near_shards",
    )(*heads, own, *pieces, *thirds)


def project_third(blocks, so_far, rest, part):
    _, frames, columns = blocks.shape
    return pl.pallas_call(
        project_third_kernel,
        out_shape=jax.ShapeDtypeStruct((1, frames, 4 * columns), blocks.dtype),
        in_specs=[WHOLE] * 4,
        out_specs=IN_HBM,
        scratch_shapes=[pltpu.VMEM((frames, columns), jnp.bfloat16), pltpu.SemaphoreType.DMA((4,))],
        compiler_params=params(24),
        cost_estimate=projection_cost(frames, rest.shape[1], columns),
        name="project_third_shard",
    )(blocks, so_far, rest, part)


def per_device(ctx, fsdp, queries, key_rows, value_rows, lengths, out_weight):
    def exchange(array, axis, flip):
        size = ctx if axis == "ctx" else fsdp
        return lax.ppermute(array, axis, [(i, i ^ flip) for i in range(size)])

    def exchange_chips(arrays):
        return [exchange(array, "ctx", flip) for flip, array in zip(FLIPS[1:], arrays)]

    def exchange_in_plane(array):
        return lax.ppermute(array, "ctx", [(i, i ^ (4 if i % 2 else 2)) for i in range(ctx)])

    def exchange_along(array, *flips):
        pairs = [(i * fsdp + z, i * fsdp + (z ^ flips[i % 2])) for i in range(ctx) for z in range(fsdp)]
        return lax.ppermute(array, ("ctx", "fsdp"), pairs)

    core = place_in_group() & 1
    split_columns = fsdp == 4
    lengths = jnp.broadcast_to(lengths, (8, 128))
    rows, half = copy_in(queries, key_rows, value_rows, out_weight, split_columns)
    if split_columns:
        fetched = exchange_along(half, 2, 1)
    else:
        half = lax.all_gather(half, "fsdp", axis=1, tiled=True)

    own, *by_chip = turn(rows)
    same = exchange_chips(by_chip)
    own_other = exchange(own[1:], "ctx", 1)
    if split_columns:
        fetched, own_other, lengths = lax.optimization_barrier((fetched, own_other, lengths))
        passed = exchange_in_plane(fetched)
        depth = half.shape[0]
        part = depth // 2 + 16
        third = lax.dynamic_slice_in_dim(fetched, core * (depth - part), part, 0)
        third = exchange_along(third, 1, 2)
    same, own_other = lax.optimization_barrier((same, own_other))
    other = exchange(stack_keys_and_values(same), "ctx", 1)
    same = [own, *same]

    groups = ctx // HEADS
    rest = None
    if groups > 1:
        pairs = [own[1:], own_other]
        for at, array in enumerate(same[1:]):
            pairs += [array[1:], other[at]]
        across = [[head + first for first in range(0, ctx, HEADS)] for head in range(HEADS)]
        rest = lax.all_gather(jnp.stack(pairs), "ctx", axis=0, axis_index_groups=across, tiled=True)
    mixed = attend(lengths, same, own_other, other, rest, groups)

    heads = [mixed[0], *exchange_chips(mixed[1:])]
    if not split_columns:
        return project(heads, [half, exchange(half, "ctx", 1)])
    third_passed = exchange_in_plane(third)
    heads[3], fetched, third = lax.optimization_barrier((heads[3], fetched, third))
    heads[1], heads[2], passed = lax.optimization_barrier((heads[1], heads[2], passed))
    fetched_other, passed_other, third_other, third_passed_other = (
        exchange(array, "ctx", 1) for array in (fetched, passed, third, third_passed)
    )
    third_other, passed_other = lax.optimization_barrier((third_other, passed_other))
    near = [fetched, passed, fetched_other, passed_other]
    blocks, so_far, rest = project_near(heads, out_weight, near, [third, third_other, third_passed])
    return project_third(blocks, so_far, rest, third_passed_other)


def solution(mesh):
    return jax.shard_map(
        functools.partial(per_device, mesh.shape["ctx"], mesh.shape["fsdp"]),
        mesh=mesh,
        in_specs=(
            P("fsdp", "ctx", None),
            P("fsdp", "ctx", None),
            P("fsdp", "ctx", None),
            P("fsdp"),
            P(None, "fsdp"),
        ),
        out_specs=P("fsdp", "ctx", None),
        check_vma=False,
    )
```

```python
import functools
import math

import jax
import jax.numpy as jnp
from jax import lax
from jax.experimental import pallas as pl
from jax.experimental.pallas import tpu as pltpu
from jax.sharding import PartitionSpec as P

HEADS = 8
FLIPS = tuple(range(0, HEADS, 2))
WHOLE = pl.BlockSpec(memory_space=pltpu.VMEM)
IN_HBM = pl.BlockSpec(memory_space=pltpu.HBM)


def params(mebibytes=48):
    return pltpu.CompilerParams(vmem_limit_bytes=mebibytes * 1024 * 1024)


def place_in_group():
    return lax.axis_index("ctx") % HEADS


def parity_of(place):
    return ((place >> 2) ^ (place >> 1)) & 1


def copy_in_kernel(by_parity, query_ref, key_ref, value_ref, weight_ref, rows_ref, half_ref, sems):
    place = place_in_group()
    first = (parity_of(place) if by_parity else place & 1) * half_ref.shape[0]
    copies = [pltpu.make_async_copy(weight_ref.at[pl.ds(pl.multiple_of(first, 32), half_ref.shape[0])], half_ref, sems.at[3])]
    for part, ref in enumerate((query_ref, key_ref, value_ref)):
        copies.append(pltpu.make_async_copy(ref.at[0], rows_ref.at[part], sems.at[part]))
    for copy in copies:
        copy.start()
    for copy in copies:
        copy.wait()


def copy_in(queries, key_rows, value_rows, out_weight, by_parity):
    _, frames, features = queries.shape
    half = (out_weight.shape[0] // 2, out_weight.shape[1])
    arrays = [pltpu.with_memory_space_constraint(array, pltpu.HBM) for array in (queries, key_rows, value_rows, out_weight)]
    return pl.pallas_call(
        functools.partial(copy_in_kernel, by_parity),
        out_shape=[pltpu.VMEM((3, frames, features), queries.dtype), pltpu.VMEM(half, out_weight.dtype)],
        in_specs=[IN_HBM] * 4,
        out_specs=[WHOLE] * 2,
        scratch_shapes=[pltpu.SemaphoreType.DMA((4,))],
        compiler_params=params(16),
        name="copy_in",
    )(*arrays)


def turn_kernel(rows_ref, *refs):
    outs, turned = refs[:-1], refs[-1]
    features = outs[0].shape[1]
    chip = place_in_group() >> 1
    for part in range(3):
        turned[part] = rows_ref[part].T
        for flip, out_ref in zip(FLIPS, outs):
            first = pl.multiple_of((chip ^ (flip >> 1)) * features, 32)
            out_ref[part] = turned[part, pl.ds(first, features), :]


def turn(rows):
    _, frames, features = rows.shape
    return pl.pallas_call(
        turn_kernel,
        out_shape=[pltpu.VMEM((3, features // len(FLIPS), frames), rows.dtype)] * len(FLIPS),
        in_specs=[WHOLE],
        out_specs=[WHOLE] * len(FLIPS),
        scratch_shapes=[pltpu.VMEM((3, features, frames), rows.dtype)],
        compiler_params=params(16),
        name="turn_heads",
    )(rows)


def attention_kernel(groups, lengths_ref, *refs):
    each = len(FLIPS)
    same, own_other, other = refs[:each], refs[each], refs[each + 1 : each + 3]
    rest_ref = refs[each + 3] if groups > 1 else None
    outs, (keys, values) = refs[-2 - each : -2], refs[-2:]
    block = outs[0].shape[1]
    head_size = outs[0].shape[0] // 2
    place = place_in_group()
    scale = jnp.float32(math.log2(math.e) / math.sqrt(head_size))
    pad = keys.shape[2] - head_size

    def piece(at, head, part):
        rows = slice(head * head_size, (head + 1) * head_size)
        if groups > 1:
            return rest_ref[at, part - 1, rows, :]
        if at % 2 == 0:
            return same[at // 2][part, rows, :]
        return other[part - 1][at // 2 - 1, rows, :] if at > 1 else own_other[part - 1, rows, :]

    ones = jnp.where(lax.broadcasted_iota(jnp.int32, (pad, block), 0) == 0, 1.0, 0.0).astype(keys.dtype)
    at_feature = lax.broadcasted_iota(jnp.int32, (pad, block), 0)
    at_frame = lax.broadcasted_iota(jnp.int32, (pad, block), 1)

    def prepare(head):
        for at in range(groups * HEADS):
            here = slice(at * block, (at + 1) * block)
            frame = (at // HEADS * HEADS + (place ^ (at % HEADS))) * block + at_frame
            bias = jnp.where((at_feature == 0) & (frame >= lengths_ref[:1, :]), -1e30, 0.0).astype(keys.dtype)
            keys[head, here, :] = jnp.concatenate([piece(at, head, 1), bias], axis=0).T
            values[head, :, here] = jnp.concatenate([piece(at, head, 2), ones], axis=0)

    def score(head, flips):
        rows = slice(head * head_size, (head + 1) * head_size)
        query = jnp.concatenate([jnp.concatenate([same[flip // 2][0, rows, :], ones], axis=0) for flip in flips], axis=1)
        return [jnp.dot(keys[head, part, :], query, preferred_element_type=jnp.float32) for part in parts]

    parts = [slice(first, first + keys.shape[1] // 4) for first in range(0, keys.shape[1], keys.shape[1] // 4)]
    chunks = [(head, flips) for head in range(2) for flips in (FLIPS[:2], FLIPS[2:])]
    prepare(0)
    later = score(*chunks[0])
    prepare(1)
    for at, (head, flips) in enumerate(chunks):
        scores = later
        if at + 1 < len(chunks):
            later = score(*chunks[at + 1])
        row_max = functools.reduce(jnp.maximum, (jnp.max(part, axis=0, keepdims=True) for part in scores)) * scale
        mixed = jnp.zeros((values.shape[1], scores[0].shape[1]), jnp.float32)
        for part, part_scores in zip(parts, scores):
            probs = jnp.exp2(part_scores * scale - row_max).astype(jnp.bfloat16)
            mixed = mixed + jnp.dot(values[head, :, part], probs, preferred_element_type=jnp.float32)
        mixed = (mixed[:head_size] / mixed[head_size : head_size + 1]).astype(jnp.bfloat16)
        for half, flip in enumerate(flips):
            outs[flip // 2][head * head_size : (head + 1) * head_size, :] = mixed[:, half * block : (half + 1) * block]


def stack_kernel(*refs):
    for part in range(2):
        for at, ref in enumerate(refs[:-2]):
            refs[part - 2][at] = ref[1 + part]


def stack_keys_and_values(arrays):
    parts, features, frames = arrays[0].shape
    return pl.pallas_call(
        stack_kernel,
        out_shape=[pltpu.VMEM((len(arrays), features, frames), arrays[0].dtype)] * (parts - 1),
        in_specs=[WHOLE] * len(arrays),
        out_specs=[WHOLE] * (parts - 1),
        compiler_params=params(16),
        name="stack_keys_and_values",
    )(*arrays)


def attend(lengths, same, own_other, other, rest, groups):
    _, features, block = same[0].shape
    keys = groups * HEADS * block
    padded = features // 2 + 32
    rest = [] if rest is None else [rest]
    return pl.pallas_call(
        functools.partial(attention_kernel, groups),
        out_shape=[pltpu.VMEM((features, block), jnp.bfloat16)] * len(FLIPS),
        in_specs=[WHOLE] * (4 + len(FLIPS) + len(rest)),
        out_specs=[WHOLE] * len(FLIPS),
        scratch_shapes=[pltpu.VMEM((2, keys, padded), jnp.bfloat16), pltpu.VMEM((2, padded, keys), jnp.bfloat16)],
        compiler_params=params(32),
        cost_estimate=pl.CostEstimate(flops=0 * keys * keys * features, bytes_accessed=0, transcendentals=0),
        name="attend_two_heads",
    )(lengths, *same, own_other, *other, *rest)


def gather_heads(heads, turned):
    rows = heads[0].shape[0]
    for flip, ref in zip(FLIPS, heads):
        first = pl.multiple_of(((place_in_group() ^ flip) >> 1) * rows, 32)
        turned[pl.ds(first, rows), :] = ref[...]


def project_kernel(*refs):
    each = len(FLIPS)
    heads, halves, (out_ref, turned, weight) = refs[:each], refs[each : each + 2], refs[each + 2 :]
    gather_heads(heads, turned)
    half = weight.shape[0] // 2
    for other, ref in enumerate(halves):
        weight[pl.ds(pl.multiple_of(((place_in_group() & 1) ^ other) * half, 32), half), :] = ref[...]
    out_ref[0] = jnp.dot(turned[...].T, weight[...], preferred_element_type=jnp.float32).astype(out_ref.dtype)


def project_near_kernel(*refs):
    each = len(FLIPS)
    heads, own_ref, pieces, thirds = refs[:each], refs[each], refs[each + 1 : each + 5], refs[each + 5 : each + 8]
    blocks_ref, sum_ref, rest_ref, turned, weight, third = refs[each + 8 :]
    gather_heads(heads, turned)
    attention = turned[...].T
    place = place_in_group()
    core, parity = place & 1, parity_of(place)
    half = pieces[0].shape[0]
    for flip in (1, 2):
        mine = core == 2 - flip
        for other in range(2):
            here = pl.ds(pl.multiple_of((parity ^ other) * half, 32), half)
            weight[flip - 1, here, :] = jnp.where(mine, pieces[other][...], pieces[2 + other][...])
    for flip, block in enumerate((own_ref[...], weight[0], weight[1])):
        blocks_ref[flip] = jnp.dot(attention, block, preferred_element_type=jnp.float32).astype(blocks_ref.dtype)

    part, quarter = thirds[0].shape[0], half // 2
    for other in range(2):
        third[pl.ds(pl.multiple_of((core ^ other) * (half - part), 16), part), :] = thirds[other][...]
    fitting = turned[pl.ds(pl.multiple_of(parity * half, 32), half), :].T
    total = jnp.dot(fitting, third[...], preferred_element_type=jnp.float32)
    for other in range(2):
        first = (1 - parity) * half + (core ^ other) * quarter
        fitting = turned[pl.ds(pl.multiple_of(first, 32), quarter), :].T
        if other:
            rest_ref[...] = fitting
        else:
            rows = thirds[2][pl.ds(pl.multiple_of(core * (part - quarter), 16), quarter), :]
            total = total + jnp.dot(fitting, rows, preferred_element_type=jnp.float32)
    sum_ref[...] = total


def project_third_kernel(blocks_ref, sum_ref, rest_ref, part_ref, out_ref, last, sems):
    shard = lax.axis_index("fsdp")
    quarter, columns = rest_ref.shape[1], last.shape[1]

    def copy_out(flip, block_ref):
        here = pl.ds(pl.multiple_of((shard ^ flip) * columns, 128), columns)
        copy = pltpu.make_async_copy(block_ref, out_ref.at[0, :, here], sems.at[flip])
        copy.start()
        return copy

    copies = [copy_out(flip, blocks_ref.at[flip]) for flip in range(3)]
    first = (1 - (place_in_group() & 1)) * (part_ref.shape[0] - quarter)
    rows = part_ref[pl.ds(pl.multiple_of(first, 16), quarter), :]
    total = sum_ref[...] + jnp.dot(rest_ref[...], rows, preferred_element_type=jnp.float32)
    last[...] = total.astype(last.dtype)
    copies.append(copy_out(3, last))
    for copy in copies:
        copy.wait()


def projection_cost(frames, features, columns):
    return pl.CostEstimate(
        flops=2 * features * frames * columns, bytes_accessed=2 * features * columns, transcendentals=0
    )


def project(heads, halves):
    rows, frames = heads[0].shape
    features, width = len(FLIPS) * rows, halves[0].shape[1]
    return pl.pallas_call(
        project_kernel,
        out_shape=jax.ShapeDtypeStruct((1, frames, width), jnp.bfloat16),
        in_specs=[WHOLE] * (len(FLIPS) + 2),
        out_specs=WHOLE,
        scratch_shapes=[pltpu.VMEM((features, frames), jnp.bfloat16), pltpu.VMEM((features, width), jnp.bfloat16)],
        compiler_params=params(24),
        cost_estimate=projection_cost(frames, features, width),
        name="project_heads",
    )(*heads, *halves)


def project_near(heads, own, pieces, thirds):
    frames = heads[0].shape[1]
    features, columns = own.shape
    return pl.pallas_call(
        project_near_kernel,
        out_shape=[
            pltpu.VMEM((3, frames, columns), jnp.bfloat16),
            pltpu.VMEM((frames, columns), jnp.float32),
            pltpu.VMEM((frames, features // 4), jnp.bfloat16),
        ],
        in_specs=[WHOLE] * (len(FLIPS) + 8),
        out_specs=[WHOLE] * 3,
        scratch_shapes=[
            pltpu.VMEM((features, frames), jnp.bfloat16),
            pltpu.VMEM((2, features, columns), jnp.bfloat16),
            pltpu.VMEM((features // 2, columns), jnp.bfloat16),
        ],
        compiler_params=params(24),
        cost_estimate=projection_cost(frames, features, 3 * columns),
        name="project_near_shards",
    )(*heads, own, *pieces, *thirds)


def project_third(blocks, so_far, rest, part):
    _, frames, columns = blocks.shape
    return pl.pallas_call(
        project_third_kernel,
        out_shape=jax.ShapeDtypeStruct((1, frames, 4 * columns), blocks.dtype),
        in_specs=[WHOLE] * 4,
        out_specs=IN_HBM,
        scratch_shapes=[pltpu.VMEM((frames, columns), jnp.bfloat16), pltpu.SemaphoreType.DMA((4,))],
        compiler_params=params(24),
        cost_estimate=projection_cost(frames, rest.shape[1], columns),
        name="project_third_shard",
    )(blocks, so_far, rest, part)


def per_device(ctx, fsdp, queries, key_rows, value_rows, lengths, out_weight):
    def exchange(array, axis, flip):
        size = ctx if axis == "ctx" else fsdp
        return lax.ppermute(array, axis, [(i, i ^ flip) for i in range(size)])

    def exchange_chips(arrays):
        return [exchange(array, "ctx", flip) for flip, array in zip(FLIPS[1:], arrays)]

    def exchange_in_plane(array):
        return lax.ppermute(array, "ctx", [(i, i ^ (4 if i % 2 else 2)) for i in range(ctx)])

    def exchange_along(array, *flips):
        pairs = [(i * fsdp + z, i * fsdp + (z ^ flips[i % 2])) for i in range(ctx) for z in range(fsdp)]
        return lax.ppermute(array, ("ctx", "fsdp"), pairs)

    core = place_in_group() & 1
    split_columns = fsdp == 4
    lengths = jnp.broadcast_to(lengths, (8, 128))
    rows, half = copy_in(queries, key_rows, value_rows, out_weight, split_columns)
    if split_columns:
        fetched = exchange_along(half, 2, 1)
    else:
        half = lax.all_gather(half, "fsdp", axis=1, tiled=True)

    own, *by_chip = turn(rows)
    same = exchange_chips(by_chip)
    own_other = exchange(own[1:], "ctx", 1)
    if split_columns:
        fetched, own_other, lengths = lax.optimization_barrier((fetched, own_other, lengths))
        passed = exchange_in_plane(fetched)
        depth = half.shape[0]
        part = depth // 2 + 32
        third = lax.dynamic_slice_in_dim(fetched, core * (depth - part), part, 0)
        third = exchange_along(third, 1, 2)
    same, own_other = lax.optimization_barrier((same, own_other))
    other = [exchange(array, "ctx", 1) for array in stack_keys_and_values(same)]
    same = [own, *same]

    groups = ctx // HEADS
    rest = None
    if groups > 1:
        pairs = [own[1:], own_other]
        for at, array in enumerate(same[1:]):
            pairs += [array[1:], jnp.stack([other[0][at], other[1][at]])]
        across = [[head + first for first in range(0, ctx, HEADS)] for head in range(HEADS)]
        rest = lax.all_gather(jnp.stack(pairs), "ctx", axis=0, axis_index_groups=across, tiled=True)
    mixed = attend(lengths, same, own_other, other, rest, groups)

    heads = [mixed[0], *exchange_chips(mixed[1:])]
    if not split_columns:
        return project(heads, [half, exchange(half, "ctx", 1)])
    third_passed = exchange_in_plane(third)
    heads[3], fetched, third = lax.optimization_barrier((heads[3], fetched, third))
    heads[1], heads[2], passed = lax.optimization_barrier((heads[1], heads[2], passed))
    fetched_other, passed_other, third_other, third_passed_other = (
        exchange(array, "ctx", 1) for array in (fetched, passed, third, third_passed)
    )
    third_other, passed_other = lax.optimization_barrier((third_other, passed_other))
    near = [fetched, passed, fetched_other, passed_other]
    blocks, so_far, rest = project_near(heads, out_weight, near, [third, third_other, third_passed])
    return project_third(blocks, so_far, rest, third_passed_other)


def solution(mesh):
    return jax.shard_map(
        functools.partial(per_device, mesh.shape["ctx"], mesh.shape["fsdp"]),
        mesh=mesh,
        in_specs=(
            P("fsdp", "ctx", None),
            P("fsdp", "ctx", None),
            P("fsdp", "ctx", None),
            P("fsdp"),
            P(None, "fsdp"),
        ),
        out_specs=P("fsdp", "ctx", None),
        check_vma=False,
    )
```

```python
import functools
import math

import jax
import jax.numpy as jnp
from jax import lax
from jax.experimental import pallas as pl
from jax.experimental.pallas import tpu as pltpu
from jax.sharding import PartitionSpec as P

HEADS = 8
FLIPS = tuple(range(0, HEADS, 2))
WHOLE = pl.BlockSpec(memory_space=pltpu.VMEM)
IN_HBM = pl.BlockSpec(memory_space=pltpu.HBM)


def params(mebibytes=48):
    return pltpu.CompilerParams(vmem_limit_bytes=mebibytes * 1024 * 1024)


def place_in_group():
    return lax.axis_index("ctx") % HEADS


def parity_of(place):
    return ((place >> 2) ^ (place >> 1)) & 1


def copy_in_kernel(by_parity, query_ref, key_ref, value_ref, weight_ref, rows_ref, half_ref, sems):
    place = place_in_group()
    first = (parity_of(place) if by_parity else place & 1) * half_ref.shape[0]
    copies = [pltpu.make_async_copy(weight_ref.at[pl.ds(pl.multiple_of(first, 32), half_ref.shape[0])], half_ref, sems.at[3])]
    for part, ref in enumerate((query_ref, key_ref, value_ref)):
        copies.append(pltpu.make_async_copy(ref.at[0], rows_ref.at[part], sems.at[part]))
    for copy in copies:
        copy.start()
    for copy in copies:
        copy.wait()


def copy_in(queries, key_rows, value_rows, out_weight, by_parity):
    _, frames, features = queries.shape
    half = (out_weight.shape[0] // 2, out_weight.shape[1])
    arrays = [pltpu.with_memory_space_constraint(array, pltpu.HBM) for array in (queries, key_rows, value_rows, out_weight)]
    return pl.pallas_call(
        functools.partial(copy_in_kernel, by_parity),
        out_shape=[pltpu.VMEM((3, frames, features), queries.dtype), pltpu.VMEM(half, out_weight.dtype)],
        in_specs=[IN_HBM] * 4,
        out_specs=[WHOLE] * 2,
        scratch_shapes=[pltpu.SemaphoreType.DMA((4,))],
        compiler_params=params(16),
        name="copy_in",
    )(*arrays)


def turn_kernel(rows_ref, *refs):
    outs, turned = refs[:-1], refs[-1]
    features = outs[0].shape[1]
    chip = place_in_group() >> 1
    for part in range(3):
        turned[part] = rows_ref[part].T
        for flip, out_ref in zip(FLIPS, outs):
            first = pl.multiple_of((chip ^ (flip >> 1)) * features, 32)
            out_ref[part] = turned[part, pl.ds(first, features), :]


def turn(rows):
    _, frames, features = rows.shape
    return pl.pallas_call(
        turn_kernel,
        out_shape=[pltpu.VMEM((3, features // len(FLIPS), frames), rows.dtype)] * len(FLIPS),
        in_specs=[WHOLE],
        out_specs=[WHOLE] * len(FLIPS),
        scratch_shapes=[pltpu.VMEM((3, features, frames), rows.dtype)],
        compiler_params=params(16),
        name="turn_heads",
    )(rows)


def attention_kernel(groups, lengths_ref, *refs):
    each = len(FLIPS)
    same, own_other, other = refs[:each], refs[each], refs[each + 1]
    rest_ref = refs[each + 2] if groups > 1 else None
    outs, (keys, values) = refs[-2 - each : -2], refs[-2:]
    block = outs[0].shape[1]
    head_size = outs[0].shape[0] // 2
    place = place_in_group()
    scale = jnp.float32(math.log2(math.e) / math.sqrt(head_size))
    pad = keys.shape[2] - head_size

    def piece(at, head, part):
        rows = slice(head * head_size, (head + 1) * head_size)
        if groups > 1:
            return rest_ref[at, part - 1, rows, :]
        if at % 2 == 0:
            return same[at // 2][part, rows, :]
        return other[at // 2 - 1, part - 1, rows, :] if at > 1 else own_other[part - 1, rows, :]

    ones = jnp.where(lax.broadcasted_iota(jnp.int32, (pad, block), 0) == 0, 1.0, 0.0).astype(keys.dtype)
    at_feature = lax.broadcasted_iota(jnp.int32, (pad, block), 0)
    at_frame = lax.broadcasted_iota(jnp.int32, (pad, block), 1)

    def prepare(head, pieces):
        for at in pieces:
            here = slice(at * block, (at + 1) * block)
            frame = (at // HEADS * HEADS + (place ^ (at % HEADS))) * block + at_frame
            bias = jnp.where((at_feature == 0) & (frame >= lengths_ref[:1, :]), -1e30, 0.0).astype(keys.dtype)
            keys[head, here, :] = jnp.concatenate([piece(at, head, 1), bias], axis=0).T
            values[head, :, here] = jnp.concatenate([piece(at, head, 2), ones], axis=0)

    def score(head, flips):
        rows = slice(head * head_size, (head + 1) * head_size)
        query = jnp.concatenate([jnp.concatenate([same[flip // 2][0, rows, :], ones], axis=0) for flip in flips], axis=1)
        scores = []
        for part in parts:
            if flips == FLIPS[:2]:
                prepare(head, range(part.start // block, part.stop // block))
            scores.append(jnp.dot(keys[head, part, :], query, preferred_element_type=jnp.float32))
        return scores

    parts = [slice(first, first + keys.shape[1] // 4) for first in range(0, keys.shape[1], keys.shape[1] // 4)]
    chunks = [(head, flips) for head in range(2) for flips in (FLIPS[:2], FLIPS[2:])]
    later = score(*chunks[0])
    for at, (head, flips) in enumerate(chunks):
        scores = later
        if at + 1 < len(chunks):
            later = score(*chunks[at + 1])
        row_max = functools.reduce(jnp.maximum, (jnp.max(part, axis=0, keepdims=True) for part in scores)) * scale
        mixed = jnp.zeros((values.shape[1], scores[0].shape[1]), jnp.float32)
        for part, part_scores in zip(parts, scores):
            probs = jnp.exp2(part_scores * scale - row_max).astype(jnp.bfloat16)
            mixed = mixed + jnp.dot(values[head, :, part], probs, preferred_element_type=jnp.float32)
        mixed = (mixed[:head_size] / mixed[head_size : head_size + 1]).astype(jnp.bfloat16)
        for half, flip in enumerate(flips):
            outs[flip // 2][head * head_size : (head + 1) * head_size, :] = mixed[:, half * block : (half + 1) * block]


def stack_kernel(*refs):
    for at, ref in enumerate(refs[:-1]):
        refs[-1][at] = ref[1:]


def stack_keys_and_values(arrays):
    parts, features, frames = arrays[0].shape
    return pl.pallas_call(
        stack_kernel,
        out_shape=pltpu.VMEM((len(arrays), parts - 1, features, frames), arrays[0].dtype),
        in_specs=[WHOLE] * len(arrays),
        out_specs=WHOLE,
        compiler_params=params(16),
        name="stack_keys_and_values",
    )(*arrays)


def attend(lengths, same, own_other, other, rest, groups):
    _, features, block = same[0].shape
    keys = groups * HEADS * block
    padded = features // 2 + 32
    rest = [] if rest is None else [rest]
    return pl.pallas_call(
        functools.partial(attention_kernel, groups),
        out_shape=[pltpu.VMEM((features, block), jnp.bfloat16)] * len(FLIPS),
        in_specs=[WHOLE] * (3 + len(FLIPS) + len(rest)),
        out_specs=[WHOLE] * len(FLIPS),
        scratch_shapes=[pltpu.VMEM((2, keys, padded), jnp.bfloat16), pltpu.VMEM((2, padded, keys), jnp.bfloat16)],
        compiler_params=params(32),
        cost_estimate=pl.CostEstimate(flops=8 * keys * keys * features, bytes_accessed=0, transcendentals=0),
        name="attend_two_heads",
    )(lengths, *same, own_other, other, *rest)


def gather_heads(heads, turned):
    rows = heads[0].shape[0]
    for flip, ref in zip(FLIPS, heads):
        first = pl.multiple_of(((place_in_group() ^ flip) >> 1) * rows, 32)
        turned[pl.ds(first, rows), :] = ref[...]


def project_kernel(*refs):
    each = len(FLIPS)
    heads, halves, (out_ref, turned, weight) = refs[:each], refs[each : each + 2], refs[each + 2 :]
    gather_heads(heads, turned)
    half = weight.shape[0] // 2
    for other, ref in enumerate(halves):
        weight[pl.ds(pl.multiple_of(((place_in_group() & 1) ^ other) * half, 32), half), :] = ref[...]
    out_ref[0] = jnp.dot(turned[...].T, weight[...], preferred_element_type=jnp.float32).astype(out_ref.dtype)


def project_near_kernel(*refs):
    each = len(FLIPS)
    heads, own_ref, pieces, thirds = refs[:each], refs[each], refs[each + 1 : each + 5], refs[each + 5 : each + 8]
    blocks_ref, sum_ref, rest_ref, turned, weight, third = refs[each + 8 :]
    gather_heads(heads, turned)
    attention = turned[...].T
    place = place_in_group()
    core, parity = place & 1, parity_of(place)
    half = pieces[0].shape[0]
    for flip in (1, 2):
        mine = core == 2 - flip
        for other in range(2):
            here = pl.ds(pl.multiple_of((parity ^ other) * half, 32), half)
            weight[flip - 1, here, :] = jnp.where(mine, pieces[other][...], pieces[2 + other][...])
    for flip, block in enumerate((own_ref[...], weight[0], weight[1])):
        blocks_ref[flip] = jnp.dot(attention, block, preferred_element_type=jnp.float32).astype(blocks_ref.dtype)

    part, quarter = thirds[0].shape[0], half // 2
    for other in range(2):
        third[pl.ds(pl.multiple_of((core ^ other) * (half - part), 16), part), :] = thirds[other][...]
    fitting = turned[pl.ds(pl.multiple_of(parity * half, 32), half), :].T
    total = jnp.dot(fitting, third[...], preferred_element_type=jnp.float32)
    for other in range(2):
        first = (1 - parity) * half + (core ^ other) * quarter
        fitting = turned[pl.ds(pl.multiple_of(first, 32), quarter), :].T
        if other:
            rest_ref[...] = fitting
        else:
            rows = thirds[2][pl.ds(pl.multiple_of(core * (part - quarter), 16), quarter), :]
            total = total + jnp.dot(fitting, rows, preferred_element_type=jnp.float32)
    sum_ref[...] = total


def project_third_kernel(blocks_ref, sum_ref, rest_ref, part_ref, out_ref, last, sems):
    shard = lax.axis_index("fsdp")
    quarter, columns = rest_ref.shape[1], last.shape[1]

    def copy_out(flip, block_ref):
        here = pl.ds(pl.multiple_of((shard ^ flip) * columns, 128), columns)
        copy = pltpu.make_async_copy(block_ref, out_ref.at[0, :, here], sems.at[flip])
        copy.start()
        return copy

    copies = [copy_out(flip, blocks_ref.at[flip]) for flip in range(3)]
    first = (1 - (place_in_group() & 1)) * (part_ref.shape[0] - quarter)
    rows = part_ref[pl.ds(pl.multiple_of(first, 16), quarter), :]
    total = sum_ref[...] + jnp.dot(rest_ref[...], rows, preferred_element_type=jnp.float32)
    last[...] = total.astype(last.dtype)
    copies.append(copy_out(3, last))
    for copy in copies:
        copy.wait()


def projection_cost(frames, features, columns):
    return pl.CostEstimate(
        flops=2 * features * frames * columns, bytes_accessed=2 * features * columns, transcendentals=0
    )


def project(heads, halves):
    rows, frames = heads[0].shape
    features, width = len(FLIPS) * rows, halves[0].shape[1]
    return pl.pallas_call(
        project_kernel,
        out_shape=jax.ShapeDtypeStruct((1, frames, width), jnp.bfloat16),
        in_specs=[WHOLE] * (len(FLIPS) + 2),
        out_specs=WHOLE,
        scratch_shapes=[pltpu.VMEM((features, frames), jnp.bfloat16), pltpu.VMEM((features, width), jnp.bfloat16)],
        compiler_params=params(24),
        cost_estimate=projection_cost(frames, features, width),
        name="project_heads",
    )(*heads, *halves)


def project_near(heads, own, pieces, thirds):
    frames = heads[0].shape[1]
    features, columns = own.shape
    return pl.pallas_call(
        project_near_kernel,
        out_shape=[
            pltpu.VMEM((3, frames, columns), jnp.bfloat16),
            pltpu.VMEM((frames, columns), jnp.float32),
            pltpu.VMEM((frames, features // 4), jnp.bfloat16),
        ],
        in_specs=[WHOLE] * (len(FLIPS) + 8),
        out_specs=[WHOLE] * 3,
        scratch_shapes=[
            pltpu.VMEM((features, frames), jnp.bfloat16),
            pltpu.VMEM((2, features, columns), jnp.bfloat16),
            pltpu.VMEM((features // 2, columns), jnp.bfloat16),
        ],
        compiler_params=params(24),
        cost_estimate=projection_cost(frames, features, 3 * columns),
        name="project_near_shards",
    )(*heads, own, *pieces, *thirds)


def project_third(blocks, so_far, rest, part):
    _, frames, columns = blocks.shape
    return pl.pallas_call(
        project_third_kernel,
        out_shape=jax.ShapeDtypeStruct((1, frames, 4 * columns), blocks.dtype),
        in_specs=[WHOLE] * 4,
        out_specs=IN_HBM,
        scratch_shapes=[pltpu.VMEM((frames, columns), jnp.bfloat16), pltpu.SemaphoreType.DMA((4,))],
        compiler_params=params(24),
        cost_estimate=projection_cost(frames, rest.shape[1], columns),
        name="project_third_shard",
    )(blocks, so_far, rest, part)


def per_device(ctx, fsdp, queries, key_rows, value_rows, lengths, out_weight):
    def exchange(array, axis, flip):
        size = ctx if axis == "ctx" else fsdp
        return lax.ppermute(array, axis, [(i, i ^ flip) for i in range(size)])

    def exchange_chips(arrays):
        return [exchange(array, "ctx", flip) for flip, array in zip(FLIPS[1:], arrays)]

    def exchange_in_plane(array):
        return lax.ppermute(array, "ctx", [(i, i ^ (4 if i % 2 else 2)) for i in range(ctx)])

    def exchange_along(array, *flips):
        pairs = [(i * fsdp + z, i * fsdp + (z ^ flips[i % 2])) for i in range(ctx) for z in range(fsdp)]
        return lax.ppermute(array, ("ctx", "fsdp"), pairs)

    core = place_in_group() & 1
    split_columns = fsdp == 4
    lengths = jnp.broadcast_to(lengths, (8, 128))
    rows, half = copy_in(queries, key_rows, value_rows, out_weight, split_columns)
    if split_columns:
        fetched = exchange_along(half, 2, 1)
    else:
        half = lax.all_gather(half, "fsdp", axis=1, tiled=True)

    own, *by_chip = turn(rows)
    same = exchange_chips(by_chip)
    own_other = exchange(own[1:], "ctx", 1)
    if split_columns:
        fetched, own_other, lengths = lax.optimization_barrier((fetched, own_other, lengths))
        passed = exchange_in_plane(fetched)
        depth = half.shape[0]
        part = depth // 2 + 16
        third = lax.dynamic_slice_in_dim(fetched, core * (depth - part), part, 0)
        third = exchange_along(third, 1, 2)
    same, own_other = lax.optimization_barrier((same, own_other))
    other = exchange(stack_keys_and_values(same), "ctx", 1)
    same = [own, *same]

    groups = ctx // HEADS
    rest = None
    if groups > 1:
        pairs = [own[1:], own_other]
        for at, array in enumerate(same[1:]):
            pairs += [array[1:], other[at]]
        across = [[head + first for first in range(0, ctx, HEADS)] for head in range(HEADS)]
        rest = lax.all_gather(jnp.stack(pairs), "ctx", axis=0, axis_index_groups=across, tiled=True)
    mixed = attend(lengths, same, own_other, other, rest, groups)

    heads = [mixed[0], *exchange_chips(mixed[1:])]
    if not split_columns:
        return project(heads, [half, exchange(half, "ctx", 1)])
    third_passed = exchange_in_plane(third)
    heads[3], fetched = lax.optimization_barrier((heads[3], fetched))
    heads[1], heads[2], passed, third = lax.optimization_barrier((heads[1], heads[2], passed, third))
    fetched_other, passed_other, third_other, third_passed_other = (
        exchange(array, "ctx", 1) for array in (fetched, passed, third, third_passed)
    )
    third_other, passed_other = lax.optimization_barrier((third_other, passed_other))
    near = [fetched, passed, fetched_other, passed_other]
    blocks, so_far, rest = project_near(heads, out_weight, near, [third, third_other, third_passed])
    return project_third(blocks, so_far, rest, third_passed_other)


def solution(mesh):
    return jax.shard_map(
        functools.partial(per_device, mesh.shape["ctx"], mesh.shape["fsdp"]),
        mesh=mesh,
        in_specs=(
            P("fsdp", "ctx", None),
            P("fsdp", "ctx", None),
            P("fsdp", "ctx", None),
            P("fsdp"),
            P(None, "fsdp"),
        ),
        out_specs=P("fsdp", "ctx", None),
        check_vma=False,
    )
```

```python
import functools
import math

import jax
import jax.numpy as jnp
from jax import lax
from jax.experimental import pallas as pl
from jax.experimental.pallas import tpu as pltpu
from jax.sharding import PartitionSpec as P

HEADS = 8
FLIPS = tuple(range(0, HEADS, 2))
WHOLE = pl.BlockSpec(memory_space=pltpu.VMEM)
IN_HBM = pl.BlockSpec(memory_space=pltpu.HBM)


def params(mebibytes=48):
    return pltpu.CompilerParams(vmem_limit_bytes=mebibytes * 1024 * 1024)


def place_in_group():
    return lax.axis_index("ctx") % HEADS


def stage_kernel(source_ref, out_ref):
    out_ref[...] = source_ref[...]


def stage(array, flops):
    return pl.pallas_call(
        stage_kernel,
        out_shape=pltpu.VMEM(array.shape, array.dtype),
        in_specs=[WHOLE],
        out_specs=WHOLE,
        compiler_params=params(16),
        cost_estimate=pl.CostEstimate(flops=flops, bytes_accessed=0, transcendentals=0),
        name="stage_third_shard",
    )(array)


def parity_of(place):
    return ((place >> 2) ^ (place >> 1)) & 1


def copy_in_kernel(by_parity, query_ref, key_ref, value_ref, weight_ref, rows_ref, half_ref, sems):
    place = place_in_group()
    first = (parity_of(place) if by_parity else place & 1) * half_ref.shape[0]
    copies = [pltpu.make_async_copy(weight_ref.at[pl.ds(pl.multiple_of(first, 32), half_ref.shape[0])], half_ref, sems.at[3])]
    for part, ref in enumerate((query_ref, key_ref, value_ref)):
        copies.append(pltpu.make_async_copy(ref.at[0], rows_ref.at[part], sems.at[part]))
    for copy in copies:
        copy.start()
    for copy in copies:
        copy.wait()


def copy_in(queries, key_rows, value_rows, out_weight, by_parity):
    _, frames, features = queries.shape
    half = (out_weight.shape[0] // 2, out_weight.shape[1])
    arrays = [pltpu.with_memory_space_constraint(array, pltpu.HBM) for array in (queries, key_rows, value_rows, out_weight)]
    return pl.pallas_call(
        functools.partial(copy_in_kernel, by_parity),
        out_shape=[pltpu.VMEM((3, frames, features), queries.dtype), pltpu.VMEM(half, out_weight.dtype)],
        in_specs=[IN_HBM] * 4,
        out_specs=[WHOLE] * 2,
        scratch_shapes=[pltpu.SemaphoreType.DMA((4,))],
        compiler_params=params(16),
        name="copy_in",
    )(*arrays)


def turn_kernel(rows_ref, *refs):
    outs, turned = refs[:-1], refs[-1]
    features = outs[0].shape[1]
    chip = place_in_group() >> 1
    for part in range(3):
        turned[part] = rows_ref[part].T
        for flip, out_ref in zip(FLIPS, outs):
            first = pl.multiple_of((chip ^ (flip >> 1)) * features, 32)
            out_ref[part] = turned[part, pl.ds(first, features), :]


def turn(rows):
    _, frames, features = rows.shape
    return pl.pallas_call(
        turn_kernel,
        out_shape=[pltpu.VMEM((3, features // len(FLIPS), frames), rows.dtype)] * len(FLIPS),
        in_specs=[WHOLE],
        out_specs=[WHOLE] * len(FLIPS),
        scratch_shapes=[pltpu.VMEM((3, features, frames), rows.dtype)],
        compiler_params=params(16),
        name="turn_heads",
    )(rows)


def attention_kernel(groups, lengths_ref, *refs):
    each = len(FLIPS)
    same, own_other, other = refs[:each], refs[each], refs[each + 1]
    rest_ref = refs[each + 2] if groups > 1 else None
    outs, (keys, values) = refs[-2 - each : -2], refs[-2:]
    block = outs[0].shape[1]
    head_size = outs[0].shape[0] // 2
    place = place_in_group()
    scale = jnp.float32(math.log2(math.e) / math.sqrt(head_size))
    pad = keys.shape[2] - head_size

    def piece(at, head, part):
        rows = slice(head * head_size, (head + 1) * head_size)
        if groups > 1:
            return rest_ref[at, part - 1, rows, :]
        if at % 2 == 0:
            return same[at // 2][part, rows, :]
        return other[at // 2 - 1, part - 1, rows, :] if at > 1 else own_other[part - 1, rows, :]

    ones = jnp.where(lax.broadcasted_iota(jnp.int32, (pad, block), 0) == 0, 1.0, 0.0).astype(keys.dtype)
    at_feature = lax.broadcasted_iota(jnp.int32, (pad, block), 0)
    at_frame = lax.broadcasted_iota(jnp.int32, (pad, block), 1)

    def prepare(head):
        for at in range(groups * HEADS):
            here = slice(at * block, (at + 1) * block)
            frame = (at // HEADS * HEADS + (place ^ (at % HEADS))) * block + at_frame
            bias = jnp.where((at_feature == 0) & (frame >= lengths_ref[:1, :]), -1e30, 0.0).astype(keys.dtype)
            keys[head, here, :] = jnp.concatenate([piece(at, head, 1), bias], axis=0).T
            values[head, :, here] = jnp.concatenate([piece(at, head, 2), ones], axis=0)

    def score(head, flips):
        rows = slice(head * head_size, (head + 1) * head_size)
        query = jnp.concatenate([jnp.concatenate([same[flip // 2][0, rows, :], ones], axis=0) for flip in flips], axis=1)
        return [jnp.dot(keys[head, part, :], query, preferred_element_type=jnp.float32) for part in parts]

    parts = [slice(first, first + keys.shape[1] // 4) for first in range(0, keys.shape[1], keys.shape[1] // 4)]
    chunks = [(head, flips) for head in range(2) for flips in (FLIPS[:2], FLIPS[2:])]
    prepare(0)
    later = score(*chunks[0])
    prepare(1)
    for at, (head, flips) in enumerate(chunks):
        scores = later
        if at + 1 < len(chunks):
            later = score(*chunks[at + 1])
        row_max = functools.reduce(jnp.maximum, (jnp.max(part, axis=0, keepdims=True) for part in scores)) * scale
        mixed = jnp.zeros((values.shape[1], scores[0].shape[1]), jnp.float32)
        for part, part_scores in zip(parts, scores):
            probs = jnp.exp2(part_scores * scale - row_max).astype(jnp.bfloat16)
            mixed = mixed + jnp.dot(values[head, :, part], probs, preferred_element_type=jnp.float32)
        mixed = (mixed[:head_size] / mixed[head_size : head_size + 1]).astype(jnp.bfloat16)
        for half, flip in enumerate(flips):
            outs[flip // 2][head * head_size : (head + 1) * head_size, :] = mixed[:, half * block : (half + 1) * block]


def stack_kernel(*refs):
    for at, ref in enumerate(refs[:-1]):
        refs[-1][at] = ref[1:]


def stack_keys_and_values(arrays):
    parts, features, frames = arrays[0].shape
    return pl.pallas_call(
        stack_kernel,
        out_shape=pltpu.VMEM((len(arrays), parts - 1, features, frames), arrays[0].dtype),
        in_specs=[WHOLE] * len(arrays),
        out_specs=WHOLE,
        compiler_params=params(16),
        name="stack_keys_and_values",
    )(*arrays)


def attend(lengths, same, own_other, other, rest, groups):
    _, features, block = same[0].shape
    keys = groups * HEADS * block
    padded = features // 2 + 32
    rest = [] if rest is None else [rest]
    return pl.pallas_call(
        functools.partial(attention_kernel, groups),
        out_shape=[pltpu.VMEM((features, block), jnp.bfloat16)] * len(FLIPS),
        in_specs=[WHOLE] * (3 + len(FLIPS) + len(rest)),
        out_specs=[WHOLE] * len(FLIPS),
        scratch_shapes=[pltpu.VMEM((2, keys, padded), jnp.bfloat16), pltpu.VMEM((2, padded, keys), jnp.bfloat16)],
        compiler_params=params(32),
        cost_estimate=pl.CostEstimate(flops=8 * keys * keys * features, bytes_accessed=0, transcendentals=0),
        name="attend_two_heads",
    )(lengths, *same, own_other, other, *rest)


def gather_heads(heads, turned):
    rows = heads[0].shape[0]
    for flip, ref in zip(FLIPS, heads):
        first = pl.multiple_of(((place_in_group() ^ flip) >> 1) * rows, 32)
        turned[pl.ds(first, rows), :] = ref[...]


def project_kernel(*refs):
    each = len(FLIPS)
    heads, halves, (out_ref, turned, weight) = refs[:each], refs[each : each + 2], refs[each + 2 :]
    gather_heads(heads, turned)
    half = weight.shape[0] // 2
    for other, ref in enumerate(halves):
        weight[pl.ds(pl.multiple_of(((place_in_group() & 1) ^ other) * half, 32), half), :] = ref[...]
    out_ref[0] = jnp.dot(turned[...].T, weight[...], preferred_element_type=jnp.float32).astype(out_ref.dtype)


def project_near_kernel(*refs):
    each = len(FLIPS)
    heads, own_ref, pieces, thirds = refs[:each], refs[each], refs[each + 1 : each + 5], refs[each + 5 : each + 8]
    blocks_ref, sum_ref, rest_ref, turned, weight, third = refs[each + 8 :]
    gather_heads(heads, turned)
    attention = turned[...].T
    place = place_in_group()
    core, parity = place & 1, parity_of(place)
    half = pieces[0].shape[0]
    for flip in (1, 2):
        mine = core == 2 - flip
        for other in range(2):
            here = pl.ds(pl.multiple_of((parity ^ other) * half, 32), half)
            weight[flip - 1, here, :] = jnp.where(mine, pieces[other][...], pieces[2 + other][...])
    for flip, block in enumerate((own_ref[...], weight[0], weight[1])):
        blocks_ref[flip] = jnp.dot(attention, block, preferred_element_type=jnp.float32).astype(blocks_ref.dtype)

    part, quarter = thirds[0].shape[0], half // 2
    for other in range(2):
        third[pl.ds(pl.multiple_of((core ^ other) * (half - part), 16), part), :] = thirds[other][...]
    fitting = turned[pl.ds(pl.multiple_of(parity * half, 32), half), :].T
    total = jnp.dot(fitting, third[...], preferred_element_type=jnp.float32)
    for other in range(2):
        first = (1 - parity) * half + (core ^ other) * quarter
        fitting = turned[pl.ds(pl.multiple_of(first, 32), quarter), :].T
        if other:
            rest_ref[...] = fitting
        else:
            rows = thirds[2][pl.ds(pl.multiple_of(core * (part - quarter), 16), quarter), :]
            total = total + jnp.dot(fitting, rows, preferred_element_type=jnp.float32)
    sum_ref[...] = total


def project_third_kernel(blocks_ref, sum_ref, rest_ref, part_ref, out_ref, last, sems):
    shard = lax.axis_index("fsdp")
    quarter, columns = rest_ref.shape[1], last.shape[1]

    def copy_out(flip, block_ref):
        here = pl.ds(pl.multiple_of((shard ^ flip) * columns, 128), columns)
        copy = pltpu.make_async_copy(block_ref, out_ref.at[0, :, here], sems.at[flip])
        copy.start()
        return copy

    copies = [copy_out(flip, blocks_ref.at[flip]) for flip in range(3)]
    first = (1 - (place_in_group() & 1)) * (part_ref.shape[0] - quarter)
    rows = part_ref[pl.ds(pl.multiple_of(first, 16), quarter), :]
    total = sum_ref[...] + jnp.dot(rest_ref[...], rows, preferred_element_type=jnp.float32)
    last[...] = total.astype(last.dtype)
    copies.append(copy_out(3, last))
    for copy in copies:
        copy.wait()


def projection_cost(frames, features, columns):
    return pl.CostEstimate(
        flops=2 * features * frames * columns, bytes_accessed=2 * features * columns, transcendentals=0
    )


def project(heads, halves):
    rows, frames = heads[0].shape
    features, width = len(FLIPS) * rows, halves[0].shape[1]
    return pl.pallas_call(
        project_kernel,
        out_shape=jax.ShapeDtypeStruct((1, frames, width), jnp.bfloat16),
        in_specs=[WHOLE] * (len(FLIPS) + 2),
        out_specs=WHOLE,
        scratch_shapes=[pltpu.VMEM((features, frames), jnp.bfloat16), pltpu.VMEM((features, width), jnp.bfloat16)],
        compiler_params=params(24),
        cost_estimate=projection_cost(frames, features, width),
        name="project_heads",
    )(*heads, *halves)


def project_near(heads, own, pieces, thirds):
    frames = heads[0].shape[1]
    features, columns = own.shape
    return pl.pallas_call(
        project_near_kernel,
        out_shape=[
            pltpu.VMEM((3, frames, columns), jnp.bfloat16),
            pltpu.VMEM((frames, columns), jnp.float32),
            pltpu.VMEM((frames, features // 4), jnp.bfloat16),
        ],
        in_specs=[WHOLE] * (len(FLIPS) + 8),
        out_specs=[WHOLE] * 3,
        scratch_shapes=[
            pltpu.VMEM((features, frames), jnp.bfloat16),
            pltpu.VMEM((2, features, columns), jnp.bfloat16),
            pltpu.VMEM((features // 2, columns), jnp.bfloat16),
        ],
        compiler_params=params(24),
        cost_estimate=projection_cost(frames, features, 3 * columns),
        name="project_near_shards",
    )(*heads, own, *pieces, *thirds)


def project_third(blocks, so_far, rest, part):
    _, frames, columns = blocks.shape
    return pl.pallas_call(
        project_third_kernel,
        out_shape=jax.ShapeDtypeStruct((1, frames, 4 * columns), blocks.dtype),
        in_specs=[WHOLE] * 4,
        out_specs=IN_HBM,
        scratch_shapes=[pltpu.VMEM((frames, columns), jnp.bfloat16), pltpu.SemaphoreType.DMA((4,))],
        compiler_params=params(24),
        cost_estimate=projection_cost(frames, rest.shape[1], columns),
        name="project_third_shard",
    )(blocks, so_far, rest, part)


def per_device(ctx, fsdp, queries, key_rows, value_rows, lengths, out_weight):
    def exchange(array, axis, flip):
        size = ctx if axis == "ctx" else fsdp
        return lax.ppermute(array, axis, [(i, i ^ flip) for i in range(size)])

    def exchange_chips(arrays):
        return [exchange(array, "ctx", flip) for flip, array in zip(FLIPS[1:], arrays)]

    def exchange_in_plane(array):
        return lax.ppermute(array, "ctx", [(i, i ^ (4 if i % 2 else 2)) for i in range(ctx)])

    def exchange_along(array, *flips):
        pairs = [(i * fsdp + z, i * fsdp + (z ^ flips[i % 2])) for i in range(ctx) for z in range(fsdp)]
        return lax.ppermute(array, ("ctx", "fsdp"), pairs)

    core = place_in_group() & 1
    split_columns = fsdp == 4
    lengths = jnp.broadcast_to(lengths, (8, 128))
    rows, half = copy_in(queries, key_rows, value_rows, out_weight, split_columns)
    if split_columns:
        fetched = exchange_along(half, 2, 1)
    else:
        half = lax.all_gather(half, "fsdp", axis=1, tiled=True)

    own, *by_chip = turn(rows)
    same = exchange_chips(by_chip)
    own_other = exchange(own[1:], "ctx", 1)
    if split_columns:
        fetched, own_other, lengths = lax.optimization_barrier((fetched, own_other, lengths))
        passed = exchange_in_plane(fetched)
        depth = half.shape[0]
        part = depth // 2 + 16
        third = lax.dynamic_slice_in_dim(fetched, core * (depth - part), part, 0)
        third = exchange_along(third, 1, 2)
    same, own_other = lax.optimization_barrier((same, own_other))
    other = exchange(stack_keys_and_values(same), "ctx", 1)
    same = [own, *same]

    groups = ctx // HEADS
    rest = None
    if groups > 1:
        pairs = [own[1:], own_other]
        for at, array in enumerate(same[1:]):
            pairs += [array[1:], other[at]]
        across = [[head + first for first in range(0, ctx, HEADS)] for head in range(HEADS)]
        rest = lax.all_gather(jnp.stack(pairs), "ctx", axis=0, axis_index_groups=across, tiled=True)
    mixed = attend(lengths, same, own_other, other, rest, groups)

    heads = [mixed[0], *exchange_chips(mixed[1:])]
    if not split_columns:
        return project(heads, [half, exchange(half, "ctx", 1)])
    third_passed = exchange_in_plane(stage(third, 1500000000))
    heads[3], fetched, third = lax.optimization_barrier((heads[3], fetched, third))
    heads[1], heads[2], passed = lax.optimization_barrier((heads[1], heads[2], passed))
    fetched_other, passed_other, third_other, third_passed_other = (
        exchange(array, "ctx", 1) for array in (fetched, passed, third, third_passed)
    )
    third_other, passed_other = lax.optimization_barrier((third_other, passed_other))
    near = [fetched, passed, fetched_other, passed_other]
    blocks, so_far, rest = project_near(heads, out_weight, near, [third, third_other, third_passed])
    return project_third(blocks, so_far, rest, third_passed_other)


def solution(mesh):
    return jax.shard_map(
        functools.partial(per_device, mesh.shape["ctx"], mesh.shape["fsdp"]),
        mesh=mesh,
        in_specs=(
            P("fsdp", "ctx", None),
            P("fsdp", "ctx", None),
            P("fsdp", "ctx", None),
            P("fsdp"),
            P(None, "fsdp"),
        ),
        out_specs=P("fsdp", "ctx", None),
        check_vma=False,
    )
```

```python
import functools
import math

import jax
import jax.numpy as jnp
from jax import lax
from jax.experimental import pallas as pl
from jax.experimental.pallas import tpu as pltpu
from jax.sharding import PartitionSpec as P

HEADS = 8
FLIPS = tuple(range(0, HEADS, 2))
WHOLE = pl.BlockSpec(memory_space=pltpu.VMEM)
IN_HBM = pl.BlockSpec(memory_space=pltpu.HBM)


def params(mebibytes=48):
    return pltpu.CompilerParams(vmem_limit_bytes=mebibytes * 1024 * 1024)


def place_in_group():
    return lax.axis_index("ctx") % HEADS


def parity_of(place):
    return ((place >> 2) ^ (place >> 1)) & 1


def copy_in_kernel(by_parity, query_ref, key_ref, value_ref, weight_ref, rows_ref, half_ref, sems):
    place = place_in_group()
    first = (parity_of(place) if by_parity else place & 1) * half_ref.shape[0]
    copies = [pltpu.make_async_copy(weight_ref.at[pl.ds(pl.multiple_of(first, 32), half_ref.shape[0])], half_ref, sems.at[3])]
    for part, ref in enumerate((query_ref, key_ref, value_ref)):
        copies.append(pltpu.make_async_copy(ref.at[0], rows_ref.at[part], sems.at[part]))
    for copy in copies:
        copy.start()
    for copy in copies:
        copy.wait()


def copy_in(queries, key_rows, value_rows, out_weight, by_parity):
    _, frames, features = queries.shape
    half = (out_weight.shape[0] // 2, out_weight.shape[1])
    arrays = [pltpu.with_memory_space_constraint(array, pltpu.HBM) for array in (queries, key_rows, value_rows, out_weight)]
    return pl.pallas_call(
        functools.partial(copy_in_kernel, by_parity),
        out_shape=[pltpu.VMEM((3, frames, features), queries.dtype), pltpu.VMEM(half, out_weight.dtype)],
        in_specs=[IN_HBM] * 4,
        out_specs=[WHOLE] * 2,
        scratch_shapes=[pltpu.SemaphoreType.DMA((4,))],
        compiler_params=params(16),
        name="copy_in",
    )(*arrays)


def turn_kernel(rows_ref, *refs):
    outs, turned = refs[:-1], refs[-1]
    features = outs[0].shape[1]
    chip = place_in_group() >> 1
    for part in range(3):
        turned[part] = rows_ref[part].T
        for flip, out_ref in zip(FLIPS, outs):
            first = pl.multiple_of((chip ^ (flip >> 1)) * features, 32)
            out_ref[part] = turned[part, pl.ds(first, features), :]


def turn(rows):
    _, frames, features = rows.shape
    return pl.pallas_call(
        turn_kernel,
        out_shape=[pltpu.VMEM((3, features // len(FLIPS), frames), rows.dtype)] * len(FLIPS),
        in_specs=[WHOLE],
        out_specs=[WHOLE] * len(FLIPS),
        scratch_shapes=[pltpu.VMEM((3, features, frames), rows.dtype)],
        compiler_params=params(16),
        name="turn_heads",
    )(rows)


def attention_kernel(groups, lengths_ref, *refs):
    each = len(FLIPS)
    same, own_other, other = refs[:each], refs[each], refs[each + 1]
    rest_ref = refs[each + 2] if groups > 1 else None
    outs, (keys, values) = refs[-2 - each : -2], refs[-2:]
    block = outs[0].shape[1]
    head_size = outs[0].shape[0] // 2
    place = place_in_group()
    scale = jnp.float32(math.log2(math.e) / math.sqrt(head_size))
    pad = keys.shape[2] - head_size

    def piece(at, head, part):
        rows = slice(head * head_size, (head + 1) * head_size)
        if groups > 1:
            return rest_ref[at, part - 1, rows, :]
        if at % 2 == 0:
            return same[at // 2][part, rows, :]
        return other[at // 2 - 1, part - 1, rows, :] if at > 1 else own_other[part - 1, rows, :]

    ones = jnp.where(lax.broadcasted_iota(jnp.int32, (pad, block), 0) == 0, 1.0, 0.0).astype(keys.dtype)
    at_feature = lax.broadcasted_iota(jnp.int32, (pad, block), 0)
    at_frame = lax.broadcasted_iota(jnp.int32, (pad, block), 1)

    def prepare(head):
        for at in range(groups * HEADS):
            here = slice(at * block, (at + 1) * block)
            frame = (at // HEADS * HEADS + (place ^ (at % HEADS))) * block + at_frame
            bias = jnp.where((at_feature == 0) & (frame >= lengths_ref[:1, :]), -1e30, 0.0).astype(keys.dtype)
            keys[head, here, :] = jnp.concatenate([piece(at, head, 1), bias], axis=0).T
            values[head, :, here] = jnp.concatenate([piece(at, head, 2), ones], axis=0)

    def score(head, flips):
        rows = slice(head * head_size, (head + 1) * head_size)
        query = jnp.concatenate([jnp.concatenate([same[flip // 2][0, rows, :], ones], axis=0) for flip in flips], axis=1)
        return [jnp.dot(keys[head, part, :], query, preferred_element_type=jnp.float32) for part in parts]

    parts = [slice(first, first + keys.shape[1] // 4) for first in range(0, keys.shape[1], keys.shape[1] // 4)]
    chunks = [(head, flips) for head in range(2) for flips in (FLIPS[:2], FLIPS[2:])]
    prepare(0)
    later = score(*chunks[0])
    prepare(1)
    for at, (head, flips) in enumerate(chunks):
        scores = later
        if at + 1 < len(chunks):
            later = score(*chunks[at + 1])
        row_max = functools.reduce(jnp.maximum, (jnp.max(part, axis=0, keepdims=True) for part in scores)) * scale
        mixed = jnp.zeros((values.shape[1], scores[0].shape[1]), jnp.float32)
        for part, part_scores in zip(parts, scores):
            probs = jnp.exp2(part_scores * scale - row_max).astype(jnp.bfloat16)
            mixed = mixed + jnp.dot(values[head, :, part], probs, preferred_element_type=jnp.float32)
        mixed = (mixed[:head_size] / mixed[head_size : head_size + 1]).astype(jnp.bfloat16)
        for half, flip in enumerate(flips):
            outs[flip // 2][head * head_size : (head + 1) * head_size, :] = mixed[:, half * block : (half + 1) * block]


def stack_kernel(*refs):
    for at, ref in enumerate(refs[:-1]):
        refs[-1][at] = ref[1:]


def stack_keys_and_values(arrays):
    parts, features, frames = arrays[0].shape
    return pl.pallas_call(
        stack_kernel,
        out_shape=pltpu.VMEM((len(arrays), parts - 1, features, frames), arrays[0].dtype),
        in_specs=[WHOLE] * len(arrays),
        out_specs=WHOLE,
        compiler_params=params(16),
        name="stack_keys_and_values",
    )(*arrays)


def attend(lengths, same, own_other, other, rest, groups):
    _, features, block = same[0].shape
    keys = groups * HEADS * block
    padded = features // 2 + 32
    rest = [] if rest is None else [rest]
    return pl.pallas_call(
        functools.partial(attention_kernel, groups),
        out_shape=[pltpu.VMEM((features, block), jnp.bfloat16)] * len(FLIPS),
        in_specs=[WHOLE] * (3 + len(FLIPS) + len(rest)),
        out_specs=[WHOLE] * len(FLIPS),
        scratch_shapes=[pltpu.VMEM((2, keys, padded), jnp.bfloat16), pltpu.VMEM((2, padded, keys), jnp.bfloat16)],
        compiler_params=params(32),
        cost_estimate=pl.CostEstimate(flops=8 * keys * keys * features, bytes_accessed=0, transcendentals=0),
        name="attend_two_heads",
    )(lengths, *same, own_other, other, *rest)


def gather_heads(heads, turned):
    rows = heads[0].shape[0]
    for flip, ref in zip(FLIPS, heads):
        first = pl.multiple_of(((place_in_group() ^ flip) >> 1) * rows, 32)
        turned[pl.ds(first, rows), :] = ref[...]


def project_kernel(*refs):
    each = len(FLIPS)
    heads, halves, (out_ref, turned, weight) = refs[:each], refs[each : each + 2], refs[each + 2 :]
    gather_heads(heads, turned)
    half = weight.shape[0] // 2
    for other, ref in enumerate(halves):
        weight[pl.ds(pl.multiple_of(((place_in_group() & 1) ^ other) * half, 32), half), :] = ref[...]
    out_ref[0] = jnp.dot(turned[...].T, weight[...], preferred_element_type=jnp.float32).astype(out_ref.dtype)


def project_near_kernel(*refs):
    each = len(FLIPS)
    heads, own_ref, pieces, thirds = refs[:each], refs[each], refs[each + 1 : each + 5], refs[each + 5 : each + 8]
    blocks_ref, sum_ref, rest_ref, turned, weight, third = refs[each + 8 :]
    gather_heads(heads, turned)
    attention = turned[...].T
    place = place_in_group()
    core, parity = place & 1, parity_of(place)
    half = pieces[0].shape[0]
    for flip in (1, 2):
        mine = core == 2 - flip
        for other in range(2):
            here = pl.ds(pl.multiple_of((parity ^ other) * half, 32), half)
            weight[flip - 1, here, :] = jnp.where(mine, pieces[other][...], pieces[2 + other][...])
    for flip, block in enumerate((own_ref[...], weight[0], weight[1])):
        blocks_ref[flip] = jnp.dot(attention, block, preferred_element_type=jnp.float32).astype(blocks_ref.dtype)

    part, quarter = thirds[0].shape[0], half // 2
    for other in range(2):
        third[pl.ds(pl.multiple_of((core ^ other) * (half - part), 16), part), :] = thirds[other][...]
    fitting = turned[pl.ds(pl.multiple_of(parity * half, 32), half), :].T
    total = jnp.dot(fitting, third[...], preferred_element_type=jnp.float32)
    for other in range(2):
        first = (1 - parity) * half + (core ^ other) * quarter
        fitting = turned[pl.ds(pl.multiple_of(first, 32), quarter), :].T
        if other:
            rest_ref[...] = fitting
        else:
            rows = thirds[2][pl.ds(pl.multiple_of(core * (part - quarter), 16), quarter), :]
            total = total + jnp.dot(fitting, rows, preferred_element_type=jnp.float32)
    sum_ref[...] = total


def project_third_kernel(blocks_ref, sum_ref, rest_ref, part_ref, out_ref, last, sems):
    shard = lax.axis_index("fsdp")
    quarter, columns = rest_ref.shape[1], last.shape[1]

    def copy_out(flip, block_ref, frames, sem):
        here = pl.ds(pl.multiple_of((shard ^ flip) * columns, 128), columns)
        copy = pltpu.make_async_copy(block_ref, out_ref.at[0, frames, here], sems.at[sem])
        copy.start()
        return copy

    copies = [copy_out(flip, blocks_ref.at[flip], pl.ds(0, last.shape[0]), flip) for flip in range(3)]
    first = (1 - (place_in_group() & 1)) * (part_ref.shape[0] - quarter)
    rows = part_ref[pl.ds(pl.multiple_of(first, 16), quarter), :]
    half = last.shape[0] // 2
    for at in range(2):
        frames = pl.ds(at * half, half)
        total = sum_ref[frames, :] + jnp.dot(rest_ref[frames, :], rows, preferred_element_type=jnp.float32)
        last[frames, :] = total.astype(last.dtype)
        copies.append(copy_out(3, last.at[frames], frames, 3 + at))
    for copy in copies:
        copy.wait()


def projection_cost(frames, features, columns):
    return pl.CostEstimate(
        flops=2 * features * frames * columns, bytes_accessed=2 * features * columns, transcendentals=0
    )


def project(heads, halves):
    rows, frames = heads[0].shape
    features, width = len(FLIPS) * rows, halves[0].shape[1]
    return pl.pallas_call(
        project_kernel,
        out_shape=jax.ShapeDtypeStruct((1, frames, width), jnp.bfloat16),
        in_specs=[WHOLE] * (len(FLIPS) + 2),
        out_specs=WHOLE,
        scratch_shapes=[pltpu.VMEM((features, frames), jnp.bfloat16), pltpu.VMEM((features, width), jnp.bfloat16)],
        compiler_params=params(24),
        cost_estimate=projection_cost(frames, features, width),
        name="project_heads",
    )(*heads, *halves)


def project_near(heads, own, pieces, thirds):
    frames = heads[0].shape[1]
    features, columns = own.shape
    return pl.pallas_call(
        project_near_kernel,
        out_shape=[
            pltpu.VMEM((3, frames, columns), jnp.bfloat16),
            pltpu.VMEM((frames, columns), jnp.float32),
            pltpu.VMEM((frames, features // 4), jnp.bfloat16),
        ],
        in_specs=[WHOLE] * (len(FLIPS) + 8),
        out_specs=[WHOLE] * 3,
        scratch_shapes=[
            pltpu.VMEM((features, frames), jnp.bfloat16),
            pltpu.VMEM((2, features, columns), jnp.bfloat16),
            pltpu.VMEM((features // 2, columns), jnp.bfloat16),
        ],
        compiler_params=params(24),
        cost_estimate=projection_cost(frames, features, 3 * columns),
        name="project_near_shards",
    )(*heads, own, *pieces, *thirds)


def project_third(blocks, so_far, rest, part):
    _, frames, columns = blocks.shape
    return pl.pallas_call(
        project_third_kernel,
        out_shape=jax.ShapeDtypeStruct((1, frames, 4 * columns), blocks.dtype),
        in_specs=[WHOLE] * 4,
        out_specs=IN_HBM,
        scratch_shapes=[pltpu.VMEM((frames, columns), jnp.bfloat16), pltpu.SemaphoreType.DMA((5,))],
        compiler_params=params(24),
        cost_estimate=projection_cost(frames, rest.shape[1], columns),
        name="project_third_shard",
    )(blocks, so_far, rest, part)


def per_device(ctx, fsdp, queries, key_rows, value_rows, lengths, out_weight):
    def exchange(array, axis, flip):
        size = ctx if axis == "ctx" else fsdp
        return lax.ppermute(array, axis, [(i, i ^ flip) for i in range(size)])

    def exchange_chips(arrays):
        return [exchange(array, "ctx", flip) for flip, array in zip(FLIPS[1:], arrays)]

    def exchange_in_plane(array):
        return lax.ppermute(array, "ctx", [(i, i ^ (4 if i % 2 else 2)) for i in range(ctx)])

    def exchange_along(array, *flips):
        pairs = [(i * fsdp + z, i * fsdp + (z ^ flips[i % 2])) for i in range(ctx) for z in range(fsdp)]
        return lax.ppermute(array, ("ctx", "fsdp"), pairs)

    core = place_in_group() & 1
    split_columns = fsdp == 4
    lengths = jnp.broadcast_to(lengths, (8, 128))
    rows, half = copy_in(queries, key_rows, value_rows, out_weight, split_columns)
    if split_columns:
        fetched = exchange_along(half, 2, 1)
    else:
        half = lax.all_gather(half, "fsdp", axis=1, tiled=True)

    own, *by_chip = turn(rows)
    same = exchange_chips(by_chip)
    own_other = exchange(own[1:], "ctx", 1)
    if split_columns:
        fetched, own_other, lengths = lax.optimization_barrier((fetched, own_other, lengths))
        passed = exchange_in_plane(fetched)
        depth = half.shape[0]
        part = depth // 2 + 16
        third = lax.dynamic_slice_in_dim(fetched, core * (depth - part), part, 0)
        third = exchange_along(third, 1, 2)
    same, own_other = lax.optimization_barrier((same, own_other))
    other = exchange(stack_keys_and_values(same), "ctx", 1)
    same = [own, *same]

    groups = ctx // HEADS
    rest = None
    if groups > 1:
        pairs = [own[1:], own_other]
        for at, array in enumerate(same[1:]):
            pairs += [array[1:], other[at]]
        across = [[head + first for first in range(0, ctx, HEADS)] for head in range(HEADS)]
        rest = lax.all_gather(jnp.stack(pairs), "ctx", axis=0, axis_index_groups=across, tiled=True)
    mixed = attend(lengths, same, own_other, other, rest, groups)

    heads = [mixed[0], *exchange_chips(mixed[1:])]
    if not split_columns:
        return project(heads, [half, exchange(half, "ctx", 1)])
    third_passed = exchange_in_plane(third)
    heads[3], fetched, third = lax.optimization_barrier((heads[3], fetched, third))
    heads[1], heads[2], passed = lax.optimization_barrier((heads[1], heads[2], passed))
    fetched_other, passed_other, third_other, third_passed_other = (
        exchange(array, "ctx", 1) for array in (fetched, passed, third, third_passed)
    )
    third_other, passed_other = lax.optimization_barrier((third_other, passed_other))
    near = [fetched, passed, fetched_other, passed_other]
    blocks, so_far, rest = project_near(heads, out_weight, near, [third, third_other, third_passed])
    return project_third(blocks, so_far, rest, third_passed_other)


def solution(mesh):
    return jax.shard_map(
        functools.partial(per_device, mesh.shape["ctx"], mesh.shape["fsdp"]),
        mesh=mesh,
        in_specs=(
            P("fsdp", "ctx", None),
            P("fsdp", "ctx", None),
            P("fsdp", "ctx", None),
            P("fsdp"),
            P(None, "fsdp"),
        ),
        out_specs=P("fsdp", "ctx", None),
        check_vma=False,
    )
```

```python
import functools
import math

import jax
import jax.numpy as jnp
from jax import lax
from jax.experimental import pallas as pl
from jax.experimental.pallas import tpu as pltpu
from jax.sharding import PartitionSpec as P

HEADS = 8
FLIPS = tuple(range(0, HEADS, 2))
WHOLE = pl.BlockSpec(memory_space=pltpu.VMEM)
IN_HBM = pl.BlockSpec(memory_space=pltpu.HBM)


def params(mebibytes=48):
    return pltpu.CompilerParams(vmem_limit_bytes=mebibytes * 1024 * 1024)


def place_in_group():
    return lax.axis_index("ctx") % HEADS


def parity_of(place):
    return ((place >> 2) ^ (place >> 1)) & 1


def copy_in_kernel(by_parity, query_ref, key_ref, value_ref, weight_ref, rows_ref, half_ref, sems):
    place = place_in_group()
    first = (parity_of(place) if by_parity else place & 1) * half_ref.shape[0]
    copies = [pltpu.make_async_copy(weight_ref.at[pl.ds(pl.multiple_of(first, 32), half_ref.shape[0])], half_ref, sems.at[3])]
    for part, ref in enumerate((query_ref, key_ref, value_ref)):
        copies.append(pltpu.make_async_copy(ref.at[0], rows_ref.at[part], sems.at[part]))
    for copy in copies:
        copy.start()
    for copy in copies:
        copy.wait()


def copy_in(queries, key_rows, value_rows, out_weight, by_parity):
    _, frames, features = queries.shape
    half = (out_weight.shape[0] // 2, out_weight.shape[1])
    arrays = [pltpu.with_memory_space_constraint(array, pltpu.HBM) for array in (queries, key_rows, value_rows, out_weight)]
    return pl.pallas_call(
        functools.partial(copy_in_kernel, by_parity),
        out_shape=[pltpu.VMEM((3, frames, features), queries.dtype), pltpu.VMEM(half, out_weight.dtype)],
        in_specs=[IN_HBM] * 4,
        out_specs=[WHOLE] * 2,
        scratch_shapes=[pltpu.SemaphoreType.DMA((4,))],
        compiler_params=params(16),
        name="copy_in",
    )(*arrays)


def turn_kernel(rows_ref, *refs):
    outs, turned = refs[:-1], refs[-1]
    features = outs[0].shape[1]
    chip = place_in_group() >> 1
    for part in range(3):
        turned[part] = rows_ref[part].T
        for flip, out_ref in zip(FLIPS, outs):
            first = pl.multiple_of((chip ^ (flip >> 1)) * features, 32)
            out_ref[part] = turned[part, pl.ds(first, features), :]


def turn(rows):
    _, frames, features = rows.shape
    return pl.pallas_call(
        turn_kernel,
        out_shape=[pltpu.VMEM((3, features // len(FLIPS), frames), rows.dtype)] * len(FLIPS),
        in_specs=[WHOLE],
        out_specs=[WHOLE] * len(FLIPS),
        scratch_shapes=[pltpu.VMEM((3, features, frames), rows.dtype)],
        compiler_params=params(16),
        name="turn_heads",
    )(rows)


def attention_kernel(groups, lengths_ref, *refs):
    each = len(FLIPS)
    same, own_other, other = refs[:each], refs[each], refs[each + 1]
    rest_ref = refs[each + 2] if groups > 1 else None
    outs, (keys, values) = refs[-2 - each : -2], refs[-2:]
    block = outs[0].shape[1]
    head_size = outs[0].shape[0] // 2
    place = place_in_group()
    scale = jnp.float32(math.log2(math.e) / math.sqrt(head_size))
    pad = keys.shape[2] - head_size

    def piece(at, head, part):
        rows = slice(head * head_size, (head + 1) * head_size)
        if groups > 1:
            return rest_ref[at, part - 1, rows, :]
        if at % 2 == 0:
            return same[at // 2][part, rows, :]
        return other[at // 2 - 1, part - 1, rows, :] if at > 1 else own_other[part - 1, rows, :]

    ones = jnp.where(lax.broadcasted_iota(jnp.int32, (pad, block), 0) == 0, 1.0, 0.0).astype(keys.dtype)
    at_feature = lax.broadcasted_iota(jnp.int32, (pad, block), 0)
    at_frame = lax.broadcasted_iota(jnp.int32, (pad, block), 1)

    def prepare(head):
        for at in range(groups * HEADS):
            here = slice(at * block, (at + 1) * block)
            frame = (at // HEADS * HEADS + (place ^ (at % HEADS))) * block + at_frame
            bias = jnp.where((at_feature == 0) & (frame >= lengths_ref[:1, :]), -1e30, 0.0).astype(keys.dtype)
            keys[head, here, :] = jnp.concatenate([piece(at, head, 1), bias], axis=0).T
            values[head, :, here] = jnp.concatenate([piece(at, head, 2), ones], axis=0)

    def score(head, flips):
        rows = slice(head * head_size, (head + 1) * head_size)
        query = jnp.concatenate([jnp.concatenate([same[flip // 2][0, rows, :], ones], axis=0) for flip in flips], axis=1)
        return [jnp.dot(keys[head, part, :], query, preferred_element_type=jnp.float32) for part in parts]

    parts = [slice(first, first + keys.shape[1] // 2) for first in range(0, keys.shape[1], keys.shape[1] // 2)]
    chunks = [(head, flips) for head in range(2) for flips in (FLIPS[:2], FLIPS[2:])]
    prepare(0)
    later = score(*chunks[0])
    prepare(1)
    for at, (head, flips) in enumerate(chunks):
        scores = later
        if at + 1 < len(chunks):
            later = score(*chunks[at + 1])
        row_max = functools.reduce(jnp.maximum, (jnp.max(part, axis=0, keepdims=True) for part in scores)) * scale
        mixed = jnp.zeros((values.shape[1], scores[0].shape[1]), jnp.float32)
        for part, part_scores in zip(parts, scores):
            probs = jnp.exp2(part_scores * scale - row_max).astype(jnp.bfloat16)
            mixed = mixed + jnp.dot(values[head, :, part], probs, preferred_element_type=jnp.float32)
        mixed = (mixed[:head_size] / mixed[head_size : head_size + 1]).astype(jnp.bfloat16)
        for half, flip in enumerate(flips):
            outs[flip // 2][head * head_size : (head + 1) * head_size, :] = mixed[:, half * block : (half + 1) * block]


def stack_kernel(*refs):
    for at, ref in enumerate(refs[:-1]):
        refs[-1][at] = ref[1:]


def stack_keys_and_values(arrays):
    parts, features, frames = arrays[0].shape
    return pl.pallas_call(
        stack_kernel,
        out_shape=pltpu.VMEM((len(arrays), parts - 1, features, frames), arrays[0].dtype),
        in_specs=[WHOLE] * len(arrays),
        out_specs=WHOLE,
        compiler_params=params(16),
        name="stack_keys_and_values",
    )(*arrays)


def attend(lengths, same, own_other, other, rest, groups):
    _, features, block = same[0].shape
    keys = groups * HEADS * block
    padded = features // 2 + 32
    rest = [] if rest is None else [rest]
    return pl.pallas_call(
        functools.partial(attention_kernel, groups),
        out_shape=[pltpu.VMEM((features, block), jnp.bfloat16)] * len(FLIPS),
        in_specs=[WHOLE] * (3 + len(FLIPS) + len(rest)),
        out_specs=[WHOLE] * len(FLIPS),
        scratch_shapes=[pltpu.VMEM((2, keys, padded), jnp.bfloat16), pltpu.VMEM((2, padded, keys), jnp.bfloat16)],
        compiler_params=params(32),
        cost_estimate=pl.CostEstimate(flops=8 * keys * keys * features, bytes_accessed=0, transcendentals=0),
        name="attend_two_heads",
    )(lengths, *same, own_other, other, *rest)


def gather_heads(heads, turned):
    rows = heads[0].shape[0]
    for flip, ref in zip(FLIPS, heads):
        first = pl.multiple_of(((place_in_group() ^ flip) >> 1) * rows, 32)
        turned[pl.ds(first, rows), :] = ref[...]


def project_kernel(*refs):
    each = len(FLIPS)
    heads, halves, (out_ref, turned, weight) = refs[:each], refs[each : each + 2], refs[each + 2 :]
    gather_heads(heads, turned)
    half = weight.shape[0] // 2
    for other, ref in enumerate(halves):
        weight[pl.ds(pl.multiple_of(((place_in_group() & 1) ^ other) * half, 32), half), :] = ref[...]
    out_ref[0] = jnp.dot(turned[...].T, weight[...], preferred_element_type=jnp.float32).astype(out_ref.dtype)


def project_near_kernel(*refs):
    each = len(FLIPS)
    heads, own_ref, pieces, thirds = refs[:each], refs[each], refs[each + 1 : each + 5], refs[each + 5 : each + 8]
    blocks_ref, sum_ref, rest_ref, turned, weight, third = refs[each + 8 :]
    gather_heads(heads, turned)
    attention = turned[...].T
    place = place_in_group()
    core, parity = place & 1, parity_of(place)
    half = pieces[0].shape[0]
    for flip in (1, 2):
        mine = core == 2 - flip
        for other in range(2):
            here = pl.ds(pl.multiple_of((parity ^ other) * half, 32), half)
            weight[flip - 1, here, :] = jnp.where(mine, pieces[other][...], pieces[2 + other][...])
    for flip, block in enumerate((own_ref[...], weight[0], weight[1])):
        blocks_ref[flip] = jnp.dot(attention, block, preferred_element_type=jnp.float32).astype(blocks_ref.dtype)

    part, quarter = thirds[0].shape[0], half // 2
    for other in range(2):
        third[pl.ds(pl.multiple_of((core ^ other) * (half - part), 16), part), :] = thirds[other][...]
    fitting = turned[pl.ds(pl.multiple_of(parity * half, 32), half), :].T
    total = jnp.dot(fitting, third[...], preferred_element_type=jnp.float32)
    for other in range(2):
        first = (1 - parity) * half + (core ^ other) * quarter
        fitting = turned[pl.ds(pl.multiple_of(first, 32), quarter), :].T
        if other:
            rest_ref[...] = fitting
        else:
            rows = thirds[2][pl.ds(pl.multiple_of(core * (part - quarter), 16), quarter), :]
            total = total + jnp.dot(fitting, rows, preferred_element_type=jnp.float32)
    sum_ref[...] = total


def project_third_kernel(blocks_ref, sum_ref, rest_ref, part_ref, out_ref, last, sems):
    shard = lax.axis_index("fsdp")
    quarter, columns = rest_ref.shape[1], last.shape[1]

    def copy_out(flip, block_ref):
        here = pl.ds(pl.multiple_of((shard ^ flip) * columns, 128), columns)
        copy = pltpu.make_async_copy(block_ref, out_ref.at[0, :, here], sems.at[flip])
        copy.start()
        return copy

    copies = [copy_out(flip, blocks_ref.at[flip]) for flip in range(3)]
    first = (1 - (place_in_group() & 1)) * (part_ref.shape[0] - quarter)
    rows = part_ref[pl.ds(pl.multiple_of(first, 16), quarter), :]
    total = sum_ref[...] + jnp.dot(rest_ref[...], rows, preferred_element_type=jnp.float32)
    last[...] = total.astype(last.dtype)
    copies.append(copy_out(3, last))
    for copy in copies:
        copy.wait()


def projection_cost(frames, features, columns):
    return pl.CostEstimate(
        flops=2 * features * frames * columns, bytes_accessed=2 * features * columns, transcendentals=0
    )


def project(heads, halves):
    rows, frames = heads[0].shape
    features, width = len(FLIPS) * rows, halves[0].shape[1]
    return pl.pallas_call(
        project_kernel,
        out_shape=jax.ShapeDtypeStruct((1, frames, width), jnp.bfloat16),
        in_specs=[WHOLE] * (len(FLIPS) + 2),
        out_specs=WHOLE,
        scratch_shapes=[pltpu.VMEM((features, frames), jnp.bfloat16), pltpu.VMEM((features, width), jnp.bfloat16)],
        compiler_params=params(24),
        cost_estimate=projection_cost(frames, features, width),
        name="project_heads",
    )(*heads, *halves)


def project_near(heads, own, pieces, thirds):
    frames = heads[0].shape[1]
    features, columns = own.shape
    return pl.pallas_call(
        project_near_kernel,
        out_shape=[
            pltpu.VMEM((3, frames, columns), jnp.bfloat16),
            pltpu.VMEM((frames, columns), jnp.float32),
            pltpu.VMEM((frames, features // 4), jnp.bfloat16),
        ],
        in_specs=[WHOLE] * (len(FLIPS) + 8),
        out_specs=[WHOLE] * 3,
        scratch_shapes=[
            pltpu.VMEM((features, frames), jnp.bfloat16),
            pltpu.VMEM((2, features, columns), jnp.bfloat16),
            pltpu.VMEM((features // 2, columns), jnp.bfloat16),
        ],
        compiler_params=params(24),
        cost_estimate=projection_cost(frames, features, 3 * columns),
        name="project_near_shards",
    )(*heads, own, *pieces, *thirds)


def project_third(blocks, so_far, rest, part):
    _, frames, columns = blocks.shape
    return pl.pallas_call(
        project_third_kernel,
        out_shape=jax.ShapeDtypeStruct((1, frames, 4 * columns), blocks.dtype),
        in_specs=[WHOLE] * 4,
        out_specs=IN_HBM,
        scratch_shapes=[pltpu.VMEM((frames, columns), jnp.bfloat16), pltpu.SemaphoreType.DMA((4,))],
        compiler_params=params(24),
        cost_estimate=projection_cost(frames, rest.shape[1], columns),
        name="project_third_shard",
    )(blocks, so_far, rest, part)


def per_device(ctx, fsdp, queries, key_rows, value_rows, lengths, out_weight):
    def exchange(array, axis, flip):
        size = ctx if axis == "ctx" else fsdp
        return lax.ppermute(array, axis, [(i, i ^ flip) for i in range(size)])

    def exchange_chips(arrays):
        return [exchange(array, "ctx", flip) for flip, array in zip(FLIPS[1:], arrays)]

    def exchange_in_plane(array):
        return lax.ppermute(array, "ctx", [(i, i ^ (4 if i % 2 else 2)) for i in range(ctx)])

    def exchange_along(array, *flips):
        pairs = [(i * fsdp + z, i * fsdp + (z ^ flips[i % 2])) for i in range(ctx) for z in range(fsdp)]
        return lax.ppermute(array, ("ctx", "fsdp"), pairs)

    core = place_in_group() & 1
    split_columns = fsdp == 4
    lengths = jnp.broadcast_to(lengths, (8, 128))
    rows, half = copy_in(queries, key_rows, value_rows, out_weight, split_columns)
    if split_columns:
        fetched = exchange_along(half, 2, 1)
    else:
        half = lax.all_gather(half, "fsdp", axis=1, tiled=True)

    own, *by_chip = turn(rows)
    same = exchange_chips(by_chip)
    own_other = exchange(own[1:], "ctx", 1)
    if split_columns:
        fetched, own_other, lengths = lax.optimization_barrier((fetched, own_other, lengths))
        passed = exchange_in_plane(fetched)
        depth = half.shape[0]
        part = depth // 2 + 16
        third = lax.dynamic_slice_in_dim(fetched, core * (depth - part), part, 0)
        third = exchange_along(third, 1, 2)
    same, own_other = lax.optimization_barrier((same, own_other))
    other = exchange(stack_keys_and_values(same), "ctx", 1)
    same = [own, *same]

    groups = ctx // HEADS
    rest = None
    if groups > 1:
        pairs = [own[1:], own_other]
        for at, array in enumerate(same[1:]):
            pairs += [array[1:], other[at]]
        across = [[head + first for first in range(0, ctx, HEADS)] for head in range(HEADS)]
        rest = lax.all_gather(jnp.stack(pairs), "ctx", axis=0, axis_index_groups=across, tiled=True)
    mixed = attend(lengths, same, own_other, other, rest, groups)

    heads = [mixed[0], *exchange_chips(mixed[1:])]
    if not split_columns:
        return project(heads, [half, exchange(half, "ctx", 1)])
    third_passed = exchange_in_plane(third)
    heads[3], fetched, third = lax.optimization_barrier((heads[3], fetched, third))
    heads[1], heads[2], passed = lax.optimization_barrier((heads[1], heads[2], passed))
    fetched_other, passed_other, third_other, third_passed_other = (
        exchange(array, "ctx", 1) for array in (fetched, passed, third, third_passed)
    )
    third_other, passed_other = lax.optimization_barrier((third_other, passed_other))
    near = [fetched, passed, fetched_other, passed_other]
    blocks, so_far, rest = project_near(heads, out_weight, near, [third, third_other, third_passed])
    return project_third(blocks, so_far, rest, third_passed_other)


def solution(mesh):
    return jax.shard_map(
        functools.partial(per_device, mesh.shape["ctx"], mesh.shape["fsdp"]),
        mesh=mesh,
        in_specs=(
            P("fsdp", "ctx", None),
            P("fsdp", "ctx", None),
            P("fsdp", "ctx", None),
            P("fsdp"),
            P(None, "fsdp"),
        ),
        out_specs=P("fsdp", "ctx", None),
        check_vma=False,
    )
```
